32 devices in a mesh: layer: 16 (over z, x, core), row: 2 (over y).
Axes of the slice: x: 2, y: 2, z: 4, core: 2. Of those that a mesh axis runs over, the one named last changes fastest.
Arguments:
- coupling: bfloat16 [16, 1024, 1024], P('layer', 'row'), may hold values from -1 to 1, as said below
- band_off: int32 [16], P('layer'), may hold values from 0 to 32
- band_width: int32 [16], P('layer'), may hold values from 1 to 3
- incident: float32 [32, 1024], P(None, 'row'), may hold values from -6 to 6
- cotangent: float32 [32, 1024], P(None, 'row'), may hold values from -6 to 6
Outputs:
- transmitted: float32 [16, 32, 1024], P('layer', None, 'row')
- adjoint: float32 [16, 32, 1024], P('layer', None, 'row')
The draws below stay inside these ranges and needn't reach their ends.
Inputs may be any that keep to these rules, and one draw needn't show every extreme that they name: coupling is antisymmetric in its last two dimensions.
All inputs are finite; a program needn't handle non-finite values.
Results may differ from the reference program's by a relative error of at most 0.012.
The reference program's roundings to bfloat16 on the way count: a program that leaves them out, or rounds other values in their place, can miss the bound.
Values may be sent and summed in bfloat16 or wider, within the bound.
No kernel may reach another device: no remote copies, remote signals or barrier semaphores. Data moves between devices by JAX's collectives and lax.ppermute only.
A program may use at most 64 MiB of HBM per device.

```python
import math
import jax
import jax.numpy as jnp
from jax import lax

M = 1024
BLOCK = 16
GROUP = 8
FIELDS = 32
LAYERS = 16


def draw_coupling(key, part):
    base = jax.random.normal(key, (LAYERS, M, M), jnp.float32)
    factor = 0.75 / math.sqrt(14.0 * BLOCK) / math.sqrt(2.0)
    return ((base - jnp.swapaxes(base, 1, 2)) * factor).astype(jnp.bfloat16)


def plant(drawn, stream_key, smallest, top_value):
    longest = drawn.shape.index(max(drawn.shape))
    spots = []
    for shift in (0, 1):
        where = [jax.random.randint(jax.random.fold_in(stream_key, axis), (), 0, length) for axis, length in enumerate(drawn.shape)]
        where[longest] = (where[longest] + shift) % drawn.shape[longest]
        spots.append(tuple(where))
    return drawn.at[spots[0]].set(smallest).at[spots[1]].set(top_value)


def steps_of(rng, extent, cuts, least, largest):
    level = 1.0
    for position, parts in cuts:
        draws = jax.random.uniform(jax.random.fold_in(jax.random.fold_in(rng, 6), position), (parts,), jnp.float32, least / len(cuts), largest / len(cuts))
        level = level * jnp.repeat(jnp.exp(draws), extent[position] // parts).reshape((-1,) + (1,) * (len(extent) - 1 - position))
    return level


def scatter_about(rng, dims, spread, most, split=(), kind=jnp.bfloat16):
    result = jax.random.normal(rng, dims, jnp.float32) * spread
    if len(split) > 0:
        result = steps_of(rng, dims, split, -0.22, 0.18) * result
    return jnp.clip(result, min=-most, max=most).astype(kind)


def setup_inputs(seed: int = 0) -> dict:
    streams_of = jax.random.split(jax.random.key(seed), 6)
    coupling = draw_coupling(jax.random.fold_in(streams_of[5], 71), 0)
    band_off = plant(jax.random.randint(streams_of[1], (LAYERS,), 0, M // (2 * BLOCK) + 1), jax.random.fold_in(streams_of[1], 1), 0, (M // (2 * BLOCK) + 1) - 1).astype(jnp.int32)
    band_width = plant(jax.random.randint(streams_of[2], (LAYERS,), 1, 4), jax.random.fold_in(streams_of[2], 1), 1, 3).astype(jnp.int32)
    incident = scatter_about(streams_of[3], (FIELDS, M), 1.0, 6.0, ((1, 2),), jnp.float32)
    cotangent = scatter_about(streams_of[4], (FIELDS, M), 1.0, 6.0, ((1, 2),), jnp.float32)
    return dict(coupling=coupling, band_off=band_off, band_width=band_width, incident=incident, cotangent=cotangent)


def band_mask(row_ids, col_ids, offset, half_width):
    diff = col_ids[None, :] // BLOCK - row_ids[:, None] // BLOCK
    return (jnp.abs(diff - offset) <= half_width) | (jnp.abs(diff + offset) <= half_width)


def layer_map(args):
    coupled, offset, half_width = args
    indices = jnp.arange(M, dtype=jnp.int32)
    banded = jnp.where(band_mask(indices, indices, offset, half_width), coupled, jnp.zeros_like(coupled))
    identity = jnp.eye(M, dtype=jnp.float32)
    section = (identity + banded.astype(jnp.float32) / 4.0).astype(jnp.bfloat16)
    for divisor in (3.0, 2.0, 1.0):
        section = (identity + jnp.dot(banded, section, preferred_element_type=jnp.float32) / divisor).astype(jnp.bfloat16)
    return section


def reference(coupling, band_off, band_width, incident, cotangent):
    layer_maps = lax.map(layer_map, (coupling, band_off, band_width))

    def forward(field_now, one_map):
        nxt = jnp.dot(field_now, one_map.astype(jnp.float32).T, precision=lax.Precision.HIGHEST)
        return nxt, nxt

    def backward(field_now, one_map):
        nxt = jnp.dot(field_now, one_map.astype(jnp.float32), precision=lax.Precision.HIGHEST)
        return nxt, nxt

    _, forward_all = lax.scan(forward, incident, layer_maps)
    _, backward_all = lax.scan(backward, cotangent, layer_maps, reverse=True)
    transmitted = jnp.repeat(forward_all[GROUP - 1::GROUP], GROUP, axis=0)
    adjoint = jnp.repeat(backward_all[0::GROUP], GROUP, axis=0)
    return transmitted, adjoint
```

```python
import functools

import jax
import jax.numpy as jnp
from jax import lax
from jax.experimental import pallas as pl
from jax.experimental.pallas import tpu as pltpu
from jax.sharding import PartitionSpec as P

BLOCK = 16
GROUP = 8
LANES = 128
TILE = 256
WINDOW = TILE + 2 * LANES
BLOCKS_PER_LANES = LANES // BLOCK
DEGREE = 4


def fold_kernel(off_ref, width_ref, coupling_ref, folded_ref):
    rows, orders = coupling_ref.shape[1:]
    first = off_ref[0] - width_ref[0]
    last = off_ref[0] + width_ref[0]
    first_block = lax.axis_index("row") * (rows // BLOCK)
    lane = lax.broadcasted_iota(jnp.int32, (BLOCK, LANES), 1)
    sub = lax.broadcasted_iota(jnp.int32, (BLOCK, LANES), 0)
    top = orders // LANES - 1
    for local in range(rows // BLOCK):
        block = first_block + local
        start = (block + first) * BLOCK
        tile = start >> 7
        shift = start & (LANES - 1)
        here = slice(local * BLOCK, (local + 1) * BLOCK)

        def part(index):
            column = pl.multiple_of(jnp.clip(index, 0, top) * LANES, LANES)
            return coupling_ref[0, here, pl.ds(column, LANES)].astype(jnp.float32)

        near = lane >= shift
        column = jnp.where(near, lane, lane + LANES) + tile * LANES
        limit = jnp.minimum((block + last + 1) * BLOCK, orders)
        keep = (column > block * BLOCK + sub) & (column < limit)
        folded = jnp.where(keep, jnp.where(near, part(tile), part(tile + 1)), 0.0)
        is_last = block * BLOCK + sub == orders - 1
        folded = jnp.where(is_last, first.astype(jnp.float32), folded)
        folded_ref[here, :] = folded.astype(jnp.bfloat16)


def fold(coupling, band_off, band_width):
    return pl.pallas_call(
        fold_kernel,
        out_shape=jax.ShapeDtypeStruct((coupling.shape[1], LANES), jnp.bfloat16),
        in_specs=[
            pl.BlockSpec(memory_space=pltpu.SMEM),
            pl.BlockSpec(memory_space=pltpu.SMEM),
            pl.BlockSpec(memory_space=pltpu.VMEM),
        ],
        out_specs=pl.BlockSpec(memory_space=pltpu.VMEM),
        name="fold",
    )(band_off, band_width, coupling)


def load_pieces(pieces, places, folds, sems):
    slot = lax.axis_index("layer") % GROUP
    row = lax.axis_index("row")
    copies = []
    for index, (piece, (layer_mask, row_mask)) in enumerate(zip(pieces, places)):
        rows = piece.shape[0]
        copies.append(
            pltpu.make_async_copy(
                piece,
                folds.at[slot ^ layer_mask, pl.ds((row ^ row_mask) * rows, rows)],
                sems.at[index],
            )
        )
    for copy in copies:
        copy.start()
    return copies


def fill_masks(masks):
    lane = lax.broadcasted_iota(jnp.int32, (BLOCK, LANES), 1)
    for n in range(masks.shape[0]):
        for k in range(masks.shape[1]):
            at = lane + (LANES * k - BLOCK * n)
            masks[n, k] = ((at >= 0) & (at < LANES)).astype(jnp.float32).astype(jnp.bfloat16)


def expand(folds, slot, masks, window):
    orders = folds.shape[1]
    last_row = folds[slot, orders - BLOCK : orders, :].astype(jnp.float32)[BLOCK - 1 :, :]
    first = jnp.max(last_row).astype(jnp.int32)
    sub = lax.broadcasted_iota(jnp.int32, (BLOCK, LANES), 0)
    fine = first & (BLOCKS_PER_LANES - 1)
    for block in range(orders // BLOCK):
        run = folds[slot, block * BLOCK : (block + 1) * BLOCK, :]
        if block == orders // BLOCK - 1:
            run = jnp.where(sub == BLOCK - 1, 0.0, run.astype(jnp.float32)).astype(jnp.bfloat16)
        t, inner = divmod(block, TILE // BLOCK)
        base, offset = divmod(inner, BLOCKS_PER_LANES)
        here = slice(inner * BLOCK, (inner + 1) * BLOCK)
        for k in range(3):
            lanes = slice((base + k) * LANES, (base + k + 1) * LANES)
            window[t, here, lanes] = run * masks[offset + fine, k]
    return (first >> 3) & (orders // LANES - 1)


def banded_product(v, window, start, xs, zs):
    fields, orders = v.shape
    tiles = orders // LANES
    narrow = v.astype(jnp.bfloat16)
    for u in range(tiles):
        part = narrow[:, u * LANES : (u + 1) * LANES]
        xs[u] = part
        xs[u + tiles] = part
    sums = [None] * tiles
    for t in range(orders // TILE):
        product = jnp.dot(
            narrow[:, t * TILE : (t + 1) * TILE], window[t], preferred_element_type=jnp.float32
        )
        for k in range(WINDOW // LANES):
            u = (t * (TILE // LANES) + k) % tiles
            part = product[:, k * LANES : (k + 1) * LANES]
            sums[u] = part if sums[u] is None else sums[u] + part
    for u in range(tiles):
        zs[u] = sums[u]
        zs[u + tiles] = sums[u]
    moved = [xs[start + u] for u in range(tiles)]
    back = (tiles - start) & (tiles - 1)
    outs = []
    for t in range(orders // TILE):
        first = t * (TILE // LANES)
        seen = jnp.concatenate(
            [moved[(first + k) % tiles] for k in range(WINDOW // LANES)], axis=1
        )
        product = lax.dot_general(
            seen, window[t], (((1,), (1,)), ((), ())), preferred_element_type=jnp.float32
        )
        for k in range(TILE // LANES):
            outs.append(zs[back + first + k] - product[:, k * LANES : (k + 1) * LANES])
    return jnp.concatenate(outs, axis=1)


def run_layer(x, sign, window, start, xs, zs):
    v = x
    for divisor in range(DEGREE, 0, -1):
        v = x + (sign * (1.0 / divisor)) * banded_product(v, window, start, xs, zs)
    return v


def cascade(x, forward, folds, masks, windows, xs, zs):
    sign = jnp.where(forward, -1.0, 1.0)

    def slot_of(k):
        return jnp.where(forward, k, GROUP - 1 - k)

    def pair(i, carry):
        x, start = carry
        other = expand(folds, slot_of(2 * i + 1), masks, windows[1])
        x = run_layer(x, sign, windows[0], start, xs, zs)
        start = expand(folds, slot_of(jnp.minimum(2 * i + 2, GROUP - 1)), masks, windows[0])
        x = run_layer(x, sign, windows[1], other, xs, zs)
        return x, start

    start = expand(folds, slot_of(0), masks, windows[0])
    x, _ = lax.fori_loop(0, GROUP // 2, pair, (x, start))
    return x


def cascade_kernel(step, groups, places, *refs):
    last = step == groups - 1
    n = len(places)
    pieces, refs = refs[:n], refs[n:]
    if step == 0:
        count = len([p for p in places if p[0] == 0])
        fields, refs = refs[:count], refs[count:]
    else:
        x_ref, kept_forward, kept_adjoint = refs[:3]
        refs = refs[3:]
    outs, (folds, masks, window0, window1, xs, zs, sems) = refs[:-7], refs[-7:]
    layer = lax.axis_index("layer")
    row = lax.axis_index("row")
    group = layer // GROUP
    copies = load_pieces(pieces, places, folds, sems)
    fill_masks(masks)
    window0[...] = jnp.zeros_like(window0)
    window1[...] = jnp.zeros_like(window1)
    for copy in copies:
        copy.wait()
    orders = folds.shape[1]
    if step == 0:
        row_masks = [p[1] for p in places if p[0] == 0]
        panel = fields[0].shape[1]
        parts = [ref[...] for ref in fields]
        ordered = []
        for want in range(len(parts)):
            chosen = parts[0]
            for mask, part in zip(row_masks, parts):
                chosen = jnp.where((row ^ mask) == want, part, chosen)
            ordered.append(chosen)
        x = jnp.concatenate(ordered, axis=1)
    else:
        x = x_ref[...].astype(jnp.float32)
    forward = group == step
    backward = group == groups - 1 - step
    x = cascade(x, forward, folds, masks, (window0, window1), xs, zs)
    panel = outs[0].shape[-1]
    if not last:
        outs[-1][...] = x.astype(jnp.bfloat16)
    mine = x[:, :panel]
    for index in range(1, orders // panel):
        mine = jnp.where(row == index, x[:, index * panel : (index + 1) * panel], mine)
    if step == 0:
        outs[0][0] = mine
    else:
        outs[0][0] = jnp.where(forward, mine, kept_forward[0])
        outs[1][0] = jnp.where(backward, mine, kept_adjoint[0])


def run_step(step, groups, places, pieces, fields, kept, field_count, panel, orders):
    kept_shape = jax.ShapeDtypeStruct((1, field_count, panel), jnp.float32)
    out_shape = [kept_shape] if step == 0 else [kept_shape, kept_shape]
    if step < groups - 1:
        out_shape.append(jax.ShapeDtypeStruct((field_count, orders), jnp.bfloat16))
    vmem = pl.BlockSpec(memory_space=pltpu.VMEM)
    window = pltpu.VMEM((orders // TILE, TILE, WINDOW), jnp.bfloat16)
    tiles = orders // LANES
    return pl.pallas_call(
        functools.partial(cascade_kernel, step, groups, places),
        out_shape=out_shape,
        in_specs=[pl.BlockSpec(memory_space=pl.ANY)] * len(pieces)
        + [vmem] * (len(fields) + len(kept)),
        out_specs=[vmem] * len(out_shape),
        scratch_shapes=[
            pltpu.VMEM((GROUP, orders, LANES), jnp.bfloat16),
            pltpu.VMEM((2 * BLOCKS_PER_LANES - 1, 3, BLOCK, LANES), jnp.bfloat16),
            window,
            window,
            pltpu.VMEM((2 * tiles, field_count, LANES), jnp.bfloat16),
            pltpu.VMEM((2 * tiles, field_count, LANES), jnp.float32),
            pltpu.SemaphoreType.DMA((len(pieces),)),
        ],
        compiler_params=pltpu.CompilerParams(vmem_limit_bytes=32 * 1024 * 1024),
        name=f"cascade_{step}",
    )(*pieces, *fields, *kept)


def on_device(coupling, band_off, band_width, incident, cotangent):
    panel, orders = coupling.shape[1:]
    layers = lax.axis_size("layer")
    rows = lax.axis_size("row")
    groups = layers // GROUP
    field_count = incident.shape[0]
    group = lax.axis_index("layer") // GROUP

    def across(array, layer_mask, row_mask):
        pairs = [
            (l * rows + r, (l ^ layer_mask) * rows + (r ^ row_mask))
            for l in range(layers)
            for r in range(rows)
        ]
        return lax.ppermute(array, ("layer", "row"), pairs)

    field = jnp.where(group == 0, incident, cotangent)
    fields = [field] + [across(field, 0, mask) for mask in range(1, rows)]
    folded = fold(coupling, band_off, band_width)
    places = [(a, b) for a in range(0, GROUP, 2) for b in range(rows)]
    pieces = [folded if place == (0, 0) else across(folded, *place) for place in places]
    pieces += [across(piece, 1, 0) for piece in pieces]
    places += [(a ^ 1, b) for a, b in places]

    kept = []
    for step in range(groups):
        results = run_step(
            step, groups, places, pieces, fields, kept, field_count, panel, orders
        )
        if step == groups - 1:
            return tuple(results)
        kept = [results[0], results[0]] if step == 0 else list(results[:2])
        pairs = []
        for index in range(GROUP * rows):
            forward_from = step * GROUP * rows + index
            adjoint_from = (groups - 1 - step) * GROUP * rows + index
            pairs.append((forward_from, forward_from + GROUP * rows))
            pairs.append((adjoint_from, adjoint_from - GROUP * rows))
        fields = [lax.ppermute(results[-1], ("layer", "row"), pairs)]


def solution(mesh):
    in_specs = (P("layer", "row", None), P("layer"), P("layer"), P(None, "row"), P(None, "row"))
    out_specs = (P("layer", None, "row"), P("layer", None, "row"))
    return jax.shard_map(
        on_device, mesh=mesh, in_specs=in_specs, out_specs=out_specs, check_vma=False
    )
```

```python
import functools

import jax
import jax.numpy as jnp
from jax import lax
from jax.experimental import pallas as pl
from jax.experimental.pallas import tpu as pltpu
from jax.sharding import PartitionSpec as P

BLOCK = 16
GROUP = 8
LANES = 128
BLOCKS_PER_LANES = LANES // BLOCK
DEGREE = 4


def fold_kernel(off_ref, width_ref, coupling_ref, folded_ref):
    rows, orders = coupling_ref.shape[1:]
    first = off_ref[0] - width_ref[0]
    last = off_ref[0] + width_ref[0]
    first_block = lax.axis_index("row") * (rows // BLOCK)
    lane = lax.broadcasted_iota(jnp.int32, (BLOCK, LANES), 1)
    sub = lax.broadcasted_iota(jnp.int32, (BLOCK, LANES), 0)
    top = orders // LANES - 1
    for local in range(rows // BLOCK):
        block = first_block + local
        start = (block + first) * BLOCK
        tile = start >> 7
        shift = start & (LANES - 1)
        here = slice(local * BLOCK, (local + 1) * BLOCK)

        def part(index):
            column = pl.multiple_of(jnp.clip(index, 0, top) * LANES, LANES)
            return coupling_ref[0, here, pl.ds(column, LANES)].astype(jnp.float32)

        near = lane >= shift
        column = jnp.where(near, lane, lane + LANES) + tile * LANES
        limit = jnp.minimum((block + last + 1) * BLOCK, orders)
        keep = (column > block * BLOCK + sub) & (column < limit)
        folded = jnp.where(keep, jnp.where(near, part(tile), part(tile + 1)), 0.0)
        is_last = block * BLOCK + sub == orders - 1
        folded = jnp.where(is_last, first.astype(jnp.float32), folded)
        folded = pltpu.roll(folded, (-first * BLOCK) & (LANES - 1), 1)
        folded_ref[here, :] = folded.astype(jnp.bfloat16)


def fold(coupling, band_off, band_width):
    return pl.pallas_call(
        fold_kernel,
        out_shape=jax.ShapeDtypeStruct((coupling.shape[1], LANES), jnp.bfloat16),
        in_specs=[
            pl.BlockSpec(memory_space=pltpu.SMEM),
            pl.BlockSpec(memory_space=pltpu.SMEM),
            pl.BlockSpec(memory_space=pltpu.VMEM),
        ],
        out_specs=pl.BlockSpec(memory_space=pltpu.VMEM),
        name="fold",
    )(band_off, band_width, coupling)


def load_pieces(pieces, places, folds, sems):
    slot = lax.axis_index("layer") % GROUP
    row = lax.axis_index("row")
    copies = []
    for index, (piece, (layer_mask, row_mask)) in enumerate(zip(pieces, places)):
        rows = piece.shape[0]
        copies.append(
            pltpu.make_async_copy(
                piece,
                folds.at[slot ^ layer_mask, pl.ds((row ^ row_mask) * rows, rows)],
                sems.at[index],
            )
        )
    for copy in copies:
        copy.start()
    return copies


def fill_masks(masks):
    row = lax.broadcasted_iota(jnp.int32, (LANES, LANES), 0)
    lane = lax.broadcasted_iota(jnp.int32, (LANES, LANES), 1)
    masks[0] = (lane >= row // BLOCK * BLOCK).astype(jnp.float32).astype(jnp.bfloat16)
    masks[1] = (row >= lane // BLOCK * BLOCK).astype(jnp.float32).astype(jnp.bfloat16)
    masks[2] = (row < LANES - 1).astype(jnp.float32).astype(jnp.bfloat16)


def expand(folds, slot, masks, upper, lower):
    orders = folds.shape[1]
    tiles = orders // LANES
    last_row = folds[slot, orders - BLOCK : orders, :].astype(jnp.float32)[BLOCK - 1 :, :]
    first = jnp.max(last_row).astype(jnp.int32)
    for t in range(tiles):
        run = folds[slot, t * LANES : (t + 1) * LANES, :]
        if t == tiles - 1:
            run = run * masks[2]
        near = run * masks[0]
        upper[t, :, :LANES] = near
        upper[t, :, LANES:] = run - near
        turned = run.T
        near = turned * masks[1]
        lower[t, :, :LANES] = near
        lower[(t + 1) % tiles, :, LANES:] = turned - near
    return first


def banded_product(v, upper, lower, start, xs, zs):
    tiles = len(v)
    whole = start >> 3
    fine = (start & (BLOCKS_PER_LANES - 1)) * BLOCK
    lane = lax.broadcasted_iota(jnp.int32, v[0].shape, 1)
    turned = [pltpu.roll(part, (LANES - fine) & (LANES - 1), 1) for part in v]
    for u in range(tiles):
        moved = jnp.where(lane < LANES - fine, turned[u], turned[(u + 1) % tiles])
        xs[u] = moved.astype(jnp.bfloat16)
    first = [
        jnp.dot(v[t].astype(jnp.bfloat16), upper[t], preferred_element_type=jnp.float32)
        for t in range(tiles)
    ]
    sums = [first[t][:, :LANES] + first[t - 1][:, LANES:] for t in range(tiles)]
    turned = [pltpu.roll(part, fine, 1) for part in sums]
    for u in range(tiles):
        zs[u] = jnp.where(lane >= fine, turned[u], turned[u - 1])
    second = [
        jnp.dot(
            xs[(whole + u) & (tiles - 1)], lower[u], preferred_element_type=jnp.float32
        )
        for u in range(tiles)
    ]
    return [
        zs[(u - whole) & (tiles - 1)]
        - (second[u][:, :LANES] + second[(u + 1) % tiles][:, LANES:])
        for u in range(tiles)
    ]


def run_layer(x, sign, upper, lower, start, xs, zs):
    v = x
    for divisor in range(DEGREE, 0, -1):
        scale = sign * (1.0 / divisor)
        product = banded_product(v, upper, lower, start, xs, zs)
        v = [part + scale * term for part, term in zip(x, product)]
    return v


def cascade(x, forward, folds, masks, windows, xs, zs):
    sign = jnp.where(forward, -1.0, 1.0)

    def slot_of(k):
        return jnp.where(forward, k, GROUP - 1 - k)

    def pair(i, carry):
        x, start = carry
        other = expand(folds, slot_of(2 * i + 1), masks, *windows[1])
        x = run_layer(x, sign, *windows[0], start, xs, zs)
        start = expand(folds, slot_of(jnp.minimum(2 * i + 2, GROUP - 1)), masks, *windows[0])
        x = run_layer(x, sign, *windows[1], other, xs, zs)
        return x, start

    tiles = folds.shape[1] // LANES
    x = [x[:, u * LANES : (u + 1) * LANES] for u in range(tiles)]
    start = expand(folds, slot_of(0), masks, *windows[0])
    x, _ = lax.fori_loop(0, GROUP // 2, pair, (x, start))
    return jnp.concatenate(x, axis=1)


def cascade_kernel(step, groups, places, *refs):
    last = step == groups - 1
    n = len(places)
    pieces, refs = refs[:n], refs[n:]
    if step == 0:
        count = len([p for p in places if p[0] == 0])
        fields, refs = refs[:count], refs[count:]
    else:
        x_ref, kept_forward, kept_adjoint = refs[:3]
        refs = refs[3:]
    outs, (folds, masks, *tiles, xs, zs, sems) = refs[:-9], refs[-9:]
    layer = lax.axis_index("layer")
    row = lax.axis_index("row")
    group = layer // GROUP
    copies = load_pieces(pieces, places, folds, sems)
    fill_masks(masks)
    for copy in copies:
        copy.wait()
    orders = folds.shape[1]
    if step == 0:
        row_masks = [p[1] for p in places if p[0] == 0]
        panel = fields[0].shape[1]
        parts = [ref[...] for ref in fields]
        ordered = []
        for want in range(len(parts)):
            chosen = parts[0]
            for mask, part in zip(row_masks, parts):
                chosen = jnp.where((row ^ mask) == want, part, chosen)
            ordered.append(chosen)
        x = jnp.concatenate(ordered, axis=1)
    else:
        x = x_ref[...].astype(jnp.float32)
    forward = group == step
    backward = group == groups - 1 - step
    x = cascade(x, forward, folds, masks, (tiles[:2], tiles[2:]), xs, zs)
    panel = outs[0].shape[-1]
    if not last:
        outs[-1][...] = x.astype(jnp.bfloat16)
    mine = x[:, :panel]
    for index in range(1, orders // panel):
        mine = jnp.where(row == index, x[:, index * panel : (index + 1) * panel], mine)
    if step == 0:
        outs[0][0] = mine
    else:
        outs[0][0] = jnp.where(forward, mine, kept_forward[0])
        outs[1][0] = jnp.where(backward, mine, kept_adjoint[0])


def run_step(step, groups, places, pieces, fields, kept, field_count, panel, orders):
    kept_shape = jax.ShapeDtypeStruct((1, field_count, panel), jnp.float32)
    out_shape = [kept_shape] if step == 0 else [kept_shape, kept_shape]
    if step < groups - 1:
        out_shape.append(jax.ShapeDtypeStruct((field_count, orders), jnp.bfloat16))
    vmem = pl.BlockSpec(memory_space=pltpu.VMEM)
    tiles = orders // LANES
    window = pltpu.VMEM((tiles, LANES, 2 * LANES), jnp.bfloat16)
    return pl.pallas_call(
        functools.partial(cascade_kernel, step, groups, places),
        out_shape=out_shape,
        in_specs=[pl.BlockSpec(memory_space=pl.ANY)] * len(pieces)
        + [vmem] * (len(fields) + len(kept)),
        out_specs=[vmem] * len(out_shape),
        scratch_shapes=[
            pltpu.VMEM((GROUP, orders, LANES), jnp.bfloat16),
            pltpu.VMEM((3, LANES, LANES), jnp.bfloat16),
            window,
            window,
            window,
            window,
            pltpu.VMEM((tiles, field_count, LANES), jnp.bfloat16),
            pltpu.VMEM((tiles, field_count, LANES), jnp.float32),
            pltpu.SemaphoreType.DMA((len(pieces),)),
        ],
        compiler_params=pltpu.CompilerParams(vmem_limit_bytes=32 * 1024 * 1024),
        name=f"cascade_{step}",
    )(*pieces, *fields, *kept)


def on_device(coupling, band_off, band_width, incident, cotangent):
    panel, orders = coupling.shape[1:]
    layers = lax.axis_size("layer")
    rows = lax.axis_size("row")
    groups = layers // GROUP
    field_count = incident.shape[0]
    group = lax.axis_index("layer") // GROUP

    def across(array, layer_mask, row_mask):
        pairs = [
            (l * rows + r, (l ^ layer_mask) * rows + (r ^ row_mask))
            for l in range(layers)
            for r in range(rows)
        ]
        return lax.ppermute(array, ("layer", "row"), pairs)

    field = jnp.where(group == 0, incident, cotangent)
    fields = [field] + [across(field, 0, mask) for mask in range(1, rows)]
    folded = fold(coupling, band_off, band_width)
    places = [(a, b) for a in range(0, GROUP, 2) for b in range(rows)]
    pieces = [folded if place == (0, 0) else across(folded, *place) for place in places]
    pieces += [across(piece, 1, 0) for piece in pieces]
    places += [(a ^ 1, b) for a, b in places]

    kept = []
    for step in range(groups):
        results = run_step(
            step, groups, places, pieces, fields, kept, field_count, panel, orders
        )
        if step == groups - 1:
            return tuple(results)
        kept = [results[0], results[0]] if step == 0 else list(results[:2])
        pairs = []
        for index in range(GROUP * rows):
            forward_from = step * GROUP * rows + index
            adjoint_from = (groups - 1 - step) * GROUP * rows + index
            pairs.append((forward_from, forward_from + GROUP * rows))
            pairs.append((adjoint_from, adjoint_from - GROUP * rows))
        fields = [lax.ppermute(results[-1], ("layer", "row"), pairs)]


def solution(mesh):
    in_specs = (P("layer", "row", None), P("layer"), P("layer"), P(None, "row"), P(None, "row"))
    out_specs = (P("layer", None, "row"), P("layer", None, "row"))
    return jax.shard_map(
        on_device, mesh=mesh, in_specs=in_specs, out_specs=out_specs, check_vma=False
    )
```

```python
import functools

import jax
import jax.numpy as jnp
from jax import lax
from jax.experimental import pallas as pl
from jax.experimental.pallas import tpu as pltpu
from jax.sharding import PartitionSpec as P

BLOCK = 16
GROUP = 8
LANES = 128
BLOCKS_PER_LANES = LANES // BLOCK
DEGREE = 4


def fold_kernel(
    off_hbm, width_hbm, coupling_hbm, incident_ref, cotangent_ref,
    folded_ref, field_ref, off_ref, width_ref, coupling_ref, sems,
):
    rows, orders = coupling_hbm.shape[1:]
    chunk = min(rows, LANES)
    copies = [
        pltpu.make_async_copy(off_hbm, off_ref, sems.at[0]),
        pltpu.make_async_copy(width_hbm, width_ref, sems.at[1]),
    ]
    for index in range(rows // chunk):
        here = pl.ds(index * chunk, chunk)
        copies.append(
            pltpu.make_async_copy(
                coupling_hbm.at[0, here], coupling_ref.at[here], sems.at[2 + index]
            )
        )
    for copy in copies:
        copy.start()
    group = lax.axis_index("layer") // GROUP
    field_ref[...] = jnp.where(group == 0, incident_ref[...], cotangent_ref[...])
    copies[0].wait()
    copies[1].wait()
    first = off_ref[0] - width_ref[0]
    last = off_ref[0] + width_ref[0]
    first_block = lax.axis_index("row") * (rows // BLOCK)
    lane = lax.broadcasted_iota(jnp.int32, (BLOCK, LANES), 1)
    sub = lax.broadcasted_iota(jnp.int32, (BLOCK, LANES), 0)
    top = orders // LANES - 1
    for local in range(rows // BLOCK):
        if local * BLOCK % chunk == 0:
            copies[2 + local * BLOCK // chunk].wait()
        block = first_block + local
        start = (block + first) * BLOCK
        tile = start >> 7
        shift = start & (LANES - 1)
        here = slice(local * BLOCK, (local + 1) * BLOCK)

        def part(index):
            column = pl.multiple_of(jnp.clip(index, 0, top) * LANES, LANES)
            return coupling_ref[here, pl.ds(column, LANES)].astype(jnp.float32)

        near = lane >= shift
        column = jnp.where(near, lane, lane + LANES) + tile * LANES
        limit = jnp.minimum((block + last + 1) * BLOCK, orders)
        keep = (column > block * BLOCK + sub) & (column < limit)
        folded = jnp.where(keep, jnp.where(near, part(tile), part(tile + 1)), 0.0)
        is_last = block * BLOCK + sub == orders - 1
        folded = jnp.where(is_last, first.astype(jnp.float32), folded)
        folded = pltpu.roll(folded, (-first * BLOCK) & (LANES - 1), 1)
        folded_ref[here, :] = folded.astype(jnp.bfloat16)


def fold(coupling, band_off, band_width, incident, cotangent):
    rows, orders = coupling.shape[1:]
    hbm = pl.BlockSpec(memory_space=pltpu.HBM)
    vmem = pl.BlockSpec(memory_space=pltpu.VMEM)
    return pl.pallas_call(
        fold_kernel,
        out_shape=[
            jax.ShapeDtypeStruct((rows, LANES), jnp.bfloat16),
            jax.ShapeDtypeStruct(incident.shape, jnp.float32),
        ],
        in_specs=[hbm, hbm, hbm, vmem, vmem],
        out_specs=[vmem, vmem],
        scratch_shapes=[
            pltpu.SMEM((1,), jnp.int32),
            pltpu.SMEM((1,), jnp.int32),
            pltpu.VMEM((rows, orders), jnp.bfloat16),
            pltpu.SemaphoreType.DMA((2 + rows // min(rows, LANES),)),
        ],
        name="fold",
    )(band_off, band_width, coupling, incident, cotangent)


def load_pieces(pieces, folds, sems):
    slot = lax.axis_index("layer") % GROUP
    row = lax.axis_index("row")
    shares = len(pieces) // GROUP
    rows = pieces[0].shape[0]

    def copy(piece, at, share, index):
        return pltpu.make_async_copy(
            piece, folds.at[at, pl.ds(share * rows, rows)], sems.at[index]
        )

    for index, piece in enumerate(pieces):
        layer_mask, row_mask = divmod(index, shares)
        copy(piece, slot ^ layer_mask, row ^ row_mask, index).start()

    def wait_layer(at):
        for share in range(shares):
            copy(pieces[0], at, share, (slot ^ at) * shares + (row ^ share)).wait()

    return wait_layer


def fill_masks(masks):
    row = lax.broadcasted_iota(jnp.int32, (LANES, LANES), 0)
    lane = lax.broadcasted_iota(jnp.int32, (LANES, LANES), 1)
    masks[0] = (lane >= row // BLOCK * BLOCK).astype(jnp.float32).astype(jnp.bfloat16)
    masks[1] = (row >= lane // BLOCK * BLOCK).astype(jnp.float32).astype(jnp.bfloat16)
    masks[2] = (row < LANES - 1).astype(jnp.float32).astype(jnp.bfloat16)


def expand(folds, slot, masks, upper, lower):
    orders = folds.shape[1]
    tiles = orders // LANES
    last_row = folds[slot, orders - BLOCK : orders, :].astype(jnp.float32)[BLOCK - 1 :, :]
    first = jnp.max(last_row).astype(jnp.int32)
    for t in range(tiles):
        run = folds[slot, t * LANES : (t + 1) * LANES, :]
        if t == tiles - 1:
            run = run * masks[2]
        near = run * masks[0]
        upper[t, :, :LANES] = near
        upper[t, :, LANES:] = run - near
        turned = run.T
        near = turned * masks[1]
        lower[t, :, :LANES] = near
        lower[(t + 1) % tiles, :, LANES:] = turned - near
    return first


def banded_product(v, upper, lower, start, xs, zs):
    tiles = len(v)
    whole = start >> 3
    fine = (start & (BLOCKS_PER_LANES - 1)) * BLOCK
    lane = lax.broadcasted_iota(jnp.int32, v[0].shape, 1)
    turned = [pltpu.roll(part, (LANES - fine) & (LANES - 1), 1) for part in v]
    for u in range(tiles):
        moved = jnp.where(lane < LANES - fine, turned[u], turned[(u + 1) % tiles])
        xs[u] = moved.astype(jnp.bfloat16)
    first = [
        jnp.dot(v[t].astype(jnp.bfloat16), upper[t], preferred_element_type=jnp.float32)
        for t in range(tiles)
    ]
    sums = [first[t][:, :LANES] + first[t - 1][:, LANES:] for t in range(tiles)]
    turned = [pltpu.roll(part, fine, 1) for part in sums]
    for u in range(tiles):
        zs[u] = jnp.where(lane >= fine, turned[u], turned[u - 1])
    second = [
        jnp.dot(
            xs[(whole + u) & (tiles - 1)], lower[u], preferred_element_type=jnp.float32
        )
        for u in range(tiles)
    ]
    return [
        zs[(u - whole) & (tiles - 1)]
        - (second[u][:, :LANES] + second[(u + 1) % tiles][:, LANES:])
        for u in range(tiles)
    ]


def run_layer(x, sign, upper, lower, start, xs, zs):
    v = x
    for divisor in range(DEGREE, 0, -1):
        scale = sign * (1.0 / divisor)
        product = banded_product(v, upper, lower, start, xs, zs)
        v = [part + scale * term for part, term in zip(x, product)]
    return v


def cascade(x, forward, folds, wait_layer, masks, windows, xs, zs):
    sign = jnp.where(forward, -1.0, 1.0)

    def slot_of(k):
        return jnp.where(forward, k, GROUP - 1 - k)

    def pair(i, carry):
        x, start = carry
        wait_layer(slot_of(2 * i + 1))
        other = expand(folds, slot_of(2 * i + 1), masks, *windows[1])
        x = run_layer(x, sign, *windows[0], start, xs, zs)
        following = 2 * i + 2

        @pl.when(following < GROUP)
        def _():
            wait_layer(slot_of(following))

        following = slot_of(jnp.minimum(following, GROUP - 1))
        start = expand(folds, following, masks, *windows[0])
        x = run_layer(x, sign, *windows[1], other, xs, zs)
        return x, start

    tiles = folds.shape[1] // LANES
    x = [x[:, u * LANES : (u + 1) * LANES] for u in range(tiles)]
    wait_layer(slot_of(0))
    start = expand(folds, slot_of(0), masks, *windows[0])
    x, _ = lax.fori_loop(0, GROUP // 2, pair, (x, start))
    return jnp.concatenate(x, axis=1)


def cascade_kernel(step, groups, n, *refs):
    last = step == groups - 1
    pieces, refs = refs[:n], refs[n:]
    shares = n // GROUP
    if step == 0:
        fields, refs = refs[:shares], refs[shares:]
    else:
        x_ref, kept_forward, kept_adjoint = refs[:3]
        refs = refs[3:]
    outs, (folds, masks, *tiles, xs, zs, sems) = refs[:-9], refs[-9:]
    row = lax.axis_index("row")
    group = lax.axis_index("layer") // GROUP
    wait_layer = load_pieces(pieces, folds, sems)
    fill_masks(masks)
    orders = folds.shape[1]
    if step == 0:
        parts = [ref[...] for ref in fields]
        ordered = []
        for want in range(shares):
            chosen = parts[0]
            for mask, part in enumerate(parts):
                chosen = jnp.where((row ^ mask) == want, part, chosen)
            ordered.append(chosen)
        x = jnp.concatenate(ordered, axis=1)
    else:
        x = x_ref[...].astype(jnp.float32)
    forward = group == step
    backward = group == groups - 1 - step
    x = cascade(x, forward, folds, wait_layer, masks, (tiles[:2], tiles[2:]), xs, zs)
    panel = outs[0].shape[-1]
    if not last:
        outs[-1][...] = x.astype(jnp.bfloat16)
    mine = x[:, :panel]
    for index in range(1, orders // panel):
        mine = jnp.where(row == index, x[:, index * panel : (index + 1) * panel], mine)
    if step == 0:
        outs[0][0] = mine
    else:
        outs[0][0] = jnp.where(forward, mine, kept_forward[0])
        outs[1][0] = jnp.where(backward, mine, kept_adjoint[0])


def run_step(step, groups, pieces, fields, kept, field_count, panel, orders):
    kept_shape = jax.ShapeDtypeStruct((1, field_count, panel), jnp.float32)
    out_shape = [kept_shape] if step == 0 else [kept_shape, kept_shape]
    if step < groups - 1:
        out_shape.append(jax.ShapeDtypeStruct((field_count, orders), jnp.bfloat16))
    vmem = pl.BlockSpec(memory_space=pltpu.VMEM)
    tiles = orders // LANES
    window = pltpu.VMEM((tiles, LANES, 2 * LANES), jnp.bfloat16)
    return pl.pallas_call(
        functools.partial(cascade_kernel, step, groups, len(pieces)),
        out_shape=out_shape,
        in_specs=[pl.BlockSpec(memory_space=pltpu.HBM)]
        + [pl.BlockSpec(memory_space=pl.ANY)] * (len(pieces) - 1)
        + [vmem] * (len(fields) + len(kept)),
        out_specs=[vmem] * len(out_shape),
        scratch_shapes=[
            pltpu.VMEM((GROUP, orders, LANES), jnp.bfloat16),
            pltpu.VMEM((3, LANES, LANES), jnp.bfloat16),
            window,
            window,
            window,
            window,
            pltpu.VMEM((tiles, field_count, LANES), jnp.bfloat16),
            pltpu.VMEM((tiles, field_count, LANES), jnp.float32),
            pltpu.SemaphoreType.DMA((len(pieces),)),
        ],
        compiler_params=pltpu.CompilerParams(vmem_limit_bytes=32 * 1024 * 1024),
        name=f"cascade_{step}",
    )(*pieces, *fields, *kept)


def gather_pieces(own, across, rows):
    bits = [(0, 1 << b) for b in range(rows.bit_length() - 1)]
    bits += [(1 << b, 0) for b in range(1, GROUP.bit_length() - 1)]
    count = len(bits)
    pieces = {0: own}

    def step_of(which):
        return [sum(bits[b][axis] for b in which) for axis in (0, 1)]

    def send(array, which):
        return across(array, *step_of(which))

    subsets = sorted(range(1, 1 << count), key=lambda m: (m.bit_count(), m))
    for subset in [m for m in subsets if m.bit_count() == 1] + subsets[-1:]:
        pieces[subset] = send(own, [b for b in range(count) if subset >> b & 1])
    for subset in subsets[count:-1]:
        which = [b for b in range(count) if subset >> b & 1]
        link = next((b for b in which if (b + 1) % count in which), which[0])
        pieces[subset] = send(pieces[subset ^ 1 << link], [link])
    placed = [None] * (GROUP * rows)
    for subset, piece in pieces.items():
        layer_mask, row_mask = step_of([b for b in range(count) if subset >> b & 1])
        placed[layer_mask * rows + row_mask] = piece
        placed[(layer_mask ^ 1) * rows + row_mask] = across(piece, 1, 0)
    return placed


def on_device(coupling, band_off, band_width, incident, cotangent):
    panel, orders = coupling.shape[1:]
    layers = lax.axis_size("layer")
    rows = lax.axis_size("row")
    groups = layers // GROUP
    field_count = incident.shape[0]

    def across(array, layer_mask, row_mask):
        pairs = [
            (l * rows + r, (l ^ layer_mask) * rows + (r ^ row_mask))
            for l in range(layers)
            for r in range(rows)
        ]
        return lax.ppermute(array, ("layer", "row"), pairs)

    folded, field = fold(coupling, band_off, band_width, incident, cotangent)
    pieces = gather_pieces(folded, across, rows)
    fields = [field] + [across(field, 0, mask) for mask in range(1, rows)]

    kept = []
    for step in range(groups):
        results = run_step(step, groups, pieces, fields, kept, field_count, panel, orders)
        if step == groups - 1:
            return tuple(results)
        kept = [results[0], results[0]] if step == 0 else list(results[:2])
        pairs = []
        for index in range(GROUP * rows):
            forward_from = step * GROUP * rows + index
            adjoint_from = (groups - 1 - step) * GROUP * rows + index
            pairs.append((forward_from, forward_from + GROUP * rows))
            pairs.append((adjoint_from, adjoint_from - GROUP * rows))
        fields = [lax.ppermute(results[-1], ("layer", "row"), pairs)]


def solution(mesh):
    in_specs = (P("layer", "row", None), P("layer"), P("layer"), P(None, "row"), P(None, "row"))
    out_specs = (P("layer", None, "row"), P("layer", None, "row"))
    return jax.shard_map(
        on_device, mesh=mesh, in_specs=in_specs, out_specs=out_specs, check_vma=False
    )
```

```python
import functools

import jax
import jax.numpy as jnp
from jax import lax
from jax.experimental import pallas as pl
from jax.experimental.pallas import tpu as pltpu
from jax.sharding import PartitionSpec as P

BLOCK = 16
GROUP = 8
LANES = 128
BLOCKS_PER_LANES = LANES // BLOCK
DEGREE = 4


def fold_kernel(
    off_hbm, width_hbm, coupling_hbm, incident_ref, cotangent_ref,
    folded_ref, field_ref, off_ref, width_ref, coupling_ref, sems,
):
    rows, orders = coupling_hbm.shape[1:]
    chunk = min(rows, LANES)
    copies = [
        pltpu.make_async_copy(off_hbm, off_ref, sems.at[0]),
        pltpu.make_async_copy(width_hbm, width_ref, sems.at[1]),
    ]
    for index in range(rows // chunk):
        here = pl.ds(index * chunk, chunk)
        copies.append(
            pltpu.make_async_copy(
                coupling_hbm.at[0, here], coupling_ref.at[here], sems.at[2 + index]
            )
        )
    for copy in copies:
        copy.start()
    group = lax.axis_index("layer") // GROUP
    field_ref[...] = jnp.where(group == 0, incident_ref[...], cotangent_ref[...])
    copies[0].wait()
    copies[1].wait()
    first = off_ref[0] - width_ref[0]
    last = off_ref[0] + width_ref[0]
    first_block = lax.axis_index("row") * (rows // BLOCK)
    lane = lax.broadcasted_iota(jnp.int32, (BLOCK, LANES), 1)
    sub = lax.broadcasted_iota(jnp.int32, (BLOCK, LANES), 0)
    top = orders // LANES - 1
    for local in range(rows // BLOCK):
        if local * BLOCK % chunk == 0:
            copies[2 + local * BLOCK // chunk].wait()
        block = first_block + local
        start = (block + first) * BLOCK
        tile = start >> 7
        shift = start & (LANES - 1)
        here = slice(local * BLOCK, (local + 1) * BLOCK)

        def part(index):
            column = pl.multiple_of(jnp.clip(index, 0, top) * LANES, LANES)
            return coupling_ref[here, pl.ds(column, LANES)].astype(jnp.float32)

        near = lane >= shift
        column = jnp.where(near, lane, lane + LANES) + tile * LANES
        limit = jnp.minimum((block + last + 1) * BLOCK, orders)
        keep = (column > block * BLOCK + sub) & (column < limit)
        folded = jnp.where(keep, jnp.where(near, part(tile), part(tile + 1)), 0.0)
        is_last = block * BLOCK + sub == orders - 1
        folded = jnp.where(is_last, first.astype(jnp.float32), folded)
        folded = pltpu.roll(folded, (-first * BLOCK) & (LANES - 1), 1)
        folded = folded.astype(jnp.bfloat16)
        for share in range(folded_ref.shape[0]):
            folded_ref[share, here, :] = folded


def fold(coupling, band_off, band_width, incident, cotangent, shares):
    rows, orders = coupling.shape[1:]
    hbm = pl.BlockSpec(memory_space=pltpu.HBM)
    vmem = pl.BlockSpec(memory_space=pltpu.VMEM)
    return pl.pallas_call(
        fold_kernel,
        out_shape=[
            jax.ShapeDtypeStruct((shares, rows, LANES), jnp.bfloat16),
            jax.ShapeDtypeStruct(incident.shape, jnp.float32),
        ],
        in_specs=[hbm, hbm, hbm, vmem, vmem],
        out_specs=[vmem, vmem],
        scratch_shapes=[
            pltpu.SMEM((1,), jnp.int32),
            pltpu.SMEM((1,), jnp.int32),
            pltpu.VMEM((rows, orders), jnp.bfloat16),
            pltpu.SemaphoreType.DMA((2 + rows // min(rows, LANES),)),
        ],
        name="fold",
    )(band_off, band_width, coupling, incident, cotangent)


def layer_source(same, other):
    core = lax.axis_index("layer") & 1

    def read(at, rows):
        mine = same[at >> 1, rows, :]
        return jnp.where((at & 1) == core, mine, other[at >> 1, rows, :])

    return read


def fill_masks(masks):
    row = lax.broadcasted_iota(jnp.int32, (LANES, LANES), 0)
    lane = lax.broadcasted_iota(jnp.int32, (LANES, LANES), 1)
    masks[0] = (lane >= row // BLOCK * BLOCK).astype(jnp.float32).astype(jnp.bfloat16)
    masks[1] = (row >= lane // BLOCK * BLOCK).astype(jnp.float32).astype(jnp.bfloat16)
    masks[2] = (row < LANES - 1).astype(jnp.float32).astype(jnp.bfloat16)


def expand(read, slot, masks, upper, lower):
    tiles = upper.shape[0]
    last_rows = read(slot, slice(tiles * LANES - BLOCK, tiles * LANES))
    last_row = last_rows.astype(jnp.float32)[BLOCK - 1 :, :]
    first = jnp.max(last_row).astype(jnp.int32)
    for t in range(tiles):
        run = read(slot, slice(t * LANES, (t + 1) * LANES))
        if t == tiles - 1:
            run = run * masks[2]
        near = run * masks[0]
        upper[t, :, :LANES] = near
        upper[t, :, LANES:] = run - near
        turned = run.T
        near = turned * masks[1]
        lower[t, :, :LANES] = near
        lower[(t + 1) % tiles, :, LANES:] = turned - near
    return first


def banded_product(v, upper, lower, start, xs, zs):
    tiles = len(v)
    whole = start >> 3
    fine = (start & (BLOCKS_PER_LANES - 1)) * BLOCK
    lane = lax.broadcasted_iota(jnp.int32, v[0].shape, 1)
    turned = [pltpu.roll(part, (LANES - fine) & (LANES - 1), 1) for part in v]
    for u in range(tiles):
        moved = jnp.where(lane < LANES - fine, turned[u], turned[(u + 1) % tiles])
        xs[u] = moved.astype(jnp.bfloat16)
    first = [
        jnp.dot(v[t].astype(jnp.bfloat16), upper[t], preferred_element_type=jnp.float32)
        for t in range(tiles)
    ]
    sums = [first[t][:, :LANES] + first[t - 1][:, LANES:] for t in range(tiles)]
    turned = [pltpu.roll(part, fine, 1) for part in sums]
    for u in range(tiles):
        zs[u] = jnp.where(lane >= fine, turned[u], turned[u - 1])
    second = [
        jnp.dot(
            xs[(whole + u) & (tiles - 1)], lower[u], preferred_element_type=jnp.float32
        )
        for u in range(tiles)
    ]
    return [
        zs[(u - whole) & (tiles - 1)]
        - (second[u][:, :LANES] + second[(u + 1) % tiles][:, LANES:])
        for u in range(tiles)
    ]


def run_layer(x, sign, upper, lower, start, xs, zs):
    v = x
    for divisor in range(DEGREE, 0, -1):
        scale = sign * (1.0 / divisor)
        product = banded_product(v, upper, lower, start, xs, zs)
        v = [part + scale * term for part, term in zip(x, product)]
    return v


def cascade(x, forward, read, masks, windows, xs, zs):
    sign = jnp.where(forward, -1.0, 1.0)

    def slot_of(k):
        return jnp.where(forward, k, GROUP - 1 - k)

    def pair(i, carry):
        x, start = carry
        other = expand(read, slot_of(2 * i + 1), masks, *windows[1])
        x = run_layer(x, sign, *windows[0], start, xs, zs)
        following = slot_of(jnp.minimum(2 * i + 2, GROUP - 1))
        start = expand(read, following, masks, *windows[0])
        x = run_layer(x, sign, *windows[1], other, xs, zs)
        return x, start

    tiles = xs.shape[0]
    x = [x[:, u * LANES : (u + 1) * LANES] for u in range(tiles)]
    start = expand(read, slot_of(0), masks, *windows[0])
    x, _ = lax.fori_loop(0, GROUP // 2, pair, (x, start))
    return jnp.concatenate(x, axis=1)


def cascade_kernel(step, groups, shares, same, other, *refs):
    last = step == groups - 1
    if step == 0:
        fields, refs = refs[:shares], refs[shares:]
    else:
        x_ref, kept_forward, kept_adjoint = refs[:3]
        refs = refs[3:]
    outs, (masks, *tiles, xs, zs) = refs[:-7], refs[-7:]
    row = lax.axis_index("row")
    group = lax.axis_index("layer") // GROUP
    fill_masks(masks)
    orders = same.shape[1]
    if step == 0:
        parts = [ref[...] for ref in fields]
        ordered = []
        for want in range(shares):
            chosen = parts[0]
            for mask, part in enumerate(parts):
                chosen = jnp.where((row ^ mask) == want, part, chosen)
            ordered.append(chosen)
        x = jnp.concatenate(ordered, axis=1)
    else:
        x = x_ref[...].astype(jnp.float32)
    forward = group == step
    backward = group == groups - 1 - step
    read = layer_source(same, other)
    x = cascade(x, forward, read, masks, (tiles[:2], tiles[2:]), xs, zs)
    panel = outs[0].shape[-1]
    if not last:
        outs[-1][...] = x.astype(jnp.bfloat16)
    mine = x[:, :panel]
    for index in range(1, orders // panel):
        mine = jnp.where(row == index, x[:, index * panel : (index + 1) * panel], mine)
    if step == 0:
        outs[0][0] = mine
    else:
        outs[0][0] = jnp.where(forward, mine, kept_forward[0])
        outs[1][0] = jnp.where(backward, mine, kept_adjoint[0])


def run_step(step, groups, same, other, fields, kept, panel):
    orders = same.shape[1]
    field_count = fields[0].shape[0]
    kept_shape = jax.ShapeDtypeStruct((1, field_count, panel), jnp.float32)
    out_shape = [kept_shape] if step == 0 else [kept_shape, kept_shape]
    if step < groups - 1:
        out_shape.append(jax.ShapeDtypeStruct((field_count, orders), jnp.bfloat16))
    vmem = pl.BlockSpec(memory_space=pltpu.VMEM)
    tiles = orders // LANES
    window = pltpu.VMEM((tiles, LANES, 2 * LANES), jnp.bfloat16)
    return pl.pallas_call(
        functools.partial(cascade_kernel, step, groups, orders // panel),
        out_shape=out_shape,
        in_specs=[vmem] * (2 + len(fields) + len(kept)),
        out_specs=[vmem] * len(out_shape),
        scratch_shapes=[
            pltpu.VMEM((3, LANES, LANES), jnp.bfloat16),
            window,
            window,
            window,
            window,
            pltpu.VMEM((tiles, field_count, LANES), jnp.bfloat16),
            pltpu.VMEM((tiles, field_count, LANES), jnp.float32),
        ],
        compiler_params=pltpu.CompilerParams(vmem_limit_bytes=24 * 1024 * 1024),
        name=f"cascade_{step}",
    )(same, other, *fields, *kept)


def on_device(coupling, band_off, band_width, incident, cotangent):
    panel, orders = coupling.shape[1:]
    layers = lax.axis_size("layer")
    rows = lax.axis_size("row")
    groups = layers // GROUP

    def across(array, layer_mask, row_mask):
        pairs = [
            (l * rows + r, (l ^ layer_mask) * rows + (r ^ row_mask))
            for l in range(layers)
            for r in range(rows)
        ]
        return lax.ppermute(array, ("layer", "row"), pairs)

    shares = GROUP // 2 * rows
    folded, field = fold(coupling, band_off, band_width, incident, cotangent, shares)
    fields = [field] + [across(field, 0, mask) for mask in range(1, rows)]
    same_core = [
        [l * rows + r for l in range(first, first + GROUP, 2) for r in range(rows)]
        for start in range(0, layers, GROUP)
        for first in (start, start + 1)
    ]
    same = lax.all_to_all(folded, ("layer", "row"), 0, 0, axis_index_groups=same_core)
    same = same.reshape(GROUP // 2, orders, LANES)
    other = across(same, 1, 0)

    kept = []
    for step in range(groups):
        results = run_step(step, groups, same, other, fields, kept, panel)
        if step == groups - 1:
            return tuple(results)
        kept = [results[0], results[0]] if step == 0 else list(results[:2])
        pairs = []
        for index in range(GROUP * rows):
            forward_from = step * GROUP * rows + index
            adjoint_from = (groups - 1 - step) * GROUP * rows + index
            pairs.append((forward_from, forward_from + GROUP * rows))
            pairs.append((adjoint_from, adjoint_from - GROUP * rows))
        fields = [lax.ppermute(results[-1], ("layer", "row"), pairs)]


def solution(mesh):
    in_specs = (P("layer", "row", None), P("layer"), P("layer"), P(None, "row"), P(None, "row"))
    out_specs = (P("layer", None, "row"), P("layer", None, "row"))
    return jax.shard_map(
        on_device, mesh=mesh, in_specs=in_specs, out_specs=out_specs, check_vma=False
    )
```

```python
import functools

import jax
import jax.numpy as jnp
from jax import lax
from jax.experimental import pallas as pl
from jax.experimental.pallas import tpu as pltpu
from jax.sharding import PartitionSpec as P

BLOCK = 16
GROUP = 8
LANES = 128
BLOCKS_PER_LANES = LANES // BLOCK
DEGREE = 4


def fold_kernel(
    off_hbm, width_hbm, coupling_hbm, incident_ref, cotangent_ref,
    folded_ref, field_ref, off_ref, width_ref, coupling_ref, sems,
):
    rows, orders = coupling_hbm.shape[1:]
    chunk = min(rows, LANES)
    copies = [
        pltpu.make_async_copy(off_hbm, off_ref, sems.at[0]),
        pltpu.make_async_copy(width_hbm, width_ref, sems.at[1]),
    ]
    for index in range(rows // chunk):
        here = pl.ds(index * chunk, chunk)
        copies.append(
            pltpu.make_async_copy(
                coupling_hbm.at[0, here], coupling_ref.at[here], sems.at[2 + index]
            )
        )
    for copy in copies:
        copy.start()
    group = lax.axis_index("layer") // GROUP
    field_ref[...] = jnp.where(group == 0, incident_ref[...], cotangent_ref[...])
    copies[0].wait()
    copies[1].wait()
    first = off_ref[0] - width_ref[0]
    last = off_ref[0] + width_ref[0]
    first_block = lax.axis_index("row") * (rows // BLOCK)
    lane = lax.broadcasted_iota(jnp.int32, (BLOCK, LANES), 1)
    sub = lax.broadcasted_iota(jnp.int32, (BLOCK, LANES), 0)
    top = orders // LANES - 1
    for local in range(rows // BLOCK):
        if local * BLOCK % chunk == 0:
            copies[2 + local * BLOCK // chunk].wait()
        block = first_block + local
        start = (block + first) * BLOCK
        tile = start >> 7
        shift = start & (LANES - 1)
        here = slice(local * BLOCK, (local + 1) * BLOCK)

        def part(index):
            column = pl.multiple_of(jnp.clip(index, 0, top) * LANES, LANES)
            return coupling_ref[here, pl.ds(column, LANES)].astype(jnp.float32)

        near = lane >= shift
        column = jnp.where(near, lane, lane + LANES) + tile * LANES
        limit = jnp.minimum((block + last + 1) * BLOCK, orders)
        keep = (column > block * BLOCK + sub) & (column < limit)
        folded = jnp.where(keep, jnp.where(near, part(tile), part(tile + 1)), 0.0)
        is_last = block * BLOCK + sub == orders - 1
        folded = jnp.where(is_last, first.astype(jnp.float32), folded)
        folded = pltpu.roll(folded, (-first * BLOCK) & (LANES - 1), 1)
        folded = folded.astype(jnp.bfloat16)
        for share in range(folded_ref.shape[0]):
            folded_ref[share, here, :] = folded


def fold(coupling, band_off, band_width, incident, cotangent, shares):
    rows, orders = coupling.shape[1:]
    hbm = pl.BlockSpec(memory_space=pltpu.HBM)
    vmem = pl.BlockSpec(memory_space=pltpu.VMEM)
    return pl.pallas_call(
        fold_kernel,
        out_shape=[
            jax.ShapeDtypeStruct((shares, rows, LANES), jnp.bfloat16),
            jax.ShapeDtypeStruct(incident.shape, jnp.float32),
        ],
        in_specs=[hbm, hbm, hbm, vmem, vmem],
        out_specs=[vmem, vmem],
        scratch_shapes=[
            pltpu.SMEM((1,), jnp.int32),
            pltpu.SMEM((1,), jnp.int32),
            pltpu.VMEM((rows, orders), jnp.bfloat16),
            pltpu.SemaphoreType.DMA((2 + rows // min(rows, LANES),)),
        ],
        name="fold",
    )(band_off, band_width, coupling, incident, cotangent)


def layer_source(same, other):
    core = lax.axis_index("layer") & 1

    def read(at, rows):
        mine = same[at >> 1, rows, :]
        return jnp.where((at & 1) == core, mine, other[at >> 1, rows, :])

    return read


def fill_masks(masks):
    row = lax.broadcasted_iota(jnp.int32, (LANES, LANES), 0)
    lane = lax.broadcasted_iota(jnp.int32, (LANES, LANES), 1)
    masks[0] = (lane >= row // BLOCK * BLOCK).astype(jnp.float32).astype(jnp.bfloat16)
    masks[1] = (row >= lane // BLOCK * BLOCK).astype(jnp.float32).astype(jnp.bfloat16)
    masks[2] = (row < LANES - 1).astype(jnp.float32).astype(jnp.bfloat16)


def expand(read, slot, masks, upper, lower):
    tiles = upper.shape[0]
    last_rows = read(slot, slice(tiles * LANES - BLOCK, tiles * LANES))
    last_row = last_rows.astype(jnp.float32)[BLOCK - 1 :, :]
    first = jnp.max(last_row).astype(jnp.int32)
    for t in range(tiles):
        run = read(slot, slice(t * LANES, (t + 1) * LANES))
        if t == tiles - 1:
            run = run * masks[2]
        near = run * masks[0]
        upper[t, :, :LANES] = near
        upper[t, :, LANES:] = run - near
        turned = run.T
        near = turned * masks[1]
        lower[t, :, :LANES] = near
        lower[(t + 1) % tiles, :, LANES:] = turned - near
    return first


def tile_products(parts, matrices):
    fields = parts[0].shape[0]
    none = jnp.zeros_like(parts[0])
    products = []
    for t in range(0, len(parts), 2):
        spread = jnp.concatenate(
            [
                jnp.concatenate([parts[t], none], axis=1),
                jnp.concatenate([none, parts[t + 1]], axis=1),
            ],
            axis=0,
        )
        both = matrices[t : t + 2].reshape(2 * LANES, 2 * LANES)
        product = jnp.dot(spread, both, preferred_element_type=jnp.float32)
        products += [product[:fields], product[fields:]]
    return products


def banded_product(v, upper, lower, start, xs, zs):
    tiles = len(v)
    whole = start >> 3
    fine = (start & (BLOCKS_PER_LANES - 1)) * BLOCK
    lane = lax.broadcasted_iota(jnp.int32, v[0].shape, 1)
    turned = [pltpu.roll(part, (LANES - fine) & (LANES - 1), 1) for part in v]
    for u in range(tiles):
        moved = jnp.where(lane < LANES - fine, turned[u], turned[(u + 1) % tiles])
        xs[u] = moved.astype(jnp.bfloat16)
    first = tile_products([part.astype(jnp.bfloat16) for part in v], upper)
    sums = [first[t][:, :LANES] + first[t - 1][:, LANES:] for t in range(tiles)]
    turned = [pltpu.roll(part, fine, 1) for part in sums]
    for u in range(tiles):
        zs[u] = jnp.where(lane >= fine, turned[u], turned[u - 1])
    second = tile_products([xs[(whole + u) & (tiles - 1)] for u in range(tiles)], lower)
    return [
        zs[(u - whole) & (tiles - 1)]
        - (second[u][:, :LANES] + second[(u + 1) % tiles][:, LANES:])
        for u in range(tiles)
    ]


def run_layer(x, sign, upper, lower, start, xs, zs):
    v = x
    for divisor in range(DEGREE, 0, -1):
        scale = sign * (1.0 / divisor)
        product = banded_product(v, upper, lower, start, xs, zs)
        v = [part + scale * term for part, term in zip(x, product)]
    return v


def cascade(x, forward, read, masks, windows, xs, zs):
    sign = jnp.where(forward, -1.0, 1.0)

    def slot_of(k):
        return jnp.where(forward, k, GROUP - 1 - k)

    def pair(i, carry):
        x, start = carry
        other = expand(read, slot_of(2 * i + 1), masks, *windows[1])
        x = run_layer(x, sign, *windows[0], start, xs, zs)
        following = slot_of(jnp.minimum(2 * i + 2, GROUP - 1))
        start = expand(read, following, masks, *windows[0])
        x = run_layer(x, sign, *windows[1], other, xs, zs)
        return x, start

    tiles = xs.shape[0]
    x = [x[:, u * LANES : (u + 1) * LANES] for u in range(tiles)]
    start = expand(read, slot_of(0), masks, *windows[0])
    x, _ = lax.fori_loop(0, GROUP // 2, pair, (x, start))
    return jnp.concatenate(x, axis=1)


def cascade_kernel(step, groups, shares, same, other, *refs):
    last = step == groups - 1
    if step == 0:
        fields, refs = refs[:shares], refs[shares:]
    else:
        x_ref, kept_forward, kept_adjoint = refs[:3]
        refs = refs[3:]
    outs, (masks, *tiles, xs, zs) = refs[:-7], refs[-7:]
    row = lax.axis_index("row")
    group = lax.axis_index("layer") // GROUP
    fill_masks(masks)
    orders = same.shape[1]
    if step == 0:
        parts = [ref[...] for ref in fields]
        ordered = []
        for want in range(shares):
            chosen = parts[0]
            for mask, part in enumerate(parts):
                chosen = jnp.where((row ^ mask) == want, part, chosen)
            ordered.append(chosen)
        x = jnp.concatenate(ordered, axis=1)
    else:
        x = x_ref[...].astype(jnp.float32)
    forward = group == step
    backward = group == groups - 1 - step
    read = layer_source(same, other)
    x = cascade(x, forward, read, masks, (tiles[:2], tiles[2:]), xs, zs)
    panel = outs[0].shape[-1]
    if not last:
        outs[-1][...] = x.astype(jnp.bfloat16)
    mine = x[:, :panel]
    for index in range(1, orders // panel):
        mine = jnp.where(row == index, x[:, index * panel : (index + 1) * panel], mine)
    if step == 0:
        outs[0][0] = mine
    else:
        outs[0][0] = jnp.where(forward, mine, kept_forward[0])
        outs[1][0] = jnp.where(backward, mine, kept_adjoint[0])


def run_step(step, groups, same, other, fields, kept, panel):
    orders = same.shape[1]
    field_count = fields[0].shape[0]
    kept_shape = jax.ShapeDtypeStruct((1, field_count, panel), jnp.float32)
    out_shape = [kept_shape] if step == 0 else [kept_shape, kept_shape]
    if step < groups - 1:
        out_shape.append(jax.ShapeDtypeStruct((field_count, orders), jnp.bfloat16))
    vmem = pl.BlockSpec(memory_space=pltpu.VMEM)
    tiles = orders // LANES
    window = pltpu.VMEM((tiles, LANES, 2 * LANES), jnp.bfloat16)
    return pl.pallas_call(
        functools.partial(cascade_kernel, step, groups, orders // panel),
        out_shape=out_shape,
        in_specs=[vmem] * (2 + len(fields) + len(kept)),
        out_specs=[vmem] * len(out_shape),
        scratch_shapes=[
            pltpu.VMEM((3, LANES, LANES), jnp.bfloat16),
            window,
            window,
            window,
            window,
            pltpu.VMEM((tiles, field_count, LANES), jnp.bfloat16),
            pltpu.VMEM((tiles, field_count, LANES), jnp.float32),
        ],
        compiler_params=pltpu.CompilerParams(vmem_limit_bytes=24 * 1024 * 1024),
        name=f"cascade_{step}",
    )(same, other, *fields, *kept)


def on_device(coupling, band_off, band_width, incident, cotangent):
    panel, orders = coupling.shape[1:]
    layers = lax.axis_size("layer")
    rows = lax.axis_size("row")
    groups = layers // GROUP

    def across(array, layer_mask, row_mask):
        pairs = [
            (l * rows + r, (l ^ layer_mask) * rows + (r ^ row_mask))
            for l in range(layers)
            for r in range(rows)
        ]
        return lax.ppermute(array, ("layer", "row"), pairs)

    shares = GROUP // 2 * rows
    folded, field = fold(coupling, band_off, band_width, incident, cotangent, shares)
    fields = [field] + [across(field, 0, mask) for mask in range(1, rows)]
    same_core = [
        [l * rows + r for l in range(first, first + GROUP, 2) for r in range(rows)]
        for start in range(0, layers, GROUP)
        for first in (start, start + 1)
    ]
    same = lax.all_to_all(folded, ("layer", "row"), 0, 0, axis_index_groups=same_core)
    same = same.reshape(GROUP // 2, orders, LANES)
    other = across(same, 1, 0)

    kept = []
    for step in range(groups):
        results = run_step(step, groups, same, other, fields, kept, panel)
        if step == groups - 1:
            return tuple(results)
        kept = [results[0], results[0]] if step == 0 else list(results[:2])
        pairs = []
        for index in range(GROUP * rows):
            forward_from = step * GROUP * rows + index
            adjoint_from = (groups - 1 - step) * GROUP * rows + index
            pairs.append((forward_from, forward_from + GROUP * rows))
            pairs.append((adjoint_from, adjoint_from - GROUP * rows))
        fields = [lax.ppermute(results[-1], ("layer", "row"), pairs)]


def solution(mesh):
    in_specs = (P("layer", "row", None), P("layer"), P("layer"), P(None, "row"), P(None, "row"))
    out_specs = (P("layer", None, "row"), P("layer", None, "row"))
    return jax.shard_map(
        on_device, mesh=mesh, in_specs=in_specs, out_specs=out_specs, check_vma=False
    )
```

```python
import functools

import jax
import jax.numpy as jnp
from jax import lax
from jax.experimental import pallas as pl
from jax.experimental.pallas import tpu as pltpu
from jax.sharding import PartitionSpec as P

BLOCK = 16
GROUP = 8
LANES = 128
BLOCKS_PER_LANES = LANES // BLOCK
PACKED = LANES - BLOCK
DEGREE = 4


def fold_kernel(
    off_hbm, width_hbm, coupling_hbm, incident_ref, cotangent_ref,
    folded_ref, field_ref, off_ref, width_ref, coupling_ref, sems,
):
    rows, orders = coupling_hbm.shape[1:]
    chunk = min(rows, LANES)
    copies = [
        pltpu.make_async_copy(off_hbm, off_ref, sems.at[0]),
        pltpu.make_async_copy(width_hbm, width_ref, sems.at[1]),
    ]
    for index in range(rows // chunk):
        here = pl.ds(index * chunk, chunk)
        copies.append(
            pltpu.make_async_copy(
                coupling_hbm.at[0, here], coupling_ref.at[here], sems.at[2 + index]
            )
        )
    for copy in copies:
        copy.start()
    group = lax.axis_index("layer") // GROUP
    field_ref[...] = jnp.where(group == 0, incident_ref[...], cotangent_ref[...])
    copies[0].wait()
    copies[1].wait()
    first = off_ref[0] - width_ref[0]
    last = off_ref[0] + width_ref[0]
    first_block = lax.axis_index("row") * (rows // BLOCK)
    lane = lax.broadcasted_iota(jnp.int32, (BLOCK, LANES), 1)
    sub = lax.broadcasted_iota(jnp.int32, (BLOCK, LANES), 0)
    top = orders // LANES - 1
    for local in range(rows // BLOCK):
        if local * BLOCK % chunk == 0:
            copies[2 + local * BLOCK // chunk].wait()
            runs = []
        block = first_block + local
        start = (block + first) * BLOCK
        tile = start >> 7
        shift = start & (LANES - 1)
        here = slice(local * BLOCK, (local + 1) * BLOCK)

        def part(index):
            column = pl.multiple_of(jnp.clip(index, 0, top) * LANES, LANES)
            return coupling_ref[here, pl.ds(column, LANES)].astype(jnp.float32)

        near = lane >= shift
        column = jnp.where(near, lane, lane + LANES) + tile * LANES
        limit = jnp.minimum((block + last + 1) * BLOCK, orders)
        keep = (column > block * BLOCK + sub) & (column < limit)
        folded = jnp.where(keep, jnp.where(near, part(tile), part(tile + 1)), 0.0)
        is_last = block * BLOCK + sub == orders - 1
        folded = jnp.where(is_last, first.astype(jnp.float32), folded)
        runs.append(pltpu.roll(folded, (-first * BLOCK) & (LANES - 1), 1))
        if len(runs) == BLOCKS_PER_LANES:
            base = local * BLOCK // LANES * PACKED
            for b, run in enumerate(runs[:-1]):
                hole = lane // BLOCK == (b - 1) % BLOCKS_PER_LANES
                folded_ref[base + b * BLOCK : base + (b + 1) * BLOCK, :] = jnp.where(
                    hole, runs[-1], run
                ).astype(jnp.bfloat16)


def fold(coupling, band_off, band_width, incident, cotangent):
    rows, orders = coupling.shape[1:]
    hbm = pl.BlockSpec(memory_space=pltpu.HBM)
    vmem = pl.BlockSpec(memory_space=pltpu.VMEM)
    return pl.pallas_call(
        fold_kernel,
        out_shape=[
            jax.ShapeDtypeStruct((rows // LANES * PACKED, LANES), jnp.bfloat16),
            jax.ShapeDtypeStruct(incident.shape, jnp.float32),
        ],
        in_specs=[hbm, hbm, hbm, vmem, vmem],
        out_specs=[vmem, vmem],
        scratch_shapes=[
            pltpu.SMEM((1,), jnp.int32),
            pltpu.SMEM((1,), jnp.int32),
            pltpu.VMEM((rows, orders), jnp.bfloat16),
            pltpu.SemaphoreType.DMA((2 + rows // min(rows, LANES),)),
        ],
        name="fold",
    )(band_off, band_width, coupling, incident, cotangent)


def batch_kernel(*refs):
    for index, piece in enumerate(refs[:-1]):
        refs[-1][index] = piece[...]


def batch(pieces):
    vmem = pl.BlockSpec(memory_space=pltpu.VMEM)
    return pl.pallas_call(
        batch_kernel,
        out_shape=jax.ShapeDtypeStruct((len(pieces), *pieces[0].shape), pieces[0].dtype),
        in_specs=[vmem] * len(pieces),
        out_specs=vmem,
        name="batch",
    )(*pieces)


def place(pieces, distances, folds):
    slot = lax.axis_index("layer") % GROUP
    row = lax.axis_index("row")
    for (ref, index), (layer_mask, row_mask) in zip(pieces, distances):
        rows = ref.shape[1]
        here = pl.ds(pl.multiple_of((row ^ row_mask) * rows, BLOCK), rows)
        folds[slot ^ layer_mask, here, :] = ref[index]


def fill_masks(masks):
    row = lax.broadcasted_iota(jnp.int32, (LANES, LANES), 0)
    lane = lax.broadcasted_iota(jnp.int32, (LANES, LANES), 1)
    masks[0] = (lane >= row // BLOCK * BLOCK).astype(jnp.float32).astype(jnp.bfloat16)
    masks[1] = (row >= lane // BLOCK * BLOCK).astype(jnp.float32).astype(jnp.bfloat16)
    masks[2] = (row < LANES - 1).astype(jnp.float32).astype(jnp.bfloat16)
    own = lane // BLOCK != (row // BLOCK + BLOCKS_PER_LANES - 1) % BLOCKS_PER_LANES
    masks[3] = own.astype(jnp.float32).astype(jnp.bfloat16)


def expand(folds, slot, masks, upper, lower):
    tiles = upper.shape[0]
    lane = lax.broadcasted_iota(jnp.int32, (1, LANES), 1)
    eighth = folds[slot, (tiles - 1) * PACKED : (tiles - 1) * PACKED + BLOCK, :]
    last_row = eighth.astype(jnp.float32)[BLOCK - 1 :, :]
    last_row = jnp.where(lane >= PACKED, last_row, -float(LANES))
    first = jnp.max(last_row).astype(jnp.int32)
    for t in range(tiles):
        packed = folds[slot, t * PACKED : (t + 1) * PACKED, :]
        own = packed * masks[3, :PACKED, :]
        rest = packed - own
        eighth = [rest[b : b + BLOCK] for b in range(0, PACKED, BLOCK)]
        while len(eighth) > 1:
            eighth = [sum(eighth[i : i + 2][1:], eighth[i]) for i in range(0, len(eighth), 2)]
        run = jnp.concatenate([own, eighth[0]], axis=0)
        if t == tiles - 1:
            run = run * masks[2]
        near = run * masks[0]
        upper[t, :, :LANES] = near
        upper[t, :, LANES:] = run - near
        turned = run.T
        near = turned * masks[1]
        lower[t, :, :LANES] = near
        lower[(t + 1) % tiles, :, LANES:] = turned - near
    return first


def banded_product(v, upper, lower, start, xs, zs):
    tiles = len(v)
    whole = start >> 3
    fine = (start & (BLOCKS_PER_LANES - 1)) * BLOCK
    lane = lax.broadcasted_iota(jnp.int32, v[0].shape, 1)
    turned = [pltpu.roll(part, (LANES - fine) & (LANES - 1), 1) for part in v]
    for u in range(tiles):
        moved = jnp.where(lane < LANES - fine, turned[u], turned[(u + 1) % tiles])
        xs[u] = moved.astype(jnp.bfloat16)
    first = [
        jnp.dot(v[t].astype(jnp.bfloat16), upper[t], preferred_element_type=jnp.float32)
        for t in range(tiles)
    ]
    sums = [first[t][:, :LANES] + first[t - 1][:, LANES:] for t in range(tiles)]
    turned = [pltpu.roll(part, fine, 1) for part in sums]
    for u in range(tiles):
        zs[u] = jnp.where(lane >= fine, turned[u], turned[u - 1])
    second = [
        jnp.dot(
            xs[(whole + u) & (tiles - 1)], lower[u], preferred_element_type=jnp.float32
        )
        for u in range(tiles)
    ]
    return [
        zs[(u - whole) & (tiles - 1)]
        - (second[u][:, :LANES] + second[(u + 1) % tiles][:, LANES:])
        for u in range(tiles)
    ]


def run_layer(x, sign, upper, lower, start, xs, zs):
    v = x
    for divisor in range(DEGREE, 0, -1):
        scale = sign * (1.0 / divisor)
        product = banded_product(v, upper, lower, start, xs, zs)
        v = [part + scale * term for part, term in zip(x, product)]
    return v


def cascade(x, forward, folds, masks, windows, xs, zs):
    sign = jnp.where(forward, -1.0, 1.0)

    def slot_of(k):
        return jnp.where(forward, k, GROUP - 1 - k)

    def pair(i, carry):
        x, start = carry
        other = expand(folds, slot_of(2 * i + 1), masks, *windows[1])
        x = run_layer(x, sign, *windows[0], start, xs, zs)
        following = slot_of(jnp.minimum(2 * i + 2, GROUP - 1))
        start = expand(folds, following, masks, *windows[0])
        x = run_layer(x, sign, *windows[1], other, xs, zs)
        return x, start

    tiles = xs.shape[0]
    x = [x[:, u * LANES : (u + 1) * LANES] for u in range(tiles)]
    start = expand(folds, slot_of(0), masks, *windows[0])
    x, _ = lax.fori_loop(0, GROUP // 2, pair, (x, start))
    return jnp.concatenate(x, axis=1)


def cascade_kernel(step, groups, distances, shares, *refs):
    last = step == groups - 1
    pieces = []
    for count in distances[0]:
        pieces += [(refs[0], index) for index in range(count)]
        refs = refs[1:]
    if step == 0:
        fields, refs = refs[:shares], refs[shares:]
    else:
        x_ref, kept_forward, kept_adjoint = refs[:3]
        refs = refs[3:]
    outs, (folds, masks, *tiles, xs, zs) = refs[:-8], refs[-8:]
    place(pieces, distances[1], folds)
    row = lax.axis_index("row")
    group = lax.axis_index("layer") // GROUP
    fill_masks(masks)
    orders = xs.shape[0] * LANES
    if step == 0:
        parts = [ref[...] for ref in fields]
        ordered = []
        for want in range(shares):
            chosen = parts[0]
            for mask, part in enumerate(parts):
                chosen = jnp.where((row ^ mask) == want, part, chosen)
            ordered.append(chosen)
        x = jnp.concatenate(ordered, axis=1)
    else:
        x = x_ref[...].astype(jnp.float32)
    forward = group == step
    backward = group == groups - 1 - step
    x = cascade(x, forward, folds, masks, (tiles[:2], tiles[2:]), xs, zs)
    panel = outs[0].shape[-1]
    if not last:
        outs[-1][...] = x.astype(jnp.bfloat16)
    mine = x[:, :panel]
    for index in range(1, orders // panel):
        mine = jnp.where(row == index, x[:, index * panel : (index + 1) * panel], mine)
    if step == 0:
        outs[0][0] = mine
    else:
        outs[0][0] = jnp.where(forward, mine, kept_forward[0])
        outs[1][0] = jnp.where(backward, mine, kept_adjoint[0])


def run_step(step, groups, batches, distances, fields, kept, panel, orders):
    field_count = fields[0].shape[0]
    kept_shape = jax.ShapeDtypeStruct((1, field_count, panel), jnp.float32)
    out_shape = [kept_shape] if step == 0 else [kept_shape, kept_shape]
    if step < groups - 1:
        out_shape.append(jax.ShapeDtypeStruct((field_count, orders), jnp.bfloat16))
    vmem = pl.BlockSpec(memory_space=pltpu.VMEM)
    tiles = orders // LANES
    window = pltpu.VMEM((tiles, LANES, 2 * LANES), jnp.bfloat16)
    return pl.pallas_call(
        functools.partial(cascade_kernel, step, groups, distances, orders // panel),
        out_shape=out_shape,
        in_specs=[vmem] * (len(batches) + len(fields) + len(kept)),
        out_specs=[vmem] * len(out_shape),
        scratch_shapes=[
            pltpu.VMEM((GROUP, tiles * PACKED, LANES), jnp.bfloat16),
            pltpu.VMEM((4, LANES, LANES), jnp.bfloat16),
            window,
            window,
            window,
            window,
            pltpu.VMEM((tiles, field_count, LANES), jnp.bfloat16),
            pltpu.VMEM((tiles, field_count, LANES), jnp.float32),
        ],
        compiler_params=pltpu.CompilerParams(vmem_limit_bytes=24 * 1024 * 1024),
        name=f"cascade_{step}",
    )(*batches, *fields, *kept)


def gather_batches(own, across, rows):
    bits = [(0, 1 << b) for b in range(rows.bit_length() - 1)]
    bits += [(1 << b, 0) for b in range(1, GROUP.bit_length() - 1)]
    count = len(bits)

    def members(subset):
        return [b for b in range(count) if subset >> b & 1]

    def distance(subset):
        return tuple(sum(bits[b][axis] for b in members(subset)) for axis in (0, 1))

    subsets = sorted(range(1 << count), key=lambda m: (m.bit_count(), m))
    pieces = {0: own}
    for subset in subsets[1 : count + 1] + subsets[-1:]:
        pieces[subset] = across(own, *distance(subset))
    for subset in subsets[count + 1 : -1]:
        which = members(subset)
        link = next((b for b in which if (b + 1) % count in which), which[0])
        pieces[subset] = across(pieces[subset ^ 1 << link], *distance(1 << link))
    batches, counts, distances = [], [], []
    for part in (subsets[: count + 1], subsets[count + 1 :]):
        mine = batch([pieces[subset] for subset in part])
        batches += [mine, across(mine, 1, 0)]
        counts += [len(part), len(part)]
        distances += [distance(subset) for subset in part]
        distances += [(a ^ 1, b) for a, b in distances[-len(part) :]]
    return batches, (tuple(counts), tuple(distances))


def on_device(coupling, band_off, band_width, incident, cotangent):
    panel, orders = coupling.shape[1:]
    layers = lax.axis_size("layer")
    rows = lax.axis_size("row")
    groups = layers // GROUP

    def across(array, layer_mask, row_mask):
        pairs = [
            (l * rows + r, (l ^ layer_mask) * rows + (r ^ row_mask))
            for l in range(layers)
            for r in range(rows)
        ]
        return lax.ppermute(array, ("layer", "row"), pairs)

    folded, field = fold(coupling, band_off, band_width, incident, cotangent)
    fields = [field] + [across(field, 0, mask) for mask in range(1, rows)]
    batches, distances = gather_batches(folded, across, rows)

    kept = []
    for step in range(groups):
        results = run_step(
            step, groups, batches, distances, fields, kept, panel, orders
        )
        if step == groups - 1:
            return tuple(results)
        kept = [results[0], results[0]] if step == 0 else list(results[:2])
        pairs = []
        for index in range(GROUP * rows):
            forward_from = step * GROUP * rows + index
            adjoint_from = (groups - 1 - step) * GROUP * rows + index
            pairs.append((forward_from, forward_from + GROUP * rows))
            pairs.append((adjoint_from, adjoint_from - GROUP * rows))
        fields = [lax.ppermute(results[-1], ("layer", "row"), pairs)]


def solution(mesh):
    in_specs = (P("layer", "row", None), P("layer"), P("layer"), P(None, "row"), P(None, "row"))
    out_specs = (P("layer", None, "row"), P("layer", None, "row"))
    return jax.shard_map(
        on_device, mesh=mesh, in_specs=in_specs, out_specs=out_specs, check_vma=False
    )
```

```python
import functools

import jax
import jax.numpy as jnp
from jax import lax
from jax.experimental import pallas as pl
from jax.experimental.pallas import tpu as pltpu
from jax.sharding import PartitionSpec as P

BLOCK = 16
GROUP = 8
LANES = 128
BLOCKS_PER_LANES = LANES // BLOCK
PACKED = LANES - BLOCK
DEGREE = 4
SMALL_GRANT = 4 * 1024 * 1024
FIELD_PARTS = GROUP // 2


def field_rows(fields, panel):
    return -(-fields // FIELD_PARTS * (panel // LANES) // BLOCK) * BLOCK


def fold_kernel(
    off_ref, width_ref, coupling_ref, incident_ref, cotangent_ref, folded_ref, field_ref
):
    rows, orders = coupling_ref.shape[1:]
    slot = lax.axis_index("layer") % GROUP
    group = lax.axis_index("layer") // GROUP
    field_ref[...] = jnp.where(group == 0, incident_ref[...], cotangent_ref[...])
    fields, panel = field_ref.shape
    part = fields // FIELD_PARTS
    mine = field_ref[pl.ds(pl.multiple_of(slot // 2 * part, part), part), :]
    sent = [mine[:, u : u + LANES] for u in range(0, panel, LANES)]
    spare = field_rows(fields, panel) - part * len(sent)
    if spare:
        sent.append(jnp.zeros((spare, LANES), jnp.float32))
    sent = jnp.concatenate(sent, axis=0).astype(jnp.bfloat16)
    folded_ref[panel // LANES * PACKED :, :] = sent
    first = off_ref[0] - width_ref[0]
    last = off_ref[0] + width_ref[0]
    first_block = lax.axis_index("row") * (rows // BLOCK)
    lane = lax.broadcasted_iota(jnp.int32, (BLOCK, LANES), 1)
    sub = lax.broadcasted_iota(jnp.int32, (BLOCK, LANES), 0)
    top = orders // LANES - 1
    for local in range(rows // BLOCK):
        if local % BLOCKS_PER_LANES == 0:
            runs = []
        block = first_block + local
        start = (block + first) * BLOCK
        tile = start >> 7
        shift = start & (LANES - 1)
        here = slice(local * BLOCK, (local + 1) * BLOCK)

        def part(index):
            column = pl.multiple_of(jnp.clip(index, 0, top) * LANES, LANES)
            return coupling_ref[0, here, pl.ds(column, LANES)].astype(jnp.float32)

        near = lane >= shift
        column = jnp.where(near, lane, lane + LANES) + tile * LANES
        limit = jnp.minimum((block + last + 1) * BLOCK, orders)
        keep = (column > block * BLOCK + sub) & (column < limit)
        folded = jnp.where(keep, jnp.where(near, part(tile), part(tile + 1)), 0.0)
        is_last = block * BLOCK + sub == orders - 1
        folded = jnp.where(is_last, first.astype(jnp.float32), folded)
        runs.append(pltpu.roll(folded, (-first * BLOCK) & (LANES - 1), 1))
        if len(runs) == BLOCKS_PER_LANES:
            base = local * BLOCK // LANES * PACKED
            for b, run in enumerate(runs[:-1]):
                hole = lane // BLOCK == (b - 1) % BLOCKS_PER_LANES
                folded_ref[base + b * BLOCK : base + (b + 1) * BLOCK, :] = jnp.where(
                    hole, runs[-1], run
                ).astype(jnp.bfloat16)


def fold(coupling, band_off, band_width, incident, cotangent):
    rows, orders = coupling.shape[1:]
    sent = rows // LANES * PACKED + field_rows(*incident.shape)
    smem = pl.BlockSpec(memory_space=pltpu.SMEM)
    vmem = pl.BlockSpec(memory_space=pltpu.VMEM)
    return pl.pallas_call(
        fold_kernel,
        out_shape=[
            jax.ShapeDtypeStruct((sent, LANES), jnp.bfloat16),
            jax.ShapeDtypeStruct(incident.shape, jnp.float32),
        ],
        in_specs=[smem, smem, vmem, vmem, vmem],
        out_specs=[vmem, vmem],
        compiler_params=pltpu.CompilerParams(vmem_limit_bytes=SMALL_GRANT),
        name="fold",
    )(band_off, band_width, coupling, incident, cotangent)


def batch_kernel(*refs):
    for index, piece in enumerate(refs[:-1]):
        refs[-1][index] = piece[...]


def batch(pieces):
    vmem = pl.BlockSpec(memory_space=pltpu.VMEM)
    return pl.pallas_call(
        batch_kernel,
        out_shape=jax.ShapeDtypeStruct((len(pieces), *pieces[0].shape), pieces[0].dtype),
        in_specs=[vmem] * len(pieces),
        out_specs=vmem,
        compiler_params=pltpu.CompilerParams(vmem_limit_bytes=SMALL_GRANT),
        name="batch",
    )(*pieces)


def place(pieces, distances, folds):
    slot = lax.axis_index("layer") % GROUP
    row = lax.axis_index("row")
    rows = folds.shape[1] // lax.axis_size("row")
    for (ref, index), (layer_mask, row_mask) in zip(pieces, distances):
        here = pl.ds(pl.multiple_of((row ^ row_mask) * rows, BLOCK), rows)
        folds[slot ^ layer_mask, here, :] = ref[index, :rows, :]


def place_field(own, pieces, distances, field):
    slot = lax.axis_index("layer") % GROUP
    row = lax.axis_index("row")
    fields, panel = own.shape
    part, tiles = fields // FIELD_PARTS, panel // LANES
    for u in range(tiles):
        field[row * tiles + u] = own[:, u * LANES : (u + 1) * LANES]
    for (ref, index), (layer_mask, row_mask) in zip(pieces, distances):
        if row_mask and not layer_mask & 1:
            here = pl.ds(pl.multiple_of((slot ^ layer_mask) // 2 * part, part), part)
            sent = ref[index, tiles * PACKED :, :].astype(jnp.float32)
            for u in range(tiles):
                field[(row ^ row_mask) * tiles + u, here, :] = sent[u * part : (u + 1) * part]


def fill_masks(masks):
    row = lax.broadcasted_iota(jnp.int32, (LANES, LANES), 0)
    lane = lax.broadcasted_iota(jnp.int32, (LANES, LANES), 1)
    masks[0] = (lane >= row // BLOCK * BLOCK).astype(jnp.float32).astype(jnp.bfloat16)
    masks[1] = (row >= lane // BLOCK * BLOCK).astype(jnp.float32).astype(jnp.bfloat16)
    masks[2] = (row < LANES - 1).astype(jnp.float32).astype(jnp.bfloat16)
    own = lane // BLOCK != (row // BLOCK + BLOCKS_PER_LANES - 1) % BLOCKS_PER_LANES
    masks[3] = own.astype(jnp.float32).astype(jnp.bfloat16)


def expand(folds, slot, masks, upper, lower):
    tiles = upper.shape[0]
    lane = lax.broadcasted_iota(jnp.int32, (1, LANES), 1)
    eighth = folds[slot, (tiles - 1) * PACKED : (tiles - 1) * PACKED + BLOCK, :]
    last_row = eighth.astype(jnp.float32)[BLOCK - 1 :, :]
    last_row = jnp.where(lane >= PACKED, last_row, -float(LANES))
    first = jnp.max(last_row).astype(jnp.int32)
    for t in range(tiles):
        packed = folds[slot, t * PACKED : (t + 1) * PACKED, :]
        own = packed * masks[3, :PACKED, :]
        rest = packed - own
        eighth = [rest[b : b + BLOCK] for b in range(0, PACKED, BLOCK)]
        while len(eighth) > 1:
            eighth = [sum(eighth[i : i + 2][1:], eighth[i]) for i in range(0, len(eighth), 2)]
        run = jnp.concatenate([own, eighth[0]], axis=0)
        if t == tiles - 1:
            run = run * masks[2]
        near = run * masks[0]
        upper[t, :, :LANES] = near
        upper[t, :, LANES:] = run - near
        turned = run.T
        near = turned * masks[1]
        lower[t, :, :LANES] = near
        lower[(t + 1) % tiles, :, LANES:] = turned - near
    return first


def banded_product(v, upper, lower, start, xs, zs):
    tiles = len(v)
    whole = start >> 3
    fine = (start & (BLOCKS_PER_LANES - 1)) * BLOCK
    lane = lax.broadcasted_iota(jnp.int32, v[0].shape, 1)
    turned = [pltpu.roll(part, (LANES - fine) & (LANES - 1), 1) for part in v]
    for u in range(tiles):
        moved = jnp.where(lane < LANES - fine, turned[u], turned[(u + 1) % tiles])
        xs[u] = moved.astype(jnp.bfloat16)
    first = [
        jnp.dot(v[t].astype(jnp.bfloat16), upper[t], preferred_element_type=jnp.float32)
        for t in range(tiles)
    ]
    sums = [first[t][:, :LANES] + first[t - 1][:, LANES:] for t in range(tiles)]
    turned = [pltpu.roll(part, fine, 1) for part in sums]
    for u in range(tiles):
        zs[u] = jnp.where(lane >= fine, turned[u], turned[u - 1])
    second = [
        jnp.dot(
            xs[(whole + u) & (tiles - 1)], lower[u], preferred_element_type=jnp.float32
        )
        for u in range(tiles)
    ]
    return [
        zs[(u - whole) & (tiles - 1)]
        - (second[u][:, :LANES] + second[(u + 1) % tiles][:, LANES:])
        for u in range(tiles)
    ]


def run_layer(x, sign, upper, lower, start, xs, zs):
    v = x
    for divisor in range(DEGREE, 0, -1):
        scale = sign * (1.0 / divisor)
        product = banded_product(v, upper, lower, start, xs, zs)
        v = [part + scale * term for part, term in zip(x, product)]
    return v


def cascade(x, forward, folds, masks, windows, xs, zs):
    sign = jnp.where(forward, -1.0, 1.0)

    def slot_of(k):
        return jnp.where(forward, k, GROUP - 1 - k)

    def pair(i, carry):
        x, start = carry
        other = expand(folds, slot_of(2 * i + 1), masks, *windows[1])
        x = run_layer(x, sign, *windows[0], start, xs, zs)
        following = slot_of(jnp.minimum(2 * i + 2, GROUP - 1))
        start = expand(folds, following, masks, *windows[0])
        x = run_layer(x, sign, *windows[1], other, xs, zs)
        return x, start

    start = expand(folds, slot_of(0), masks, *windows[0])
    x, _ = lax.fori_loop(0, GROUP // 2, pair, (x, start))
    return jnp.concatenate(x, axis=1)


def cascade_kernel(step, groups, distances, *refs):
    last = step == groups - 1
    pieces = []
    for count in distances[0]:
        pieces += [(refs[0], index) for index in range(count)]
        refs = refs[1:]
    x_ref, *refs = refs
    kept, refs = (refs[:2], refs[2:]) if step else ((), refs)
    outs, (folds, masks, *tiles, xs, zs) = refs[:-8], refs[-8:]
    place(pieces, distances[1], folds)
    row = lax.axis_index("row")
    group = lax.axis_index("layer") // GROUP
    fill_masks(masks)
    orders = xs.shape[0] * LANES
    if step == 0:
        place_field(x_ref, pieces, distances[1], zs)
        x = [zs[u] for u in range(orders // LANES)]
    else:
        x = x_ref[...].astype(jnp.float32)
        x = [x[:, u : u + LANES] for u in range(0, orders, LANES)]
    forward = group == step
    backward = group == groups - 1 - step
    x = cascade(x, forward, folds, masks, (tiles[:2], tiles[2:]), xs, zs)
    panel = outs[0].shape[-1]
    if not last:
        outs[-1][...] = x.astype(jnp.bfloat16)
    mine = x[:, :panel]
    for index in range(1, orders // panel):
        mine = jnp.where(row == index, x[:, index * panel : (index + 1) * panel], mine)
    if step == 0:
        outs[0][0] = mine
    else:
        outs[0][0] = jnp.where(forward, mine, kept[0][0])
        outs[1][0] = jnp.where(backward, mine, kept[1][0])


def run_step(step, groups, batches, distances, field, kept, panel, orders):
    field_count = field.shape[0]
    kept_shape = jax.ShapeDtypeStruct((1, field_count, panel), jnp.float32)
    out_shape = [kept_shape] if step == 0 else [kept_shape, kept_shape]
    if step < groups - 1:
        out_shape.append(jax.ShapeDtypeStruct((field_count, orders), jnp.bfloat16))
    vmem = pl.BlockSpec(memory_space=pltpu.VMEM)
    tiles = orders // LANES
    window = pltpu.VMEM((tiles, LANES, 2 * LANES), jnp.bfloat16)
    return pl.pallas_call(
        functools.partial(cascade_kernel, step, groups, distances),
        out_shape=out_shape,
        in_specs=[vmem] * (len(batches) + 1 + len(kept)),
        out_specs=[vmem] * len(out_shape),
        scratch_shapes=[
            pltpu.VMEM((GROUP, tiles * PACKED, LANES), jnp.bfloat16),
            pltpu.VMEM((4, LANES, LANES), jnp.bfloat16),
            window,
            window,
            window,
            window,
            pltpu.VMEM((tiles, field_count, LANES), jnp.bfloat16),
            pltpu.VMEM((tiles, field_count, LANES), jnp.float32),
        ],
        compiler_params=pltpu.CompilerParams(vmem_limit_bytes=24 * 1024 * 1024),
        name=f"cascade_{step}",
    )(*batches, field, *kept)


def gather_batches(own, across, rows):
    bits = [(0, 1 << b) for b in range(rows.bit_length() - 1)]
    bits += [(1 << b, 0) for b in range(1, GROUP.bit_length() - 1)]
    count = len(bits)

    def members(subset):
        return [b for b in range(count) if subset >> b & 1]

    def distance(subset):
        return tuple(sum(bits[b][axis] for b in members(subset)) for axis in (0, 1))

    subsets = sorted(range(1 << count), key=lambda m: (m.bit_count(), m))
    pieces = {0: own}
    for subset in subsets[1 : count + 1] + subsets[-1:]:
        pieces[subset] = across(own, *distance(subset))
    for subset in subsets[count + 1 : -1]:
        which = members(subset)
        link = next((b for b in which if (b + 1) % count in which), which[0])
        pieces[subset] = across(pieces[subset ^ 1 << link], *distance(1 << link))
    batches, counts, distances = [], [], []
    for part in (subsets[: count + 1], subsets[count + 1 :]):
        mine = batch([pieces[subset] for subset in part])
        batches += [mine, across(mine, 1, 0)]
        counts += [len(part), len(part)]
        distances += [distance(subset) for subset in part]
        distances += [(a ^ 1, b) for a, b in distances[-len(part) :]]
    return batches, (tuple(counts), tuple(distances))


def on_device(coupling, band_off, band_width, incident, cotangent):
    panel, orders = coupling.shape[1:]
    layers = lax.axis_size("layer")
    rows = lax.axis_size("row")
    groups = layers // GROUP

    def across(array, layer_mask, row_mask):
        pairs = [
            (l * rows + r, (l ^ layer_mask) * rows + (r ^ row_mask))
            for l in range(layers)
            for r in range(rows)
        ]
        return lax.ppermute(array, ("layer", "row"), pairs)

    folded, field = fold(coupling, band_off, band_width, incident, cotangent)
    batches, distances = gather_batches(folded, across, rows)

    kept = []
    for step in range(groups):
        results = run_step(step, groups, batches, distances, field, kept, panel, orders)
        if step == groups - 1:
            return tuple(results)
        kept = [results[0], results[0]] if step == 0 else list(results[:2])
        pairs = []
        for index in range(GROUP * rows):
            forward_from = step * GROUP * rows + index
            adjoint_from = (groups - 1 - step) * GROUP * rows + index
            pairs.append((forward_from, forward_from + GROUP * rows))
            pairs.append((adjoint_from, adjoint_from - GROUP * rows))
        field = lax.ppermute(results[-1], ("layer", "row"), pairs)


def solution(mesh):
    in_specs = (P("layer", "row", None), P("layer"), P("layer"), P(None, "row"), P(None, "row"))
    out_specs = (P("layer", None, "row"), P("layer", None, "row"))
    return jax.shard_map(
        on_device, mesh=mesh, in_specs=in_specs, out_specs=out_specs, check_vma=False
    )
```

```python
import functools

import jax
import jax.numpy as jnp
from jax import lax
from jax.experimental import pallas as pl
from jax.experimental.pallas import tpu as pltpu
from jax.sharding import PartitionSpec as P

BLOCK = 16
GROUP = 8
LANES = 128
BLOCKS_PER_LANES = LANES // BLOCK
PACKED = LANES - BLOCK
DEGREE = 4
SMALL_GRANT = 4 * 1024 * 1024
FIELD_PARTS = GROUP // 2


def field_rows(fields, panel):
    return -(-fields // FIELD_PARTS * (panel // LANES) // BLOCK) * BLOCK


def fold_kernel(
    off_ref, width_ref, coupling_ref, field_ref, folded_ref
):
    rows, orders = coupling_ref.shape[1:]
    slot = lax.axis_index("layer") % GROUP
    fields, panel = field_ref.shape
    part = fields // FIELD_PARTS
    mine = field_ref[pl.ds(pl.multiple_of(slot // 2 * part, part), part), :]
    sent = [mine[:, u : u + LANES] for u in range(0, panel, LANES)]
    spare = field_rows(fields, panel) - part * len(sent)
    if spare:
        sent.append(jnp.zeros((spare, LANES), jnp.float32))
    sent = jnp.concatenate(sent, axis=0).astype(jnp.bfloat16)
    folded_ref[panel // LANES * PACKED :, :] = sent
    first = off_ref[0] - width_ref[0]
    last = off_ref[0] + width_ref[0]
    first_block = lax.axis_index("row") * (rows // BLOCK)
    lane = lax.broadcasted_iota(jnp.int32, (BLOCK, LANES), 1)
    sub = lax.broadcasted_iota(jnp.int32, (BLOCK, LANES), 0)
    top = orders // LANES - 1
    for local in range(rows // BLOCK):
        if local % BLOCKS_PER_LANES == 0:
            runs = []
        block = first_block + local
        start = (block + first) * BLOCK
        tile = start >> 7
        shift = start & (LANES - 1)
        here = slice(local * BLOCK, (local + 1) * BLOCK)

        def part(index):
            column = pl.multiple_of(jnp.clip(index, 0, top) * LANES, LANES)
            return coupling_ref[0, here, pl.ds(column, LANES)].astype(jnp.float32)

        near = lane >= shift
        column = jnp.where(near, lane, lane + LANES) + tile * LANES
        limit = jnp.minimum((block + last + 1) * BLOCK, orders)
        keep = (column > block * BLOCK + sub) & (column < limit)
        folded = jnp.where(keep, jnp.where(near, part(tile), part(tile + 1)), 0.0)
        is_last = block * BLOCK + sub == orders - 1
        folded = jnp.where(is_last, first.astype(jnp.float32), folded)
        runs.append(pltpu.roll(folded, (-first * BLOCK) & (LANES - 1), 1))
        if len(runs) == BLOCKS_PER_LANES:
            base = local * BLOCK // LANES * PACKED
            for b, run in enumerate(runs[:-1]):
                hole = lane // BLOCK == (b - 1) % BLOCKS_PER_LANES
                folded_ref[base + b * BLOCK : base + (b + 1) * BLOCK, :] = jnp.where(
                    hole, runs[-1], run
                ).astype(jnp.bfloat16)


def fold(coupling, band_off, band_width, field):
    rows, orders = coupling.shape[1:]
    sent = rows // LANES * PACKED + field_rows(*field.shape)
    smem = pl.BlockSpec(memory_space=pltpu.SMEM)
    vmem = pl.BlockSpec(memory_space=pltpu.VMEM)
    return pl.pallas_call(
        fold_kernel,
        out_shape=jax.ShapeDtypeStruct((sent, LANES), jnp.bfloat16),
        in_specs=[smem, smem, vmem, vmem],
        out_specs=vmem,
        compiler_params=pltpu.CompilerParams(vmem_limit_bytes=SMALL_GRANT),
        name="fold",
    )(band_off, band_width, coupling, field)


def batch_kernel(*refs):
    for index, piece in enumerate(refs[:-1]):
        refs[-1][index] = piece[...]


def batch(pieces):
    vmem = pl.BlockSpec(memory_space=pltpu.VMEM)
    return pl.pallas_call(
        batch_kernel,
        out_shape=jax.ShapeDtypeStruct((len(pieces), *pieces[0].shape), pieces[0].dtype),
        in_specs=[vmem] * len(pieces),
        out_specs=vmem,
        compiler_params=pltpu.CompilerParams(vmem_limit_bytes=SMALL_GRANT),
        name="batch",
    )(*pieces)


def place(pieces, distances, folds):
    slot = lax.axis_index("layer") % GROUP
    row = lax.axis_index("row")
    rows = folds.shape[1] // lax.axis_size("row")
    for (ref, index), (layer_mask, row_mask) in zip(pieces, distances):
        here = pl.ds(pl.multiple_of((row ^ row_mask) * rows, BLOCK), rows)
        folds[slot ^ layer_mask, here, :] = ref[index, :rows, :]


def place_field(own, pieces, distances, field):
    slot = lax.axis_index("layer") % GROUP
    row = lax.axis_index("row")
    fields, panel = own.shape
    part, tiles = fields // FIELD_PARTS, panel // LANES
    for u in range(tiles):
        field[row * tiles + u] = own[:, u * LANES : (u + 1) * LANES]
    for (ref, index), (layer_mask, row_mask) in zip(pieces, distances):
        if row_mask and not layer_mask & 1:
            here = pl.ds(pl.multiple_of((slot ^ layer_mask) // 2 * part, part), part)
            sent = ref[index, tiles * PACKED :, :].astype(jnp.float32)
            for u in range(tiles):
                field[(row ^ row_mask) * tiles + u, here, :] = sent[u * part : (u + 1) * part]


def fill_masks(masks):
    row = lax.broadcasted_iota(jnp.int32, (LANES, LANES), 0)
    lane = lax.broadcasted_iota(jnp.int32, (LANES, LANES), 1)
    masks[0] = (lane >= row // BLOCK * BLOCK).astype(jnp.float32).astype(jnp.bfloat16)
    masks[1] = (row >= lane // BLOCK * BLOCK).astype(jnp.float32).astype(jnp.bfloat16)
    masks[2] = (row < LANES - 1).astype(jnp.float32).astype(jnp.bfloat16)
    own = lane // BLOCK != (row // BLOCK + BLOCKS_PER_LANES - 1) % BLOCKS_PER_LANES
    masks[3] = own.astype(jnp.float32).astype(jnp.bfloat16)


def expand(folds, slot, masks, upper, lower):
    tiles = upper.shape[0]
    lane = lax.broadcasted_iota(jnp.int32, (1, LANES), 1)
    eighth = folds[slot, (tiles - 1) * PACKED : (tiles - 1) * PACKED + BLOCK, :]
    last_row = eighth.astype(jnp.float32)[BLOCK - 1 :, :]
    last_row = jnp.where(lane >= PACKED, last_row, -float(LANES))
    first = jnp.max(last_row).astype(jnp.int32)
    for t in range(tiles):
        packed = folds[slot, t * PACKED : (t + 1) * PACKED, :]
        own = packed * masks[3, :PACKED, :]
        rest = packed - own
        eighth = [rest[b : b + BLOCK] for b in range(0, PACKED, BLOCK)]
        while len(eighth) > 1:
            eighth = [sum(eighth[i : i + 2][1:], eighth[i]) for i in range(0, len(eighth), 2)]
        run = jnp.concatenate([own, eighth[0]], axis=0)
        if t == tiles - 1:
            run = run * masks[2]
        near = run * masks[0]
        upper[t, :, :LANES] = near
        upper[t, :, LANES:] = run - near
        turned = run.T
        near = turned * masks[1]
        lower[t, :, :LANES] = near
        lower[(t + 1) % tiles, :, LANES:] = turned - near
    return first


def banded_product(v, upper, lower, start, xs, zs):
    tiles = len(v)
    whole = start >> 3
    fine = (start & (BLOCKS_PER_LANES - 1)) * BLOCK
    lane = lax.broadcasted_iota(jnp.int32, v[0].shape, 1)
    turned = [pltpu.roll(part, (LANES - fine) & (LANES - 1), 1) for part in v]
    for u in range(tiles):
        moved = jnp.where(lane < LANES - fine, turned[u], turned[(u + 1) % tiles])
        xs[u] = moved.astype(jnp.bfloat16)
    first = [
        jnp.dot(v[t].astype(jnp.bfloat16), upper[t], preferred_element_type=jnp.float32)
        for t in range(tiles)
    ]
    sums = [first[t][:, :LANES] + first[t - 1][:, LANES:] for t in range(tiles)]
    turned = [pltpu.roll(part, fine, 1) for part in sums]
    for u in range(tiles):
        zs[u] = jnp.where(lane >= fine, turned[u], turned[u - 1])
    second = [
        jnp.dot(
            xs[(whole + u) & (tiles - 1)], lower[u], preferred_element_type=jnp.float32
        )
        for u in range(tiles)
    ]
    return [
        zs[(u - whole) & (tiles - 1)]
        - (second[u][:, :LANES] + second[(u + 1) % tiles][:, LANES:])
        for u in range(tiles)
    ]


def run_layer(x, sign, upper, lower, start, xs, zs):
    v = x
    for divisor in range(DEGREE, 0, -1):
        scale = sign * (1.0 / divisor)
        product = banded_product(v, upper, lower, start, xs, zs)
        v = [part + scale * term for part, term in zip(x, product)]
    return v


def cascade_first_kernel(distances, *refs):
    pieces = []
    for count in distances[0]:
        pieces += [(refs[0], index) for index in range(count)]
        refs = refs[1:]
    own, kept, upper, lower, starts, send, folds, masks, xs, zs = refs
    place(pieces, distances[1], folds)
    fill_masks(masks)
    place_field(own, pieces, distances[1], zs)
    x = [zs[u] for u in range(zs.shape[0])]
    forward = lax.axis_index("layer") // GROUP == 0
    sign = jnp.where(forward, -1.0, 1.0)

    def prepare(k):
        slot = jnp.where(forward, k, GROUP - 1 - k)
        start = expand(folds, slot, masks, upper.at[k], lower.at[k])
        starts[k : k + 1, :] = jnp.full((1, LANES), start, jnp.int32)
        return start

    start = prepare(0)
    for k in range(GROUP):
        following = prepare(k + 1) if k + 1 < GROUP else None
        x = run_layer(x, sign, upper.at[k], lower.at[k], start, xs, zs)
        start = following
    finish(x, kept, send)


def cascade_next_kernel(step, groups, *refs):
    upper, lower, starts, field, kept_forward, kept_adjoint = refs[:6]
    new_forward, new_adjoint, *send, xs, zs = refs[6:]
    group = lax.axis_index("layer") // GROUP
    forward = group == step
    backward = group == groups - 1 - step
    sign = jnp.where(forward, -1.0, 1.0)
    same_order = forward == (group == 0)
    x = field[...].astype(jnp.float32)
    x = [x[:, u : u + LANES] for u in range(0, x.shape[1], LANES)]

    def layer(k, x):
        at = jnp.where(same_order, k, GROUP - 1 - k)
        start = jnp.max(starts[pl.ds(at, 1), :])
        return run_layer(x, sign, upper.at[at], lower.at[at], start, xs, zs)

    x = lax.fori_loop(0, GROUP, layer, x)
    finish(x, new_forward, *send)
    mine = new_forward[0]
    new_forward[0] = jnp.where(forward, mine, kept_forward[0])
    new_adjoint[0] = jnp.where(backward, mine, kept_adjoint[0])


def finish(x, mine_ref, send=None):
    row = lax.axis_index("row")
    panel = mine_ref.shape[-1]
    if send is not None:
        for u, part in enumerate(x):
            send[:, u * LANES : (u + 1) * LANES] = part.astype(jnp.bfloat16)
    tiles = panel // LANES
    for u in range(tiles):
        mine = x[u]
        for index in range(1, len(x) // tiles):
            mine = jnp.where(row == index, x[index * tiles + u], mine)
        mine_ref[0, :, u * LANES : (u + 1) * LANES] = mine


def run_first(batches, distances, field, orders):
    count, panel = field.shape
    tiles = orders // LANES
    vmem = pl.BlockSpec(memory_space=pltpu.VMEM)
    window = jax.ShapeDtypeStruct((GROUP, tiles, LANES, 2 * LANES), jnp.bfloat16)
    return pl.pallas_call(
        functools.partial(cascade_first_kernel, distances),
        out_shape=[
            jax.ShapeDtypeStruct((1, count, panel), jnp.float32),
            window,
            window,
            jax.ShapeDtypeStruct((GROUP, LANES), jnp.int32),
            jax.ShapeDtypeStruct((count, orders), jnp.bfloat16),
        ],
        in_specs=[vmem] * (len(batches) + 1),
        out_specs=[vmem] * 5,
        scratch_shapes=[
            pltpu.VMEM((GROUP, tiles * PACKED, LANES), jnp.bfloat16),
            pltpu.VMEM((4, LANES, LANES), jnp.bfloat16),
            pltpu.VMEM((tiles, count, LANES), jnp.bfloat16),
            pltpu.VMEM((tiles, count, LANES), jnp.float32),
        ],
        compiler_params=pltpu.CompilerParams(vmem_limit_bytes=24 * 1024 * 1024),
        name="cascade_first",
    )(*batches, field)


def run_next(step, groups, upper, lower, starts, field, kept):
    count, orders = field.shape
    tiles = orders // LANES
    vmem = pl.BlockSpec(memory_space=pltpu.VMEM)
    out_shape = [jax.ShapeDtypeStruct(kept[0].shape, jnp.float32)] * 2
    if step < groups - 1:
        out_shape.append(jax.ShapeDtypeStruct(field.shape, jnp.bfloat16))
    return pl.pallas_call(
        functools.partial(cascade_next_kernel, step, groups),
        out_shape=out_shape,
        in_specs=[vmem] * 6,
        out_specs=[vmem] * len(out_shape),
        scratch_shapes=[
            pltpu.VMEM((tiles, count, LANES), jnp.bfloat16),
            pltpu.VMEM((tiles, count, LANES), jnp.float32),
        ],
        compiler_params=pltpu.CompilerParams(vmem_limit_bytes=24 * 1024 * 1024),
        name=f"cascade_{step}",
    )(upper, lower, starts, field, *kept)


def gather_batches(own, across, rows):
    bits = [(0, 1 << b) for b in range(rows.bit_length() - 1)]
    bits += [(1 << b, 0) for b in range(1, GROUP.bit_length() - 1)]
    count = len(bits)

    def members(subset):
        return [b for b in range(count) if subset >> b & 1]

    def distance(subset):
        return tuple(sum(bits[b][axis] for b in members(subset)) for axis in (0, 1))

    subsets = sorted(range(1 << count), key=lambda m: (m.bit_count(), m))
    pieces = {0: own}
    for subset in subsets[1 : count + 1] + subsets[-1:]:
        pieces[subset] = across(own, *distance(subset))
    for subset in subsets[count + 1 : -1]:
        which = members(subset)
        link = next((b for b in which if (b + 1) % count in which), which[0])
        pieces[subset] = across(pieces[subset ^ 1 << link], *distance(1 << link))
    batches, counts, distances = [], [], []
    for part in (subsets[: count + 1], subsets[count + 1 :]):
        mine = batch([pieces[subset] for subset in part])
        batches += [mine, across(mine, 1, 0)]
        counts += [len(part), len(part)]
        distances += [distance(subset) for subset in part]
        distances += [(a ^ 1, b) for a, b in distances[-len(part) :]]
    return batches, (tuple(counts), tuple(distances))


def on_device(coupling, band_off, band_width, incident, cotangent):
    panel, orders = coupling.shape[1:]
    layers = lax.axis_size("layer")
    rows = lax.axis_size("row")
    groups = layers // GROUP

    def across(array, layer_mask, row_mask):
        pairs = [
            (l * rows + r, (l ^ layer_mask) * rows + (r ^ row_mask))
            for l in range(layers)
            for r in range(rows)
        ]
        return lax.ppermute(array, ("layer", "row"), pairs)

    field = jnp.where(lax.axis_index("layer") // GROUP == 0, incident, cotangent)
    folded = fold(coupling, band_off, band_width, field)
    batches, distances = gather_batches(folded, across, rows)

    mine, upper, lower, starts, send = run_first(batches, distances, field, orders)
    kept = [mine, mine]
    for step in range(1, groups):
        pairs = []
        for index in range(GROUP * rows):
            forward_from = (step - 1) * GROUP * rows + index
            adjoint_from = (groups - step) * GROUP * rows + index
            pairs.append((forward_from, forward_from + GROUP * rows))
            pairs.append((adjoint_from, adjoint_from - GROUP * rows))
        field = lax.ppermute(send, ("layer", "row"), pairs)
        *kept, send = [*run_next(step, groups, upper, lower, starts, field, kept), None][:3]
    return tuple(kept)


def solution(mesh):
    in_specs = (P("layer", "row", None), P("layer"), P("layer"), P(None, "row"), P(None, "row"))
    out_specs = (P("layer", None, "row"), P("layer", None, "row"))
    return jax.shard_map(
        on_device, mesh=mesh, in_specs=in_specs, out_specs=out_specs, check_vma=False
    )
```

```python
import functools

import jax
import jax.numpy as jnp
from jax import lax
from jax.experimental import pallas as pl
from jax.experimental.pallas import tpu as pltpu
from jax.sharding import PartitionSpec as P

BLOCK = 16
GROUP = 8
LANES = 128
BLOCKS_PER_LANES = LANES // BLOCK
PACKED = LANES - BLOCK
DEGREE = 4
SMALL_GRANT = 4 * 1024 * 1024
FIELD_PARTS = GROUP // 2


def field_rows(fields, panel):
    return -(-fields // FIELD_PARTS * (panel // LANES) // BLOCK) * BLOCK


def fold_kernel(
    off_ref, width_ref, coupling_ref, field_ref, folded_ref
):
    rows, orders = coupling_ref.shape[1:]
    slot = lax.axis_index("layer") % GROUP
    fields, panel = field_ref.shape
    part = fields // FIELD_PARTS
    mine = field_ref[pl.ds(pl.multiple_of(slot // 2 * part, part), part), :]
    sent = [mine[:, u : u + LANES] for u in range(0, panel, LANES)]
    spare = field_rows(fields, panel) - part * len(sent)
    if spare:
        sent.append(jnp.zeros((spare, LANES), jnp.float32))
    sent = jnp.concatenate(sent, axis=0).astype(jnp.bfloat16)
    folded_ref[panel // LANES * PACKED :, :] = sent
    first = off_ref[0] - width_ref[0]
    last = off_ref[0] + width_ref[0]
    first_block = lax.axis_index("row") * (rows // BLOCK)
    lane = lax.broadcasted_iota(jnp.int32, (BLOCK, LANES), 1)
    sub = lax.broadcasted_iota(jnp.int32, (BLOCK, LANES), 0)
    top = orders // LANES - 1
    for local in range(rows // BLOCK):
        if local % BLOCKS_PER_LANES == 0:
            runs = []
        block = first_block + local
        start = (block + first) * BLOCK
        tile = start >> 7
        shift = start & (LANES - 1)
        here = slice(local * BLOCK, (local + 1) * BLOCK)

        def part(index):
            column = pl.multiple_of(jnp.clip(index, 0, top) * LANES, LANES)
            return coupling_ref[0, here, pl.ds(column, LANES)].astype(jnp.float32)

        near = lane >= shift
        column = jnp.where(near, lane, lane + LANES) + tile * LANES
        limit = jnp.minimum((block + last + 1) * BLOCK, orders)
        keep = (column > block * BLOCK + sub) & (column < limit)
        folded = jnp.where(keep, jnp.where(near, part(tile), part(tile + 1)), 0.0)
        is_last = block * BLOCK + sub == orders - 1
        folded = jnp.where(is_last, first.astype(jnp.float32), folded)
        runs.append(pltpu.roll(folded, (-first * BLOCK) & (LANES - 1), 1))
        if len(runs) == BLOCKS_PER_LANES:
            base = local * BLOCK // LANES * PACKED
            for b, run in enumerate(runs[:-1]):
                hole = lane // BLOCK == (b - 1) % BLOCKS_PER_LANES
                folded_ref[base + b * BLOCK : base + (b + 1) * BLOCK, :] = jnp.where(
                    hole, runs[-1], run
                ).astype(jnp.bfloat16)


def fold(coupling, band_off, band_width, field):
    rows, orders = coupling.shape[1:]
    sent = rows // LANES * PACKED + field_rows(*field.shape)
    smem = pl.BlockSpec(memory_space=pltpu.SMEM)
    vmem = pl.BlockSpec(memory_space=pltpu.VMEM)
    return pl.pallas_call(
        fold_kernel,
        out_shape=jax.ShapeDtypeStruct((sent, LANES), jnp.bfloat16),
        in_specs=[smem, smem, vmem, vmem],
        out_specs=vmem,
        compiler_params=pltpu.CompilerParams(vmem_limit_bytes=SMALL_GRANT),
        name="fold",
    )(band_off, band_width, coupling, field)


def batch_kernel(*refs):
    for index, piece in enumerate(refs[:-1]):
        refs[-1][index] = piece[...]


def batch(pieces):
    vmem = pl.BlockSpec(memory_space=pltpu.VMEM)
    return pl.pallas_call(
        batch_kernel,
        out_shape=jax.ShapeDtypeStruct((len(pieces), *pieces[0].shape), pieces[0].dtype),
        in_specs=[vmem] * len(pieces),
        out_specs=vmem,
        compiler_params=pltpu.CompilerParams(vmem_limit_bytes=SMALL_GRANT),
        name="batch",
    )(*pieces)


def place(pieces, distances, folds):
    slot = lax.axis_index("layer") % GROUP
    row = lax.axis_index("row")
    rows = folds.shape[1] // lax.axis_size("row")
    for (ref, index), (layer_mask, row_mask) in zip(pieces, distances):
        here = pl.ds(pl.multiple_of((row ^ row_mask) * rows, BLOCK), rows)
        folds[slot ^ layer_mask, here, :] = ref[index, :rows, :]


def place_field(own, pieces, distances, field):
    slot = lax.axis_index("layer") % GROUP
    row = lax.axis_index("row")
    fields, panel = own.shape
    part, tiles = fields // FIELD_PARTS, panel // LANES
    for u in range(tiles):
        field[row * tiles + u] = own[:, u * LANES : (u + 1) * LANES]
    for (ref, index), (layer_mask, row_mask) in zip(pieces, distances):
        if row_mask and not layer_mask & 1:
            here = pl.ds(pl.multiple_of((slot ^ layer_mask) // 2 * part, part), part)
            sent = ref[index, tiles * PACKED :, :].astype(jnp.float32)
            for u in range(tiles):
                field[(row ^ row_mask) * tiles + u, here, :] = sent[u * part : (u + 1) * part]


def fill_masks(masks):
    row = lax.broadcasted_iota(jnp.int32, (LANES, LANES), 0)
    lane = lax.broadcasted_iota(jnp.int32, (LANES, LANES), 1)
    masks[0] = (lane >= row // BLOCK * BLOCK).astype(jnp.float32).astype(jnp.bfloat16)
    masks[1] = (row >= lane // BLOCK * BLOCK).astype(jnp.float32).astype(jnp.bfloat16)
    masks[2] = (row < LANES - 1).astype(jnp.float32).astype(jnp.bfloat16)
    own = lane // BLOCK != (row // BLOCK + BLOCKS_PER_LANES - 1) % BLOCKS_PER_LANES
    masks[3] = own.astype(jnp.float32).astype(jnp.bfloat16)


def expand(folds, slot, masks, upper, lower):
    tiles = upper.shape[0]
    lane = lax.broadcasted_iota(jnp.int32, (1, LANES), 1)
    eighth = folds[slot, (tiles - 1) * PACKED : (tiles - 1) * PACKED + BLOCK, :]
    last_row = eighth.astype(jnp.float32)[BLOCK - 1 :, :]
    last_row = jnp.where(lane >= PACKED, last_row, -float(LANES))
    first = jnp.max(last_row).astype(jnp.int32)
    for t in range(tiles):
        packed = folds[slot, t * PACKED : (t + 1) * PACKED, :]
        own = packed * masks[3, :PACKED, :]
        rest = packed - own
        eighth = [rest[b : b + BLOCK] for b in range(0, PACKED, BLOCK)]
        while len(eighth) > 1:
            eighth = [sum(eighth[i : i + 2][1:], eighth[i]) for i in range(0, len(eighth), 2)]
        run = jnp.concatenate([own, eighth[0]], axis=0)
        if t == tiles - 1:
            run = run * masks[2]
        near = run * masks[0]
        upper[t, :, :LANES] = near
        upper[t, :, LANES:] = run - near
        turned = run.T
        near = turned * masks[1]
        lower[t, :, :LANES] = near
        lower[(t + 1) % tiles, :, LANES:] = turned - near
    return first


def banded_product(v, upper, lower, start, xs, zs):
    tiles = len(v)
    whole = start >> 3
    fine = (start & (BLOCKS_PER_LANES - 1)) * BLOCK
    lane = lax.broadcasted_iota(jnp.int32, v[0].shape, 1)
    turned = [pltpu.roll(part, (LANES - fine) & (LANES - 1), 1) for part in v]
    for u in range(tiles):
        moved = jnp.where(lane < LANES - fine, turned[u], turned[(u + 1) % tiles])
        xs[u] = moved.astype(jnp.bfloat16)
    first = [
        jnp.dot(v[t].astype(jnp.bfloat16), upper[t], preferred_element_type=jnp.float32)
        for t in range(tiles)
    ]
    sums = [first[t][:, :LANES] + first[t - 1][:, LANES:] for t in range(tiles)]
    turned = [pltpu.roll(part, fine, 1) for part in sums]
    for u in range(tiles):
        zs[u] = jnp.where(lane >= fine, turned[u], turned[u - 1])
    second = [
        jnp.dot(
            xs[(whole + u) & (tiles - 1)], lower[u], preferred_element_type=jnp.float32
        )
        for u in range(tiles)
    ]
    return [
        zs[(u - whole) & (tiles - 1)]
        - (second[u][:, :LANES] + second[(u + 1) % tiles][:, LANES:])
        for u in range(tiles)
    ]


def run_layer(x, sign, upper, lower, start, xs, zs):
    v = x
    for divisor in range(DEGREE, 0, -1):
        scale = sign * (1.0 / divisor)
        product = banded_product(v, upper, lower, start, xs, zs)
        v = [part + scale * term for part, term in zip(x, product)]
    return v


def cascade_first_kernel(distances, *refs):
    pieces = []
    for count in distances[0]:
        pieces += [(refs[0], index) for index in range(count)]
        refs = refs[1:]
    own, kept, upper, lower, starts, send, folds, masks, xs, zs = refs
    place(pieces, distances[1], folds)
    fill_masks(masks)
    place_field(own, pieces, distances[1], zs)
    x = [zs[u] for u in range(zs.shape[0])]
    forward = lax.axis_index("layer") // GROUP == 0
    sign = jnp.where(forward, -1.0, 1.0)

    def prepare(k):
        slot = jnp.where(forward, k, GROUP - 1 - k)
        start = expand(folds, slot, masks, upper.at[k], lower.at[k])
        starts[k] = start
        return start

    start = prepare(0)
    for k in range(GROUP):
        following = prepare(k + 1) if k + 1 < GROUP else None
        x = run_layer(x, sign, upper.at[k], lower.at[k], start, xs, zs)
        start = following
    finish(x, kept, send)


def cascade_next_kernel(step, groups, *refs):
    upper, lower, starts, field, kept_forward, kept_adjoint = refs[:6]
    new_forward, new_adjoint, *send, xs, zs = refs[6:]
    group = lax.axis_index("layer") // GROUP
    forward = group == step
    backward = group == groups - 1 - step
    sign = jnp.where(forward, -1.0, 1.0)
    same_order = forward == (group == 0)
    x = field[...].astype(jnp.float32)
    x = [x[:, u : u + LANES] for u in range(0, x.shape[1], LANES)]

    for k in range(GROUP):
        at = jnp.where(same_order, k, GROUP - 1 - k)
        x = run_layer(x, sign, upper.at[at], lower.at[at], starts[at], xs, zs)
    finish(x, new_forward, *send)
    mine = new_forward[0]
    new_forward[0] = jnp.where(forward, mine, kept_forward[0])
    new_adjoint[0] = jnp.where(backward, mine, kept_adjoint[0])


def finish(x, mine_ref, send=None):
    row = lax.axis_index("row")
    panel = mine_ref.shape[-1]
    if send is not None:
        for u, part in enumerate(x):
            send[:, u * LANES : (u + 1) * LANES] = part.astype(jnp.bfloat16)
    tiles = panel // LANES
    for u in range(tiles):
        mine = x[u]
        for index in range(1, len(x) // tiles):
            mine = jnp.where(row == index, x[index * tiles + u], mine)
        mine_ref[0, :, u * LANES : (u + 1) * LANES] = mine


def run_first(batches, distances, field, orders):
    count, panel = field.shape
    tiles = orders // LANES
    vmem = pl.BlockSpec(memory_space=pltpu.VMEM)
    window = jax.ShapeDtypeStruct((GROUP, tiles, LANES, 2 * LANES), jnp.bfloat16)
    return pl.pallas_call(
        functools.partial(cascade_first_kernel, distances),
        out_shape=[
            jax.ShapeDtypeStruct((1, count, panel), jnp.float32),
            window,
            window,
            jax.ShapeDtypeStruct((GROUP,), jnp.int32),
            jax.ShapeDtypeStruct((count, orders), jnp.bfloat16),
        ],
        in_specs=[vmem] * (len(batches) + 1),
        out_specs=[vmem, vmem, vmem, pl.BlockSpec(memory_space=pltpu.SMEM), vmem],
        scratch_shapes=[
            pltpu.VMEM((GROUP, tiles * PACKED, LANES), jnp.bfloat16),
            pltpu.VMEM((4, LANES, LANES), jnp.bfloat16),
            pltpu.VMEM((tiles, count, LANES), jnp.bfloat16),
            pltpu.VMEM((tiles, count, LANES), jnp.float32),
        ],
        compiler_params=pltpu.CompilerParams(vmem_limit_bytes=24 * 1024 * 1024),
        name="cascade_first",
    )(*batches, field)


def run_next(step, groups, upper, lower, starts, field, kept):
    count, orders = field.shape
    tiles = orders // LANES
    vmem = pl.BlockSpec(memory_space=pltpu.VMEM)
    out_shape = [jax.ShapeDtypeStruct(kept[0].shape, jnp.float32)] * 2
    if step < groups - 1:
        out_shape.append(jax.ShapeDtypeStruct(field.shape, jnp.bfloat16))
    return pl.pallas_call(
        functools.partial(cascade_next_kernel, step, groups),
        out_shape=out_shape,
        in_specs=[vmem, vmem, pl.BlockSpec(memory_space=pltpu.SMEM), vmem, vmem, vmem],
        out_specs=[vmem] * len(out_shape),
        scratch_shapes=[
            pltpu.VMEM((tiles, count, LANES), jnp.bfloat16),
            pltpu.VMEM((tiles, count, LANES), jnp.float32),
        ],
        compiler_params=pltpu.CompilerParams(vmem_limit_bytes=24 * 1024 * 1024),
        name=f"cascade_{step}",
    )(upper, lower, starts, field, *kept)


def gather_batches(own, across, rows):
    bits = [(0, 1 << b) for b in range(rows.bit_length() - 1)]
    bits += [(1 << b, 0) for b in range(1, GROUP.bit_length() - 1)]
    count = len(bits)

    def members(subset):
        return [b for b in range(count) if subset >> b & 1]

    def distance(subset):
        return tuple(sum(bits[b][axis] for b in members(subset)) for axis in (0, 1))

    pieces = {0: own}
    batches, counts, distances = [], [], []
    for number in range(1, count + 1):
        part = [m for m in range(1 << count) if m.bit_count() == number]
        for subset in part:
            which = members(subset)
            link = next((b for b in which if (b + 1) % count in which), which[0])
            pieces[subset] = across(pieces[subset ^ 1 << link], *distance(1 << link))
        part = [0] + part if number == 1 else part
        mine = batch([pieces[subset] for subset in part])
        batches += [mine, across(mine, 1, 0)]
        counts += [len(part), len(part)]
        distances += [distance(subset) for subset in part]
        distances += [(a ^ 1, b) for a, b in distances[-len(part) :]]
    return batches, (tuple(counts), tuple(distances))


def on_device(coupling, band_off, band_width, incident, cotangent):
    panel, orders = coupling.shape[1:]
    layers = lax.axis_size("layer")
    rows = lax.axis_size("row")
    groups = layers // GROUP

    def across(array, layer_mask, row_mask):
        pairs = [
            (l * rows + r, (l ^ layer_mask) * rows + (r ^ row_mask))
            for l in range(layers)
            for r in range(rows)
        ]
        return lax.ppermute(array, ("layer", "row"), pairs)

    field = jnp.where(lax.axis_index("layer") // GROUP == 0, incident, cotangent)
    folded = fold(coupling, band_off, band_width, field)
    batches, distances = gather_batches(folded, across, rows)

    mine, upper, lower, starts, send = run_first(batches, distances, field, orders)
    kept = [mine, mine]
    for step in range(1, groups):
        pairs = []
        for index in range(GROUP * rows):
            forward_from = (step - 1) * GROUP * rows + index
            adjoint_from = (groups - step) * GROUP * rows + index
            pairs.append((forward_from, forward_from + GROUP * rows))
            pairs.append((adjoint_from, adjoint_from - GROUP * rows))
        field = lax.ppermute(send, ("layer", "row"), pairs)
        *kept, send = [*run_next(step, groups, upper, lower, starts, field, kept), None][:3]
    return tuple(kept)


def solution(mesh):
    in_specs = (P("layer", "row", None), P("layer"), P("layer"), P(None, "row"), P(None, "row"))
    out_specs = (P("layer", None, "row"), P("layer", None, "row"))
    return jax.shard_map(
        on_device, mesh=mesh, in_specs=in_specs, out_specs=out_specs, check_vma=False
    )
```

```python
import functools

import jax
import jax.numpy as jnp
from jax import lax
from jax.experimental import pallas as pl
from jax.experimental.pallas import tpu as pltpu
from jax.sharding import PartitionSpec as P

BLOCK = 16
GROUP = 8
LANES = 128
BLOCKS_PER_LANES = LANES // BLOCK
PACKED = LANES - BLOCK
DEGREE = 4
GROUP_ROWS = 32
SMALL_GRANT = 4 * 1024 * 1024
FIELD_PARTS = GROUP // 2


def field_rows(fields, panel):
    return -(-fields // FIELD_PARTS * (panel // LANES) // BLOCK) * BLOCK


def fold_kernel(
    off_ref, width_ref, coupling_ref, field_ref, folded_ref
):
    rows, orders = coupling_ref.shape[1:]
    slot = lax.axis_index("layer") % GROUP
    fields, panel = field_ref.shape
    part = fields // FIELD_PARTS
    mine = field_ref[pl.ds(pl.multiple_of(slot // 2 * part, part), part), :]
    sent = [mine[:, u : u + LANES] for u in range(0, panel, LANES)]
    spare = field_rows(fields, panel) - part * len(sent)
    if spare:
        sent.append(jnp.zeros((spare, LANES), jnp.float32))
    sent = jnp.concatenate(sent, axis=0).astype(jnp.bfloat16)
    folded_ref[panel // LANES * PACKED :, :] = sent
    first = off_ref[0] - width_ref[0]
    last = off_ref[0] + width_ref[0]
    first_block = lax.axis_index("row") * (rows // BLOCK)
    lane = lax.broadcasted_iota(jnp.int32, (BLOCK, LANES), 1)
    sub = lax.broadcasted_iota(jnp.int32, (BLOCK, LANES), 0)
    top = orders // LANES - 1
    for local in range(rows // BLOCK):
        if local % BLOCKS_PER_LANES == 0:
            runs = []
        block = first_block + local
        start = (block + first) * BLOCK
        tile = start >> 7
        shift = start & (LANES - 1)
        here = slice(local * BLOCK, (local + 1) * BLOCK)

        def part(index):
            column = pl.multiple_of(jnp.clip(index, 0, top) * LANES, LANES)
            return coupling_ref[0, here, pl.ds(column, LANES)].astype(jnp.float32)

        near = lane >= shift
        column = jnp.where(near, lane, lane + LANES) + tile * LANES
        limit = jnp.minimum((block + last + 1) * BLOCK, orders)
        keep = (column > block * BLOCK + sub) & (column < limit)
        folded = jnp.where(keep, jnp.where(near, part(tile), part(tile + 1)), 0.0)
        is_last = block * BLOCK + sub == orders - 1
        folded = jnp.where(is_last, first.astype(jnp.float32), folded)
        runs.append(pltpu.roll(folded, (-first * BLOCK) & (LANES - 1), 1))
        if len(runs) == BLOCKS_PER_LANES:
            base = local * BLOCK // LANES * PACKED
            for b, run in enumerate(runs[:-1]):
                hole = lane // BLOCK == (b - 1) % BLOCKS_PER_LANES
                folded_ref[base + b * BLOCK : base + (b + 1) * BLOCK, :] = jnp.where(
                    hole, runs[-1], run
                ).astype(jnp.bfloat16)


def fold(coupling, band_off, band_width, field):
    rows, orders = coupling.shape[1:]
    sent = rows // LANES * PACKED + field_rows(*field.shape)
    smem = pl.BlockSpec(memory_space=pltpu.SMEM)
    vmem = pl.BlockSpec(memory_space=pltpu.VMEM)
    return pl.pallas_call(
        fold_kernel,
        out_shape=jax.ShapeDtypeStruct((sent, LANES), jnp.bfloat16),
        in_specs=[smem, smem, vmem, vmem],
        out_specs=vmem,
        compiler_params=pltpu.CompilerParams(vmem_limit_bytes=SMALL_GRANT),
        name="fold",
    )(band_off, band_width, coupling, field)


def batch_kernel(*refs):
    for index, piece in enumerate(refs[:-1]):
        refs[-1][index] = piece[...]


def batch(pieces):
    vmem = pl.BlockSpec(memory_space=pltpu.VMEM)
    return pl.pallas_call(
        batch_kernel,
        out_shape=jax.ShapeDtypeStruct((len(pieces), *pieces[0].shape), pieces[0].dtype),
        in_specs=[vmem] * len(pieces),
        out_specs=vmem,
        compiler_params=pltpu.CompilerParams(vmem_limit_bytes=SMALL_GRANT),
        name="batch",
    )(*pieces)


def place(pieces, distances, folds):
    slot = lax.axis_index("layer") % GROUP
    row = lax.axis_index("row")
    rows = folds.shape[1] // lax.axis_size("row")
    for (ref, index), (layer_mask, row_mask) in zip(pieces, distances):
        here = pl.ds(pl.multiple_of((row ^ row_mask) * rows, BLOCK), rows)
        folds[slot ^ layer_mask, here, :] = ref[index, :rows, :]


def place_field(own, pieces, distances, field):
    slot = lax.axis_index("layer") % GROUP
    row = lax.axis_index("row")
    fields, panel = own.shape
    part, tiles = fields // FIELD_PARTS, panel // LANES
    for u in range(tiles):
        field[row * tiles + u] = own[:, u * LANES : (u + 1) * LANES]
    for (ref, index), (layer_mask, row_mask) in zip(pieces, distances):
        if row_mask and not layer_mask & 1:
            here = pl.ds(pl.multiple_of((slot ^ layer_mask) // 2 * part, part), part)
            sent = ref[index, tiles * PACKED :, :].astype(jnp.float32)
            for u in range(tiles):
                field[(row ^ row_mask) * tiles + u, here, :] = sent[u * part : (u + 1) * part]


def fill_masks(masks):
    row = lax.broadcasted_iota(jnp.int32, (LANES, LANES), 0)
    lane = lax.broadcasted_iota(jnp.int32, (LANES, LANES), 1)
    masks[0] = (row < LANES - 1).astype(jnp.float32).astype(jnp.bfloat16)
    own = lane // BLOCK != (row // BLOCK + BLOCKS_PER_LANES - 1) % BLOCKS_PER_LANES
    masks[1] = own.astype(jnp.float32).astype(jnp.bfloat16)
    masks[2] = (row >= lane // BLOCK * BLOCK).astype(jnp.float32).astype(jnp.bfloat16)


def expand(folds, slot, masks, both):
    tiles = both.shape[0] // LANES
    lane = lax.broadcasted_iota(jnp.int32, (1, LANES), 1)
    eighth = folds[slot, (tiles - 1) * PACKED : (tiles - 1) * PACKED + BLOCK, :]
    last_row = eighth.astype(jnp.float32)[BLOCK - 1 :, :]
    last_row = jnp.where(lane >= PACKED, last_row, -float(LANES))
    first = jnp.max(last_row).astype(jnp.int32)
    near, far = [], []
    for t in range(tiles):
        packed = folds[slot, t * PACKED : (t + 1) * PACKED, :]
        own = packed * masks[1, :PACKED, :]
        rest = packed - own
        eighth = [rest[b : b + BLOCK] for b in range(0, PACKED, BLOCK)]
        while len(eighth) > 1:
            eighth = [sum(eighth[i : i + 2][1:], eighth[i]) for i in range(0, len(eighth), 2)]
        run = jnp.concatenate([own, eighth[0]], axis=0)
        if t == tiles - 1:
            run = run * masks[0]
        both[t * LANES : (t + 1) * LANES, :LANES] = run
        turned = run.T
        near.append(turned * masks[2])
        far.append(turned - near[-1])
    for t in range(tiles):
        turned = (near[t] + far[t - 1]).astype(jnp.float32)
        turned = pltpu.roll(turned, first * BLOCK & (LANES - 1), 1).astype(jnp.bfloat16)
        for b in range(BLOCKS_PER_LANES):
            at = (t * BLOCKS_PER_LANES + b + first) & (tiles * BLOCKS_PER_LANES - 1)
            here = pl.ds(pl.multiple_of(at * BLOCK, BLOCK), BLOCK)
            both[here, LANES:] = turned[b * BLOCK : (b + 1) * BLOCK]
    return first


def banded_product(v, both, start, zs):
    tiles, fields = len(v), v[0].shape[0]
    whole = start >> 3
    fine = (start & (BLOCKS_PER_LANES - 1)) * BLOCK
    lane = lax.broadcasted_iota(jnp.int32, v[0].shape, 1)
    groups = LANES // GROUP_ROWS
    keeps = [
        (lane >= c * GROUP_ROWS).astype(jnp.float32).astype(jnp.bfloat16)
        for c in range(1, groups)
    ]
    upper, lower = [[None] * tiles for _ in range(2)], [[None] * tiles for _ in range(2)]
    for t in range(tiles):
        part = v[t].astype(jnp.bfloat16)
        spread = jnp.concatenate([part] + [part * keep for keep in keeps], axis=0)
        product = jnp.dot(
            spread,
            both[t * LANES : (t + 1) * LANES, :],
            preferred_element_type=jnp.float32,
        )
        sums = [product[c * fields : (c + 1) * fields] for c in range(groups)]
        following = jnp.zeros_like(v[t])
        same = sums[-1][:, LANES:]
        for c in range(groups - 2, -1, -1):
            here = lane < (c + 1) * GROUP_ROWS
            following = jnp.where(here, sums[c + 1][:, :LANES], following)
            same = jnp.where(here, sums[c][:, LANES:], same)
        upper[0][t], upper[1][t] = sums[0][:, :LANES] - following, following
        lower[0][t], lower[1][t] = same, sums[0][:, LANES:] - same
    turned = [pltpu.roll(upper[0][t] + upper[1][t - 1], fine, 1) for t in range(tiles)]
    for t in range(tiles):
        zs[0, t] = jnp.where(lane >= fine, turned[t], turned[t - 1])
    back = (LANES - fine) & (LANES - 1)
    turned = [
        pltpu.roll(lower[0][t] + lower[1][(t + 1) % tiles], back, 1) for t in range(tiles)
    ]
    for t in range(tiles):
        zs[1, t] = jnp.where(lane < LANES - fine, turned[t], turned[(t + 1) % tiles])
    return [
        zs[0, (u - whole) & (tiles - 1)] - zs[1, (u + whole) & (tiles - 1)]
        for u in range(tiles)
    ]


def run_layer(x, sign, both, start, zs):
    v = x
    for divisor in range(DEGREE, 0, -1):
        scale = sign * (1.0 / divisor)
        product = banded_product(v, both, start, zs)
        v = [part + scale * term for part, term in zip(x, product)]
    return v


def cascade_first_kernel(distances, *refs):
    pieces = []
    for count in distances[0]:
        pieces += [(refs[0], index) for index in range(count)]
        refs = refs[1:]
    own, kept, both, starts, send, folds, masks, zs = refs
    place(pieces, distances[1], folds)
    fill_masks(masks)
    place_field(own, pieces, distances[1], zs.at[0])
    x = [zs[0, u] for u in range(zs.shape[1])]
    forward = lax.axis_index("layer") // GROUP == 0
    sign = jnp.where(forward, -1.0, 1.0)

    def prepare(k):
        slot = jnp.where(forward, k, GROUP - 1 - k)
        start = expand(folds, slot, masks, both.at[k])
        starts[k] = start
        return start

    start = prepare(0)
    for k in range(GROUP):
        following = prepare(k + 1) if k + 1 < GROUP else None
        x = run_layer(x, sign, both.at[k], start, zs)
        start = following
    finish(x, kept, send)


def cascade_next_kernel(step, groups, *refs):
    both, starts, field, kept_forward, kept_adjoint = refs[:5]
    new_forward, new_adjoint, *send, zs = refs[5:]
    group = lax.axis_index("layer") // GROUP
    forward = group == step
    backward = group == groups - 1 - step
    sign = jnp.where(forward, -1.0, 1.0)
    same_order = forward == (group == 0)
    x = field[...].astype(jnp.float32)
    x = [x[:, u : u + LANES] for u in range(0, x.shape[1], LANES)]

    for k in range(GROUP):
        at = jnp.where(same_order, k, GROUP - 1 - k)
        x = run_layer(x, sign, both.at[at], starts[at], zs)
    finish(x, new_forward, *send)
    mine = new_forward[0]
    new_forward[0] = jnp.where(forward, mine, kept_forward[0])
    new_adjoint[0] = jnp.where(backward, mine, kept_adjoint[0])


def finish(x, mine_ref, send=None):
    row = lax.axis_index("row")
    panel = mine_ref.shape[-1]
    if send is not None:
        for u, part in enumerate(x):
            send[:, u * LANES : (u + 1) * LANES] = part.astype(jnp.bfloat16)
    tiles = panel // LANES
    for u in range(tiles):
        mine = x[u]
        for index in range(1, len(x) // tiles):
            mine = jnp.where(row == index, x[index * tiles + u], mine)
        mine_ref[0, :, u * LANES : (u + 1) * LANES] = mine


def run_first(batches, distances, field, orders):
    count, panel = field.shape
    tiles = orders // LANES
    vmem = pl.BlockSpec(memory_space=pltpu.VMEM)
    return pl.pallas_call(
        functools.partial(cascade_first_kernel, distances),
        out_shape=[
            jax.ShapeDtypeStruct((1, count, panel), jnp.float32),
            jax.ShapeDtypeStruct((GROUP, orders, 2 * LANES), jnp.bfloat16),
            jax.ShapeDtypeStruct((GROUP,), jnp.int32),
            jax.ShapeDtypeStruct((count, orders), jnp.bfloat16),
        ],
        in_specs=[vmem] * (len(batches) + 1),
        out_specs=[vmem, vmem, pl.BlockSpec(memory_space=pltpu.SMEM), vmem],
        scratch_shapes=[
            pltpu.VMEM((GROUP, tiles * PACKED, LANES), jnp.bfloat16),
            pltpu.VMEM((3, LANES, LANES), jnp.bfloat16),
            pltpu.VMEM((2, tiles, count, LANES), jnp.float32),
        ],
        compiler_params=pltpu.CompilerParams(vmem_limit_bytes=24 * 1024 * 1024),
        name="cascade_first",
    )(*batches, field)


def run_next(step, groups, both, starts, field, kept):
    count, orders = field.shape
    tiles = orders // LANES
    vmem = pl.BlockSpec(memory_space=pltpu.VMEM)
    out_shape = [jax.ShapeDtypeStruct(kept[0].shape, jnp.float32)] * 2
    if step < groups - 1:
        out_shape.append(jax.ShapeDtypeStruct(field.shape, jnp.bfloat16))
    return pl.pallas_call(
        functools.partial(cascade_next_kernel, step, groups),
        out_shape=out_shape,
        in_specs=[vmem, pl.BlockSpec(memory_space=pltpu.SMEM), vmem, vmem, vmem],
        out_specs=[vmem] * len(out_shape),
        scratch_shapes=[pltpu.VMEM((2, tiles, count, LANES), jnp.float32)],
        compiler_params=pltpu.CompilerParams(vmem_limit_bytes=24 * 1024 * 1024),
        name=f"cascade_{step}",
    )(both, starts, field, *kept)


def gather_batches(own, across, rows):
    bits = [(0, 1 << b) for b in range(rows.bit_length() - 1)]
    bits += [(1 << b, 0) for b in range(1, GROUP.bit_length() - 1)]
    count = len(bits)

    def members(subset):
        return [b for b in range(count) if subset >> b & 1]

    def distance(subset):
        return tuple(sum(bits[b][axis] for b in members(subset)) for axis in (0, 1))

    subsets = sorted(range(1 << count), key=lambda m: (m.bit_count(), m))
    pieces = {0: own}
    for subset in subsets[1 : count + 1] + subsets[-1:]:
        pieces[subset] = across(own, *distance(subset))
    for subset in subsets[count + 1 : -1]:
        which = members(subset)
        link = next((b for b in which if (b + 1) % count in which), which[0])
        pieces[subset] = across(pieces[subset ^ 1 << link], *distance(1 << link))
    batches, counts, distances = [], [], []
    for part in (subsets[: count + 1], subsets[count + 1 :]):
        mine = batch([pieces[subset] for subset in part])
        batches += [mine, across(mine, 1, 0)]
        counts += [len(part), len(part)]
        distances += [distance(subset) for subset in part]
        distances += [(a ^ 1, b) for a, b in distances[-len(part) :]]
    return batches, (tuple(counts), tuple(distances))


def on_device(coupling, band_off, band_width, incident, cotangent):
    panel, orders = coupling.shape[1:]
    layers = lax.axis_size("layer")
    rows = lax.axis_size("row")
    groups = layers // GROUP

    def across(array, layer_mask, row_mask):
        pairs = [
            (l * rows + r, (l ^ layer_mask) * rows + (r ^ row_mask))
            for l in range(layers)
            for r in range(rows)
        ]
        return lax.ppermute(array, ("layer", "row"), pairs)

    field = jnp.where(lax.axis_index("layer") // GROUP == 0, incident, cotangent)
    folded = fold(coupling, band_off, band_width, field)
    batches, distances = gather_batches(folded, across, rows)

    mine, both, starts, send = run_first(batches, distances, field, orders)
    kept = [mine, mine]
    for step in range(1, groups):
        pairs = []
        for index in range(GROUP * rows):
            forward_from = (step - 1) * GROUP * rows + index
            adjoint_from = (groups - step) * GROUP * rows + index
            pairs.append((forward_from, forward_from + GROUP * rows))
            pairs.append((adjoint_from, adjoint_from - GROUP * rows))
        field = lax.ppermute(send, ("layer", "row"), pairs)
        *kept, send = [*run_next(step, groups, both, starts, field, kept), None][:3]
    return tuple(kept)


def solution(mesh):
    in_specs = (P("layer", "row", None), P("layer"), P("layer"), P(None, "row"), P(None, "row"))
    out_specs = (P("layer", None, "row"), P("layer", None, "row"))
    return jax.shard_map(
        on_device, mesh=mesh, in_specs=in_specs, out_specs=out_specs, check_vma=False
    )
```

```python
import functools

import jax
import jax.numpy as jnp
from jax import lax
from jax.experimental import pallas as pl
from jax.experimental.pallas import tpu as pltpu
from jax.sharding import PartitionSpec as P

BLOCK = 16
GROUP = 8
LANES = 128
BLOCKS_PER_LANES = LANES // BLOCK
PACKED = LANES - BLOCK
DEGREE = 4
SMALL_GRANT = 4 * 1024 * 1024
CORES = 2
FIELD_PARTS = 2


def field_rows(fields, panel):
    return -(-fields // FIELD_PARTS * (panel // LANES) // BLOCK) * BLOCK


def fold_kernel(
    off_ref, width_ref, coupling_ref, field_ref, folded_ref
):
    rows, orders = coupling_ref.shape[1:]
    slot = lax.axis_index("layer") % GROUP
    fields, panel = field_ref.shape
    part = fields // FIELD_PARTS
    mine = field_ref[pl.ds(pl.multiple_of((slot >> 1) % FIELD_PARTS * part, part), part), :]
    sent = [mine[:, u : u + LANES] for u in range(0, panel, LANES)]
    spare = field_rows(fields, panel) - part * len(sent)
    if spare:
        sent.append(jnp.zeros((spare, LANES), jnp.float32))
    sent = jnp.concatenate(sent, axis=0).astype(jnp.bfloat16)
    folded_ref[panel // LANES * PACKED :, :] = sent
    first = off_ref[0] - width_ref[0]
    last = off_ref[0] + width_ref[0]
    first_block = lax.axis_index("row") * (rows // BLOCK)
    lane = lax.broadcasted_iota(jnp.int32, (BLOCK, LANES), 1)
    sub = lax.broadcasted_iota(jnp.int32, (BLOCK, LANES), 0)
    top = orders // LANES - 1
    for local in range(rows // BLOCK):
        if local % BLOCKS_PER_LANES == 0:
            runs = []
        block = first_block + local
        start = (block + first) * BLOCK
        tile = start >> 7
        shift = start & (LANES - 1)
        here = slice(local * BLOCK, (local + 1) * BLOCK)

        def part(index):
            column = pl.multiple_of(jnp.clip(index, 0, top) * LANES, LANES)
            return coupling_ref[0, here, pl.ds(column, LANES)].astype(jnp.float32)

        near = lane >= shift
        column = jnp.where(near, lane, lane + LANES) + tile * LANES
        limit = jnp.minimum((block + last + 1) * BLOCK, orders)
        keep = (column > block * BLOCK + sub) & (column < limit)
        folded = jnp.where(keep, jnp.where(near, part(tile), part(tile + 1)), 0.0)
        is_last = block * BLOCK + sub == orders - 1
        folded = jnp.where(is_last, first.astype(jnp.float32), folded)
        runs.append(pltpu.roll(folded, (-first * BLOCK) & (LANES - 1), 1))
        if len(runs) == BLOCKS_PER_LANES:
            base = local * BLOCK // LANES * PACKED
            for b, run in enumerate(runs[:-1]):
                hole = lane // BLOCK == (b - 1) % BLOCKS_PER_LANES
                folded_ref[base + b * BLOCK : base + (b + 1) * BLOCK, :] = jnp.where(
                    hole, runs[-1], run
                ).astype(jnp.bfloat16)


def fold(coupling, band_off, band_width, field):
    rows, orders = coupling.shape[1:]
    sent = rows // LANES * PACKED + field_rows(*field.shape)
    smem = pl.BlockSpec(memory_space=pltpu.SMEM)
    vmem = pl.BlockSpec(memory_space=pltpu.VMEM)
    return pl.pallas_call(
        fold_kernel,
        out_shape=jax.ShapeDtypeStruct((sent, LANES), jnp.bfloat16),
        in_specs=[smem, smem, vmem, vmem],
        out_specs=vmem,
        compiler_params=pltpu.CompilerParams(vmem_limit_bytes=SMALL_GRANT),
        name="fold",
    )(band_off, band_width, coupling, field)


def batch_kernel(*refs):
    for index, piece in enumerate(refs[:-1]):
        refs[-1][index] = piece[...]


def batch(pieces):
    vmem = pl.BlockSpec(memory_space=pltpu.VMEM)
    return pl.pallas_call(
        batch_kernel,
        out_shape=jax.ShapeDtypeStruct((len(pieces), *pieces[0].shape), pieces[0].dtype),
        in_specs=[vmem] * len(pieces),
        out_specs=vmem,
        compiler_params=pltpu.CompilerParams(vmem_limit_bytes=SMALL_GRANT),
        name="batch",
    )(*pieces)


def place(pieces, distances, folds):
    slot = lax.axis_index("layer") % GROUP
    row = lax.axis_index("row")
    rows = folds.shape[1] // lax.axis_size("row")
    for (ref, index), (layer_mask, row_mask) in zip(pieces, distances):
        here = pl.ds(pl.multiple_of((row ^ row_mask) * rows, BLOCK), rows)
        folds[slot ^ layer_mask, here, :] = ref[index, :rows, :]


def place_field(own, pieces, distances, field):
    slot = lax.axis_index("layer") % GROUP
    row = lax.axis_index("row")
    fields, panel = own.shape
    part, tiles = fields // FIELD_PARTS, panel // LANES
    for u in range(tiles):
        field[row * tiles + u] = own[:, u * LANES : (u + 1) * LANES]
    for (ref, index), (layer_mask, row_mask) in zip(pieces, distances):
        if row_mask and not layer_mask & 1:
            sender = (slot ^ layer_mask) >> 1
            here = pl.ds(pl.multiple_of(sender % FIELD_PARTS * part, part), part)
            sent = ref[index, tiles * PACKED :, :].astype(jnp.float32)
            for u in range(tiles):
                field[(row ^ row_mask) * tiles + u, here, :] = sent[u * part : (u + 1) * part]


def fill_masks(masks):
    row = lax.broadcasted_iota(jnp.int32, (LANES, LANES), 0)
    lane = lax.broadcasted_iota(jnp.int32, (LANES, LANES), 1)
    masks[0] = (lane >= row // BLOCK * BLOCK).astype(jnp.float32).astype(jnp.bfloat16)
    masks[1] = (row >= lane // BLOCK * BLOCK).astype(jnp.float32).astype(jnp.bfloat16)
    masks[2] = (row < LANES - 1).astype(jnp.float32).astype(jnp.bfloat16)
    own = lane // BLOCK != (row // BLOCK + BLOCKS_PER_LANES - 1) % BLOCKS_PER_LANES
    masks[3] = own.astype(jnp.float32).astype(jnp.bfloat16)


def expand(folds, slot, masks, upper, lower):
    tiles = upper.shape[0]
    lane = lax.broadcasted_iota(jnp.int32, (1, LANES), 1)
    eighth = folds[slot, (tiles - 1) * PACKED : (tiles - 1) * PACKED + BLOCK, :]
    last_row = eighth.astype(jnp.float32)[BLOCK - 1 :, :]
    last_row = jnp.where(lane >= PACKED, last_row, -float(LANES))
    first = jnp.max(last_row).astype(jnp.int32)
    for t in range(tiles):
        packed = folds[slot, t * PACKED : (t + 1) * PACKED, :]
        own = packed * masks[3, :PACKED, :]
        rest = packed - own
        eighth = [rest[b : b + BLOCK] for b in range(0, PACKED, BLOCK)]
        while len(eighth) > 1:
            eighth = [sum(eighth[i : i + 2][1:], eighth[i]) for i in range(0, len(eighth), 2)]
        run = jnp.concatenate([own, eighth[0]], axis=0)
        if t == tiles - 1:
            run = run * masks[2]
        near = run * masks[0]
        upper[t, :, :LANES] = near
        upper[t, :, LANES:] = run - near
        turned = run.T
        near = turned * masks[1]
        lower[t, :, :LANES] = near
        lower[(t + 1) % tiles, :, LANES:] = turned - near
    return first


def banded_product(v, upper, lower, start, xs, zs):
    tiles = len(v)
    whole = start >> 3
    fine = (start & (BLOCKS_PER_LANES - 1)) * BLOCK
    lane = lax.broadcasted_iota(jnp.int32, v[0].shape, 1)
    turned = [pltpu.roll(part, (LANES - fine) & (LANES - 1), 1) for part in v]
    for u in range(tiles):
        moved = jnp.where(lane < LANES - fine, turned[u], turned[(u + 1) % tiles])
        xs[u] = moved.astype(jnp.bfloat16)
    first = [
        jnp.dot(v[t].astype(jnp.bfloat16), upper[t], preferred_element_type=jnp.float32)
        for t in range(tiles)
    ]
    sums = [first[t][:, :LANES] + first[t - 1][:, LANES:] for t in range(tiles)]
    turned = [pltpu.roll(part, fine, 1) for part in sums]
    for u in range(tiles):
        zs[u] = jnp.where(lane >= fine, turned[u], turned[u - 1])
    second = [
        jnp.dot(
            xs[(whole + u) & (tiles - 1)], lower[u], preferred_element_type=jnp.float32
        )
        for u in range(tiles)
    ]
    return [
        zs[(u - whole) & (tiles - 1)]
        - (second[u][:, :LANES] + second[(u + 1) % tiles][:, LANES:])
        for u in range(tiles)
    ]


def run_layer(x, sign, upper, lower, start, xs, zs):
    v = x
    for divisor in range(DEGREE, 0, -1):
        scale = sign * (1.0 / divisor)
        product = banded_product(v, upper, lower, start, xs, zs)
        v = [part + scale * term for part, term in zip(x, product)]
    return v


def cascade_first_kernel(distances, *refs):
    pieces = []
    for count in distances[0]:
        pieces += [(refs[0], index) for index in range(count)]
        refs = refs[1:]
    own, kept, upper, lower, starts, send, folds, masks, xs, zs = refs
    place(pieces, distances[1], folds)
    fill_masks(masks)
    place_field(own, pieces, distances[1], zs)
    x = [zs[u] for u in range(zs.shape[0])]
    forward = lax.axis_index("layer") // GROUP == 0
    sign = jnp.where(forward, -1.0, 1.0)

    def prepare(k):
        slot = jnp.where(forward, k, GROUP - 1 - k)
        start = expand(folds, slot, masks, upper.at[k], lower.at[k])
        starts[k : k + 1, :] = jnp.full((1, LANES), start, jnp.int32)
        return start

    start = prepare(0)
    for k in range(GROUP):
        following = prepare(k + 1) if k + 1 < GROUP else None
        x = run_layer(x, sign, upper.at[k], lower.at[k], start, xs, zs)
        start = following
    mine = own_panel(x, kept.shape[-1])
    kept[0] = mine
    kept[1] = mine
    write_whole(x, send)


def cascade_next_kernel(step, groups, *refs):
    upper, lower, starts, field, before, kept, *send, xs, zs = refs
    panel = kept.shape[-1]
    group = lax.axis_index("layer") // GROUP
    forward = group == step
    backward = group == groups - 1 - step
    sign = jnp.where(forward, -1.0, 1.0)
    same_order = forward == (group == 0)
    x = field[...].astype(jnp.float32)
    x = [x[:, u : u + LANES] for u in range(0, x.shape[1], LANES)]

    order = [jnp.where(same_order, k, GROUP - 1 - k) for k in range(GROUP)]
    begin = [jnp.max(starts[pl.ds(at, 1), :]) for at in order]
    for at, start in zip(order, begin):
        x = run_layer(x, sign, upper.at[at], lower.at[at], start, xs, zs)
    mine = own_panel(x, panel)
    kept[0] = jnp.where(forward, mine, before[0])
    kept[1] = jnp.where(backward, mine, before[1])
    if send:
        write_whole(x, *send)


def write_whole(x, send):
    for u, part in enumerate(x):
        send[:, u * LANES : (u + 1) * LANES] = part.astype(jnp.bfloat16)


def own_panel(x, panel):
    row = lax.axis_index("row")
    tiles = panel // LANES
    mine = x[:tiles]
    for index in range(1, len(x) // tiles):
        there = x[index * tiles : (index + 1) * tiles]
        mine = [jnp.where(row == index, new, old) for new, old in zip(there, mine)]
    return jnp.concatenate(mine, axis=1)


def join_kernel(mine, theirs, *outs):
    core = lax.axis_index("layer") % CORES
    count = mine.shape[1]
    for kind, out in enumerate(outs):
        for part, at in ((mine, core), (theirs, 1 - core)):
            out[0, pl.ds(pl.multiple_of(at * count, count), count), :] = part[kind]


def join(mine, theirs):
    kinds, count, panel = mine.shape
    vmem = pl.BlockSpec(memory_space=pltpu.VMEM)
    return pl.pallas_call(
        join_kernel,
        out_shape=[jax.ShapeDtypeStruct((1, CORES * count, panel), mine.dtype)] * kinds,
        in_specs=[vmem] * 2,
        out_specs=[vmem] * kinds,
        compiler_params=pltpu.CompilerParams(vmem_limit_bytes=SMALL_GRANT),
        name="join",
    )(mine, theirs)


def run_first(batches, distances, field, orders):
    count, panel = field.shape
    tiles = orders // LANES
    vmem = pl.BlockSpec(memory_space=pltpu.VMEM)
    window = jax.ShapeDtypeStruct((GROUP, tiles, LANES, 2 * LANES), jnp.bfloat16)
    return pl.pallas_call(
        functools.partial(cascade_first_kernel, distances),
        out_shape=[
            jax.ShapeDtypeStruct((2, count, panel), jnp.float32),
            window,
            window,
            jax.ShapeDtypeStruct((GROUP, LANES), jnp.int32),
            jax.ShapeDtypeStruct((count, orders), jnp.bfloat16),
        ],
        in_specs=[vmem] * (len(batches) + 1),
        out_specs=[vmem] * 5,
        scratch_shapes=[
            pltpu.VMEM((GROUP, tiles * PACKED, LANES), jnp.bfloat16),
            pltpu.VMEM((4, LANES, LANES), jnp.bfloat16),
            pltpu.VMEM((tiles, count, LANES), jnp.bfloat16),
            pltpu.VMEM((tiles, count, LANES), jnp.float32),
        ],
        compiler_params=pltpu.CompilerParams(vmem_limit_bytes=24 * 1024 * 1024),
        name="cascade_first",
    )(*batches, field)


def run_next(step, groups, upper, lower, starts, field, kept):
    count, orders = field.shape
    tiles = orders // LANES
    vmem = pl.BlockSpec(memory_space=pltpu.VMEM)
    out_shape = [jax.ShapeDtypeStruct(kept.shape, jnp.float32)]
    if step < groups - 1:
        out_shape.append(jax.ShapeDtypeStruct(field.shape, jnp.bfloat16))
    return pl.pallas_call(
        functools.partial(cascade_next_kernel, step, groups),
        out_shape=out_shape,
        in_specs=[vmem] * 5,
        out_specs=[vmem] * len(out_shape),
        scratch_shapes=[
            pltpu.VMEM((tiles, count, LANES), jnp.bfloat16),
            pltpu.VMEM((tiles, count, LANES), jnp.float32),
        ],
        compiler_params=pltpu.CompilerParams(vmem_limit_bytes=24 * 1024 * 1024),
        name=f"cascade_{step}",
    )(upper, lower, starts, field, kept)


def gather_batches(own, across, rows):
    bits = [(0, 1 << b) for b in range(rows.bit_length() - 1)]
    bits += [(1 << b, 0) for b in range(1, GROUP.bit_length() - 1)]
    count = len(bits)

    def members(subset):
        return [b for b in range(count) if subset >> b & 1]

    def distance(subset):
        return tuple(sum(bits[b][axis] for b in members(subset)) for axis in (0, 1))

    subsets = sorted(range(1 << count), key=lambda m: (m.bit_count(), m))
    pieces = {0: own}
    for subset in subsets[1 : count + 1] + subsets[-1:]:
        pieces[subset] = across(own, *distance(subset))
    for subset in subsets[count + 1 : -1]:
        which = members(subset)
        link = next((b for b in which if (b + 1) % count in which), which[0])
        pieces[subset] = across(pieces[subset ^ 1 << link], *distance(1 << link))
    batches, counts, distances = [], [], []
    for part in (subsets[: count + 1], subsets[count + 1 :]):
        mine = batch([pieces[subset] for subset in part])
        batches += [mine, across(mine, 1, 0)]
        counts += [len(part), len(part)]
        distances += [distance(subset) for subset in part]
        distances += [(a ^ 1, b) for a, b in distances[-len(part) :]]
    return batches, (tuple(counts), tuple(distances))


def on_device(coupling, band_off, band_width, incident, cotangent):
    panel, orders = coupling.shape[1:]
    layers = lax.axis_size("layer")
    rows = lax.axis_size("row")
    groups = layers // GROUP

    def across(array, layer_mask, row_mask):
        pairs = [
            (l * rows + r, (l ^ layer_mask) * rows + (r ^ row_mask))
            for l in range(layers)
            for r in range(rows)
        ]
        return lax.ppermute(array, ("layer", "row"), pairs)

    layer = lax.axis_index("layer")
    share = incident.shape[0] // CORES
    field = jnp.where(layer // GROUP == 0, incident, cotangent)
    field = lax.dynamic_slice_in_dim(field, layer % CORES * share, share)
    folded = fold(coupling, band_off, band_width, field)
    batches, distances = gather_batches(folded, across, rows)

    kept, upper, lower, starts, send = run_first(batches, distances, field, orders)
    for step in range(1, groups):
        pairs = []
        for index in range(GROUP * rows):
            forward_from = (step - 1) * GROUP * rows + index
            adjoint_from = (groups - step) * GROUP * rows + index
            pairs.append((forward_from, forward_from + GROUP * rows))
            pairs.append((adjoint_from, adjoint_from - GROUP * rows))
        field = lax.ppermute(send, ("layer", "row"), pairs)
        kept, *send = run_next(step, groups, upper, lower, starts, field, kept)
        send = send[0] if send else None
    return tuple(join(kept, across(kept, 1, 0)))


def solution(mesh):
    in_specs = (P("layer", "row", None), P("layer"), P("layer"), P(None, "row"), P(None, "row"))
    out_specs = (P("layer", None, "row"), P("layer", None, "row"))
    return jax.shard_map(
        on_device, mesh=mesh, in_specs=in_specs, out_specs=out_specs, check_vma=False
    )
```

```python
import functools

import jax
import jax.numpy as jnp
from jax import lax
from jax.experimental import pallas as pl
from jax.experimental.pallas import tpu as pltpu
from jax.sharding import PartitionSpec as P

BLOCK = 16
GROUP = 8
LANES = 128
BLOCKS_PER_LANES = LANES // BLOCK
PACKED = LANES - BLOCK
DEGREE = 4
SMALL_GRANT = 4 * 1024 * 1024
CORES = 2
SUBLANES = 8
FIELD_PARTS = 2


def field_rows(fields, panel):
    return -(-fields // FIELD_PARTS * (panel // LANES) // BLOCK) * BLOCK


def fold_kernel(coupling_ref, field_ref, folded_ref):
    rows, orders = coupling_ref.shape[1:]
    slot = lax.axis_index("layer") % GROUP
    panel = field_ref.shape[1]
    fields = field_ref.shape[0] - 2 * SUBLANES
    part = fields // FIELD_PARTS
    mine = field_ref[pl.ds(pl.multiple_of(slot // CORES % FIELD_PARTS * part, part), part), :]
    sent = [mine[:, u : u + LANES] for u in range(0, panel, LANES)]
    spare = field_rows(fields, panel) - part * len(sent)
    if spare:
        sent.append(jnp.zeros((spare, LANES), jnp.float32))
    sent = jnp.concatenate(sent, axis=0).astype(jnp.bfloat16)
    folded_ref[panel // LANES * PACKED :, :] = sent
    first = jnp.max(field_ref[fields : fields + SUBLANES, :LANES]).astype(jnp.int32)
    last = jnp.max(field_ref[fields + SUBLANES :, :LANES]).astype(jnp.int32)
    first_block = lax.axis_index("row") * (rows // BLOCK)
    lane = lax.broadcasted_iota(jnp.int32, (BLOCK, LANES), 1)
    sub = lax.broadcasted_iota(jnp.int32, (BLOCK, LANES), 0)
    top = orders // LANES - 1
    for local in range(rows // BLOCK):
        if local % BLOCKS_PER_LANES == 0:
            runs = []
        block = first_block + local
        start = (block + first) * BLOCK
        tile = start >> 7
        shift = start & (LANES - 1)
        here = slice(local * BLOCK, (local + 1) * BLOCK)

        def part(index):
            column = pl.multiple_of(jnp.clip(index, 0, top) * LANES, LANES)
            return coupling_ref[0, here, pl.ds(column, LANES)].astype(jnp.float32)

        near = lane >= shift
        column = jnp.where(near, lane, lane + LANES) + tile * LANES
        limit = jnp.minimum((block + last + 1) * BLOCK, orders)
        keep = (column > block * BLOCK + sub) & (column < limit)
        folded = jnp.where(keep, jnp.where(near, part(tile), part(tile + 1)), 0.0)
        is_last = block * BLOCK + sub == orders - 1
        folded = jnp.where(is_last, first.astype(jnp.float32), folded)
        runs.append(pltpu.roll(folded, (-first * BLOCK) & (LANES - 1), 1))
        if len(runs) == BLOCKS_PER_LANES:
            base = local * BLOCK // LANES * PACKED
            for b, run in enumerate(runs[:-1]):
                hole = lane // BLOCK == (b - 1) % BLOCKS_PER_LANES
                folded_ref[base + b * BLOCK : base + (b + 1) * BLOCK, :] = jnp.where(
                    hole, runs[-1], run
                ).astype(jnp.bfloat16)


def fold(coupling, field):
    rows, orders = coupling.shape[1:]
    sent = rows // LANES * PACKED + field_rows(field.shape[0] - 2 * SUBLANES, field.shape[1])
    vmem = pl.BlockSpec(memory_space=pltpu.VMEM)
    return pl.pallas_call(
        fold_kernel,
        out_shape=jax.ShapeDtypeStruct((sent, LANES), jnp.bfloat16),
        in_specs=[vmem, vmem],
        out_specs=vmem,
        compiler_params=pltpu.CompilerParams(vmem_limit_bytes=SMALL_GRANT),
        name="fold",
    )(coupling, field)


def batch_kernel(*refs):
    for index, piece in enumerate(refs[:-1]):
        refs[-1][index] = piece[...]


def batch(pieces):
    vmem = pl.BlockSpec(memory_space=pltpu.VMEM)
    return pl.pallas_call(
        batch_kernel,
        out_shape=jax.ShapeDtypeStruct((len(pieces), *pieces[0].shape), pieces[0].dtype),
        in_specs=[vmem] * len(pieces),
        out_specs=vmem,
        compiler_params=pltpu.CompilerParams(vmem_limit_bytes=SMALL_GRANT),
        name="batch",
    )(*pieces)


def place(pieces, distances, folds):
    slot = lax.axis_index("layer") % GROUP
    row = lax.axis_index("row")
    rows = folds.shape[1] // lax.axis_size("row")
    for (ref, index), options in zip(pieces, distances):
        layer_mask, row_mask = by_core(options)
        here = pl.ds(pl.multiple_of((row ^ row_mask) * rows, BLOCK), rows)
        folds[slot ^ layer_mask, here, :] = ref[index, :rows, :]


def by_core(options):
    core = lax.axis_index("layer") % CORES
    return [jnp.where(core == 0, *pair) for pair in zip(*options)]


def place_field(own, pieces, distances, field):
    slot = lax.axis_index("layer") % GROUP
    row = lax.axis_index("row")
    fields, panel = field.shape[1], own.shape[1]
    part, tiles = fields // FIELD_PARTS, panel // LANES
    for (ref, index), options in zip(pieces, distances):
        if not options[0][0] % CORES:
            layer_mask, row_mask = by_core(options)
            sender = (slot ^ layer_mask) // CORES
            here = pl.ds(pl.multiple_of(sender % FIELD_PARTS * part, part), part)
            sent = ref[index, tiles * PACKED :, :].astype(jnp.float32)
            for u in range(tiles):
                field[(row ^ row_mask) * tiles + u, here, :] = sent[u * part : (u + 1) * part]
    for u in range(tiles):
        field[row * tiles + u] = own[:fields, u * LANES : (u + 1) * LANES]


def fill_masks(masks):
    row = lax.broadcasted_iota(jnp.int32, (LANES, LANES), 0)
    lane = lax.broadcasted_iota(jnp.int32, (LANES, LANES), 1)
    masks[0] = (lane >= row // BLOCK * BLOCK).astype(jnp.float32).astype(jnp.bfloat16)
    masks[1] = (row >= lane // BLOCK * BLOCK).astype(jnp.float32).astype(jnp.bfloat16)
    masks[2] = (row < LANES - 1).astype(jnp.float32).astype(jnp.bfloat16)
    own = lane // BLOCK != (row // BLOCK + BLOCKS_PER_LANES - 1) % BLOCKS_PER_LANES
    masks[3] = own.astype(jnp.float32).astype(jnp.bfloat16)


def expand(folds, slot, masks, upper, lower):
    tiles = upper.shape[0]
    lane = lax.broadcasted_iota(jnp.int32, (1, LANES), 1)
    eighth = folds[slot, (tiles - 1) * PACKED : (tiles - 1) * PACKED + BLOCK, :]
    last_row = eighth.astype(jnp.float32)[BLOCK - 1 :, :]
    last_row = jnp.where(lane >= PACKED, last_row, -float(LANES))
    first = jnp.max(last_row).astype(jnp.int32)
    for t in range(tiles):
        packed = folds[slot, t * PACKED : (t + 1) * PACKED, :]
        own = packed * masks[3, :PACKED, :]
        rest = packed - own
        eighth = [rest[b : b + BLOCK] for b in range(0, PACKED, BLOCK)]
        while len(eighth) > 1:
            eighth = [sum(eighth[i : i + 2][1:], eighth[i]) for i in range(0, len(eighth), 2)]
        run = jnp.concatenate([own, eighth[0]], axis=0)
        if t == tiles - 1:
            run = run * masks[2]
        near = run * masks[0]
        upper[t, :, :LANES] = near
        upper[t, :, LANES:] = run - near
        turned = run.T
        near = turned * masks[1]
        lower[t, :, :LANES] = near
        lower[(t + 1) % tiles, :, LANES:] = turned - near
    return first


def banded_product(v, upper, lower, start, xs, zs):
    tiles = len(v)
    whole = start >> 3
    fine = (start & (BLOCKS_PER_LANES - 1)) * BLOCK
    lane = lax.broadcasted_iota(jnp.int32, v[0].shape, 1)
    turned = [pltpu.roll(part, (LANES - fine) & (LANES - 1), 1) for part in v]
    for u in range(tiles):
        moved = jnp.where(lane < LANES - fine, turned[u], turned[(u + 1) % tiles])
        xs[u] = moved.astype(jnp.bfloat16)
    first = [
        jnp.dot(v[t].astype(jnp.bfloat16), upper[t], preferred_element_type=jnp.float32)
        for t in range(tiles)
    ]
    sums = [first[t][:, :LANES] + first[t - 1][:, LANES:] for t in range(tiles)]
    turned = [pltpu.roll(part, fine, 1) for part in sums]
    for u in range(tiles):
        zs[u] = jnp.where(lane >= fine, turned[u], turned[u - 1])
    second = [
        jnp.dot(
            xs[(whole + u) & (tiles - 1)], lower[u], preferred_element_type=jnp.float32
        )
        for u in range(tiles)
    ]
    return [
        zs[(u - whole) & (tiles - 1)]
        - (second[u][:, :LANES] + second[(u + 1) % tiles][:, LANES:])
        for u in range(tiles)
    ]


def run_layer(x, sign, upper, lower, start, xs, zs):
    v = x
    for divisor in range(DEGREE, 0, -1):
        scale = sign * (1.0 / divisor)
        product = banded_product(v, upper, lower, start, xs, zs)
        v = [part + scale * term for part, term in zip(x, product)]
    return v


def cascade_first_kernel(distances, *refs):
    pieces = []
    for count in distances[0]:
        pieces += [(refs[0], index) for index in range(count)]
        refs = refs[1:]
    own, kept, upper, lower, starts, send, folds, masks, xs, zs = refs
    place(pieces, distances[1], folds)
    fill_masks(masks)
    place_field(own, pieces, distances[1], zs)
    x = [zs[u] for u in range(zs.shape[0])]
    forward = lax.axis_index("layer") // GROUP == 0
    sign = jnp.where(forward, -1.0, 1.0)

    def prepare(k):
        slot = jnp.where(forward, k, GROUP - 1 - k)
        start = expand(folds, slot, masks, upper.at[k], lower.at[k])
        starts[k : k + 1, :] = jnp.full((1, LANES), start, jnp.int32)
        return start

    start = prepare(0)
    for k in range(GROUP):
        following = prepare(k + 1) if k + 1 < GROUP else None
        x = run_layer(x, sign, upper.at[k], lower.at[k], start, xs, zs)
        start = following
    mine = own_panel(x, kept.shape[-1])
    kept[0] = mine
    kept[1] = mine
    write_whole(x, send)


def cascade_next_kernel(step, groups, *refs):
    upper, lower, starts, field, before, kept, *send, xs, zs = refs
    panel = kept.shape[-1]
    group = lax.axis_index("layer") // GROUP
    forward = group == step
    backward = group == groups - 1 - step
    sign = jnp.where(forward, -1.0, 1.0)
    same_order = forward == (group == 0)
    x = field[...].astype(jnp.float32)
    x = [x[:, u : u + LANES] for u in range(0, x.shape[1], LANES)]

    order = [jnp.where(same_order, k, GROUP - 1 - k) for k in range(GROUP)]
    begin = [jnp.max(starts[pl.ds(at, 1), :]) for at in order]
    for at, start in zip(order, begin):
        x = run_layer(x, sign, upper.at[at], lower.at[at], start, xs, zs)
    mine = own_panel(x, panel)
    kept[0] = jnp.where(forward, mine, before[0])
    kept[1] = jnp.where(backward, mine, before[1])
    if send:
        write_whole(x, *send)


def write_whole(x, send):
    for u, part in enumerate(x):
        send[:, u * LANES : (u + 1) * LANES] = part.astype(jnp.bfloat16)


def own_panel(x, panel):
    row = lax.axis_index("row")
    tiles = panel // LANES
    mine = x[:tiles]
    for index in range(1, len(x) // tiles):
        there = x[index * tiles : (index + 1) * tiles]
        mine = [jnp.where(row == index, new, old) for new, old in zip(there, mine)]
    return jnp.concatenate(mine, axis=1)


def join_kernel(mine, theirs, *outs):
    core = lax.axis_index("layer") % CORES
    count = mine.shape[1]
    for kind, out in enumerate(outs):
        for part, at in ((mine, core), (theirs, 1 - core)):
            out[0, pl.ds(pl.multiple_of(at * count, count), count), :] = part[kind]


def join(mine, theirs):
    kinds, count, panel = mine.shape
    vmem = pl.BlockSpec(memory_space=pltpu.VMEM)
    return pl.pallas_call(
        join_kernel,
        out_shape=[jax.ShapeDtypeStruct((1, CORES * count, panel), mine.dtype)] * kinds,
        in_specs=[vmem] * 2,
        out_specs=[vmem] * kinds,
        compiler_params=pltpu.CompilerParams(vmem_limit_bytes=SMALL_GRANT),
        name="join",
    )(mine, theirs)


def run_first(batches, distances, field, orders):
    count, panel = field.shape[0] - 2 * SUBLANES, field.shape[1]
    tiles = orders // LANES
    vmem = pl.BlockSpec(memory_space=pltpu.VMEM)
    window = jax.ShapeDtypeStruct((GROUP, tiles, LANES, 2 * LANES), jnp.bfloat16)
    return pl.pallas_call(
        functools.partial(cascade_first_kernel, distances),
        out_shape=[
            jax.ShapeDtypeStruct((2, count, panel), jnp.float32),
            window,
            window,
            jax.ShapeDtypeStruct((GROUP, LANES), jnp.int32),
            jax.ShapeDtypeStruct((count, orders), jnp.bfloat16),
        ],
        in_specs=[vmem] * (len(batches) + 1),
        out_specs=[vmem] * 5,
        scratch_shapes=[
            pltpu.VMEM((GROUP, tiles * PACKED, LANES), jnp.bfloat16),
            pltpu.VMEM((4, LANES, LANES), jnp.bfloat16),
            pltpu.VMEM((tiles, count, LANES), jnp.bfloat16),
            pltpu.VMEM((tiles, count, LANES), jnp.float32),
        ],
        compiler_params=pltpu.CompilerParams(vmem_limit_bytes=24 * 1024 * 1024),
        name="cascade_first",
    )(*batches, field)


def run_next(step, groups, upper, lower, starts, field, kept):
    count, orders = field.shape
    tiles = orders // LANES
    vmem = pl.BlockSpec(memory_space=pltpu.VMEM)
    out_shape = [jax.ShapeDtypeStruct(kept.shape, jnp.float32)]
    if step < groups - 1:
        out_shape.append(jax.ShapeDtypeStruct(field.shape, jnp.bfloat16))
    return pl.pallas_call(
        functools.partial(cascade_next_kernel, step, groups),
        out_shape=out_shape,
        in_specs=[vmem] * 5,
        out_specs=[vmem] * len(out_shape),
        scratch_shapes=[
            pltpu.VMEM((tiles, count, LANES), jnp.bfloat16),
            pltpu.VMEM((tiles, count, LANES), jnp.float32),
        ],
        compiler_params=pltpu.CompilerParams(vmem_limit_bytes=24 * 1024 * 1024),
        name=f"cascade_{step}",
    )(upper, lower, starts, field, kept)


def gather_batches(own, across, rows):
    bits = [(0, 1 << b) for b in range(rows.bit_length() - 1)]
    bits += [(1 << b, 0) for b in range(1, GROUP.bit_length() - 1)]
    count = len(bits)

    def members(subset):
        return [b for b in range(count) if subset >> b & 1]

    def distance(subset):
        return tuple(
            tuple(sum(bits[(b + core) % count][axis] for b in members(subset)) for axis in (0, 1))
            for core in range(CORES)
        )

    subsets = sorted(range(1 << count), key=lambda m: (m.bit_count(), m))
    pieces = {0: own}
    for subset in subsets[1 : count + 1] + subsets[-1:]:
        pieces[subset] = across(own, distance(subset))
    for subset in subsets[count + 1 : -1]:
        which = members(subset)
        link = next((b for b in which if (b + 1) % count in which), which[0])
        pieces[subset] = across(pieces[subset ^ 1 << link], distance(1 << link))
    batches, counts, distances = [], [], []
    for part in (subsets[: count + 1], subsets[count + 1 :]):
        mine = batch([pieces[subset] for subset in part])
        batches += [mine, across(mine, ((1, 0), (1, 0)))]
        counts += [len(part), len(part)]
        distances += [distance(subset) for subset in part]
        distances += [
            tuple((a ^ 1, b) for a, b in options[::-1]) for options in distances[-len(part) :]
        ]
    return batches, (tuple(counts), tuple(distances))


def on_device(coupling, band_off, band_width, incident, cotangent):
    panel, orders = coupling.shape[1:]
    layers = lax.axis_size("layer")
    rows = lax.axis_size("row")
    groups = layers // GROUP

    def across(array, options):
        pairs = []
        for l in range(layers):
            layer_mask, row_mask = options[l % CORES]
            for r in range(rows):
                pairs.append((l * rows + r, (l ^ layer_mask) * rows + (r ^ row_mask)))
        return lax.ppermute(array, ("layer", "row"), pairs)

    layer = lax.axis_index("layer")
    share = incident.shape[0] // CORES
    field = jnp.where(layer // GROUP == 0, incident, cotangent)
    field = lax.dynamic_slice_in_dim(field, layer % CORES * share, share)
    first = (band_off - band_width).astype(jnp.float32)
    last = (band_off + band_width).astype(jnp.float32)
    ends = [jnp.broadcast_to(end, (SUBLANES, panel)) for end in (first, last)]
    field = jnp.concatenate([field, *ends], axis=0)
    folded = fold(coupling, field)
    batches, distances = gather_batches(folded, across, rows)

    kept, upper, lower, starts, send = run_first(batches, distances, field, orders)
    for step in range(1, groups):
        pairs = []
        for index in range(GROUP * rows):
            forward_from = (step - 1) * GROUP * rows + index
            adjoint_from = (groups - step) * GROUP * rows + index
            pairs.append((forward_from, forward_from + GROUP * rows))
            pairs.append((adjoint_from, adjoint_from - GROUP * rows))
        field = lax.ppermute(send, ("layer", "row"), pairs)
        kept, *send = run_next(step, groups, upper, lower, starts, field, kept)
        send = send[0] if send else None
    return tuple(join(kept, across(kept, ((1, 0), (1, 0)))))


def solution(mesh):
    in_specs = (P("layer", "row", None), P("layer"), P("layer"), P(None, "row"), P(None, "row"))
    out_specs = (P("layer", None, "row"), P("layer", None, "row"))
    return jax.shard_map(
        on_device, mesh=mesh, in_specs=in_specs, out_specs=out_specs, check_vma=False
    )
```

```python
import functools

import jax
import jax.numpy as jnp
from jax import lax
from jax.experimental import pallas as pl
from jax.experimental.pallas import tpu as pltpu
from jax.sharding import PartitionSpec as P

BLOCK = 16
GROUP = 8
LANES = 128
BLOCKS_PER_LANES = LANES // BLOCK
PACKED = LANES - BLOCK
DEGREE = 4
SMALL_GRANT = 4 * 1024 * 1024
CORES = 2
SUBLANES = 8
FIELD_PARTS = 2


def field_rows(fields, panel):
    return -(-fields // FIELD_PARTS * (panel // LANES) // BLOCK) * BLOCK


def fold_kernel(coupling_ref, field_ref, folded_ref):
    rows, orders = coupling_ref.shape[1:]
    slot = lax.axis_index("layer") % GROUP
    panel = field_ref.shape[1]
    fields = field_ref.shape[0] - 2 * SUBLANES
    part = fields // FIELD_PARTS
    mine = field_ref[pl.ds(pl.multiple_of(slot // CORES % FIELD_PARTS * part, part), part), :]
    sent = [mine[:, u : u + LANES] for u in range(0, panel, LANES)]
    spare = field_rows(fields, panel) - part * len(sent)
    if spare:
        sent.append(jnp.zeros((spare, LANES), jnp.float32))
    sent = jnp.concatenate(sent, axis=0).astype(jnp.bfloat16)
    folded_ref[0, panel // LANES * PACKED :, :] = sent
    first = jnp.max(field_ref[fields : fields + SUBLANES, :LANES]).astype(jnp.int32)
    last = jnp.max(field_ref[fields + SUBLANES :, :LANES]).astype(jnp.int32)
    first_block = lax.axis_index("row") * (rows // BLOCK)
    lane = lax.broadcasted_iota(jnp.int32, (BLOCK, LANES), 1)
    sub = lax.broadcasted_iota(jnp.int32, (BLOCK, LANES), 0)
    top = orders // LANES - 1
    for local in range(rows // BLOCK):
        if local % BLOCKS_PER_LANES == 0:
            runs = []
        block = first_block + local
        start = (block + first) * BLOCK
        tile = start >> 7
        shift = start & (LANES - 1)
        here = slice(local * BLOCK, (local + 1) * BLOCK)

        def part(index):
            column = pl.multiple_of(jnp.clip(index, 0, top) * LANES, LANES)
            return coupling_ref[0, here, pl.ds(column, LANES)].astype(jnp.float32)

        near = lane >= shift
        column = jnp.where(near, lane, lane + LANES) + tile * LANES
        limit = jnp.minimum((block + last + 1) * BLOCK, orders)
        keep = (column > block * BLOCK + sub) & (column < limit)
        folded = jnp.where(keep, jnp.where(near, part(tile), part(tile + 1)), 0.0)
        is_last = block * BLOCK + sub == orders - 1
        folded = jnp.where(is_last, first.astype(jnp.float32), folded)
        runs.append(pltpu.roll(folded, (-first * BLOCK) & (LANES - 1), 1))
        if len(runs) == BLOCKS_PER_LANES:
            base = local * BLOCK // LANES * PACKED
            for b, run in enumerate(runs[:-1]):
                hole = lane // BLOCK == (b - 1) % BLOCKS_PER_LANES
                there = slice(base + b * BLOCK, base + (b + 1) * BLOCK)
                folded_ref[0, there, :] = jnp.where(hole, runs[-1], run).astype(jnp.bfloat16)


def fold(coupling, field):
    rows, orders = coupling.shape[1:]
    sent = rows // LANES * PACKED + field_rows(field.shape[0] - 2 * SUBLANES, field.shape[1])
    vmem = pl.BlockSpec(memory_space=pltpu.VMEM)
    return pl.pallas_call(
        fold_kernel,
        out_shape=jax.ShapeDtypeStruct((1, sent, LANES), jnp.bfloat16),
        in_specs=[vmem, vmem],
        out_specs=vmem,
        compiler_params=pltpu.CompilerParams(vmem_limit_bytes=SMALL_GRANT),
        name="fold",
    )(coupling, field)


def batch_kernel(*refs):
    first = 0
    for piece in refs[:-1]:
        count = piece.shape[0]
        refs[-1][first : first + count] = piece[...]
        first += count


def batch(pieces):
    vmem = pl.BlockSpec(memory_space=pltpu.VMEM)
    return pl.pallas_call(
        batch_kernel,
        out_shape=jax.ShapeDtypeStruct(
            (sum(piece.shape[0] for piece in pieces), *pieces[0].shape[1:]), pieces[0].dtype
        ),
        in_specs=[vmem] * len(pieces),
        out_specs=vmem,
        compiler_params=pltpu.CompilerParams(vmem_limit_bytes=SMALL_GRANT),
        name="batch",
    )(*pieces)


def place(pieces, distances, folds):
    slot = lax.axis_index("layer") % GROUP
    row = lax.axis_index("row")
    rows = folds.shape[1] // lax.axis_size("row")
    for (ref, index), options in zip(pieces, distances):

        @on_core(options)
        def _(layer_mask, row_mask, ref=ref, index=index):
            here = pl.ds(pl.multiple_of((row ^ row_mask) * rows, BLOCK), rows)
            folds[slot ^ layer_mask, here, :] = ref[index, :rows, :]


def on_core(options):
    core = lax.axis_index("layer") % CORES

    def run(function):
        if None in options:
            known = 1 - options.index(None)
            pl.when(core == known)(lambda: function(*options[known]))
        else:
            function(*[jnp.where(core == 0, *pair) for pair in zip(*options)])

    return run


def place_field(own, pieces, distances, field):
    slot = lax.axis_index("layer") % GROUP
    row = lax.axis_index("row")
    fields, panel = field.shape[1], own.shape[1]
    part, tiles = fields // FIELD_PARTS, panel // LANES
    for (ref, index), options in zip(pieces, distances):
        if (options[0] or options[1])[0] % CORES:
            continue

        @on_core(options)
        def _(layer_mask, row_mask, ref=ref, index=index):
            sender = (slot ^ layer_mask) // CORES
            here = pl.ds(pl.multiple_of(sender % FIELD_PARTS * part, part), part)
            sent = ref[index, tiles * PACKED :, :].astype(jnp.float32)
            for u in range(tiles):
                field[(row ^ row_mask) * tiles + u, here, :] = sent[u * part : (u + 1) * part]

    for u in range(tiles):
        field[row * tiles + u] = own[:fields, u * LANES : (u + 1) * LANES]


def fill_masks(masks):
    row = lax.broadcasted_iota(jnp.int32, (LANES, LANES), 0)
    lane = lax.broadcasted_iota(jnp.int32, (LANES, LANES), 1)
    masks[0] = (lane >= row // BLOCK * BLOCK).astype(jnp.float32).astype(jnp.bfloat16)
    masks[1] = (row >= lane // BLOCK * BLOCK).astype(jnp.float32).astype(jnp.bfloat16)
    masks[2] = (row < LANES - 1).astype(jnp.float32).astype(jnp.bfloat16)
    own = lane // BLOCK != (row // BLOCK + BLOCKS_PER_LANES - 1) % BLOCKS_PER_LANES
    masks[3] = own.astype(jnp.float32).astype(jnp.bfloat16)


def expand(folds, slot, masks, upper, lower):
    tiles = upper.shape[0]
    lane = lax.broadcasted_iota(jnp.int32, (1, LANES), 1)
    eighth = folds[slot, (tiles - 1) * PACKED : (tiles - 1) * PACKED + BLOCK, :]
    last_row = eighth.astype(jnp.float32)[BLOCK - 1 :, :]
    last_row = jnp.where(lane >= PACKED, last_row, -float(LANES))
    first = jnp.max(last_row).astype(jnp.int32)
    for t in range(tiles):
        packed = folds[slot, t * PACKED : (t + 1) * PACKED, :]
        own = packed * masks[3, :PACKED, :]
        rest = packed - own
        eighth = [rest[b : b + BLOCK] for b in range(0, PACKED, BLOCK)]
        while len(eighth) > 1:
            eighth = [sum(eighth[i : i + 2][1:], eighth[i]) for i in range(0, len(eighth), 2)]
        run = jnp.concatenate([own, eighth[0]], axis=0)
        if t == tiles - 1:
            run = run * masks[2]
        near = run * masks[0]
        upper[t, :, :LANES] = near
        upper[t, :, LANES:] = run - near
        turned = run.T
        near = turned * masks[1]
        lower[t, :, :LANES] = near
        lower[(t + 1) % tiles, :, LANES:] = turned - near
    return first


def banded_product(v, upper, lower, start, xs, zs):
    tiles = len(v)
    whole = start >> 3
    fine = (start & (BLOCKS_PER_LANES - 1)) * BLOCK
    lane = lax.broadcasted_iota(jnp.int32, v[0].shape, 1)
    turned = [pltpu.roll(part, (LANES - fine) & (LANES - 1), 1) for part in v]
    for u in range(tiles):
        moved = jnp.where(lane < LANES - fine, turned[u], turned[(u + 1) % tiles])
        xs[u] = moved.astype(jnp.bfloat16)
    first = [
        jnp.dot(v[t].astype(jnp.bfloat16), upper[t], preferred_element_type=jnp.float32)
        for t in range(tiles)
    ]
    sums = [first[t][:, :LANES] + first[t - 1][:, LANES:] for t in range(tiles)]
    turned = [pltpu.roll(part, fine, 1) for part in sums]
    for u in range(tiles):
        zs[u] = jnp.where(lane >= fine, turned[u], turned[u - 1])
    second = [
        jnp.dot(
            xs[(whole + u) & (tiles - 1)], lower[u], preferred_element_type=jnp.float32
        )
        for u in range(tiles)
    ]
    return [
        zs[(u - whole) & (tiles - 1)]
        - (second[u][:, :LANES] + second[(u + 1) % tiles][:, LANES:])
        for u in range(tiles)
    ]


def run_layer(x, sign, upper, lower, start, xs, zs):
    v = x
    for divisor in range(DEGREE, 0, -1):
        scale = sign * (1.0 / divisor)
        product = banded_product(v, upper, lower, start, xs, zs)
        v = [part + scale * term for part, term in zip(x, product)]
    return v


def cascade_first_kernel(distances, *refs):
    pieces = []
    for count in distances[0]:
        pieces += [(refs[0], index) for index in range(count)]
        refs = refs[1:]
    own, kept, upper, lower, starts, send, folds, masks, xs, zs = refs
    place(pieces, distances[1], folds)
    fill_masks(masks)
    place_field(own, pieces, distances[1], zs)
    x = [zs[u] for u in range(zs.shape[0])]
    forward = lax.axis_index("layer") // GROUP == 0
    sign = jnp.where(forward, -1.0, 1.0)

    def prepare(k):
        slot = jnp.where(forward, k, GROUP - 1 - k)
        start = expand(folds, slot, masks, upper.at[k], lower.at[k])
        starts[k : k + 1, :] = jnp.full((1, LANES), start, jnp.int32)
        return start

    start = prepare(0)
    for k in range(GROUP):
        following = prepare(k + 1) if k + 1 < GROUP else None
        x = run_layer(x, sign, upper.at[k], lower.at[k], start, xs, zs)
        start = following
    mine = own_panel(x, kept.shape[-1])
    kept[0] = mine
    kept[1] = mine
    write_whole(x, send)


def cascade_next_kernel(step, groups, *refs):
    upper, lower, starts, field, before, kept, *send, xs, zs = refs
    panel = kept.shape[-1]
    group = lax.axis_index("layer") // GROUP
    forward = group == step
    backward = group == groups - 1 - step
    sign = jnp.where(forward, -1.0, 1.0)
    same_order = forward == (group == 0)
    x = field[...].astype(jnp.float32)
    x = [x[:, u : u + LANES] for u in range(0, x.shape[1], LANES)]

    order = [jnp.where(same_order, k, GROUP - 1 - k) for k in range(GROUP)]
    begin = [jnp.max(starts[pl.ds(at, 1), :]) for at in order]
    for at, start in zip(order, begin):
        x = run_layer(x, sign, upper.at[at], lower.at[at], start, xs, zs)
    mine = own_panel(x, panel)
    kept[0] = jnp.where(forward, mine, before[0])
    kept[1] = jnp.where(backward, mine, before[1])
    if send:
        write_whole(x, *send)


def write_whole(x, send):
    for u, part in enumerate(x):
        send[:, u * LANES : (u + 1) * LANES] = part.astype(jnp.bfloat16)


def own_panel(x, panel):
    row = lax.axis_index("row")
    tiles = panel // LANES
    mine = x[:tiles]
    for index in range(1, len(x) // tiles):
        there = x[index * tiles : (index + 1) * tiles]
        mine = [jnp.where(row == index, new, old) for new, old in zip(there, mine)]
    return jnp.concatenate(mine, axis=1)


def join_kernel(mine, theirs, *outs):
    core = lax.axis_index("layer") % CORES
    count = mine.shape[1]
    for kind, out in enumerate(outs):
        for part, at in ((mine, core), (theirs, 1 - core)):
            out[0, pl.ds(pl.multiple_of(at * count, count), count), :] = part[kind]


def join(mine, theirs):
    kinds, count, panel = mine.shape
    vmem = pl.BlockSpec(memory_space=pltpu.VMEM)
    return pl.pallas_call(
        join_kernel,
        out_shape=[jax.ShapeDtypeStruct((1, CORES * count, panel), mine.dtype)] * kinds,
        in_specs=[vmem] * 2,
        out_specs=[vmem] * kinds,
        compiler_params=pltpu.CompilerParams(vmem_limit_bytes=SMALL_GRANT),
        name="join",
    )(mine, theirs)


def run_first(batches, distances, field, orders):
    count, panel = field.shape[0] - 2 * SUBLANES, field.shape[1]
    tiles = orders // LANES
    vmem = pl.BlockSpec(memory_space=pltpu.VMEM)
    window = jax.ShapeDtypeStruct((GROUP, tiles, LANES, 2 * LANES), jnp.bfloat16)
    return pl.pallas_call(
        functools.partial(cascade_first_kernel, distances),
        out_shape=[
            jax.ShapeDtypeStruct((2, count, panel), jnp.float32),
            window,
            window,
            jax.ShapeDtypeStruct((GROUP, LANES), jnp.int32),
            jax.ShapeDtypeStruct((count, orders), jnp.bfloat16),
        ],
        in_specs=[vmem] * (len(batches) + 1),
        out_specs=[vmem] * 5,
        scratch_shapes=[
            pltpu.VMEM((GROUP, tiles * PACKED, LANES), jnp.bfloat16),
            pltpu.VMEM((4, LANES, LANES), jnp.bfloat16),
            pltpu.VMEM((tiles, count, LANES), jnp.bfloat16),
            pltpu.VMEM((tiles, count, LANES), jnp.float32),
        ],
        compiler_params=pltpu.CompilerParams(vmem_limit_bytes=24 * 1024 * 1024),
        name="cascade_first",
    )(*batches, field)


def run_next(step, groups, upper, lower, starts, field, kept):
    count, orders = field.shape
    tiles = orders // LANES
    vmem = pl.BlockSpec(memory_space=pltpu.VMEM)
    out_shape = [jax.ShapeDtypeStruct(kept.shape, jnp.float32)]
    if step < groups - 1:
        out_shape.append(jax.ShapeDtypeStruct(field.shape, jnp.bfloat16))
    return pl.pallas_call(
        functools.partial(cascade_next_kernel, step, groups),
        out_shape=out_shape,
        in_specs=[vmem] * 5,
        out_specs=[vmem] * len(out_shape),
        scratch_shapes=[
            pltpu.VMEM((tiles, count, LANES), jnp.bfloat16),
            pltpu.VMEM((tiles, count, LANES), jnp.float32),
        ],
        compiler_params=pltpu.CompilerParams(vmem_limit_bytes=24 * 1024 * 1024),
        name=f"cascade_{step}",
    )(upper, lower, starts, field, kept)


def routes(count):
    if count == 3:
        return [(0, 2, 1), (0, 4, 7), (1, 4, 2), (2, 1, None)]
    ways = [*range(1, 1 << count), None]
    return [(0, *ways[k : k + 2]) for k in range(0, 1 << count, 2)]


def gather_batches(own, across, rows):
    bits = [(0, 1 << b) for b in range(rows.bit_length() - 1)]
    bits += [(1 << b, 0) for b in range(1, GROUP.bit_length() - 1)]
    other_core = ((1, 0), (1, 0))

    def distance(way):
        if way is None:
            return None
        chosen = [bit for b, bit in enumerate(bits) if way >> b & 1]
        return tuple(sum(bit[axis] for bit in chosen) for axis in (0, 1))

    arrays = [batch([own, across(own, other_core)])]
    ways = [(0, 0)]
    for source, *links in routes(len(bits)):
        arrays.append(across(arrays[source], tuple(distance(link) for link in links)))
        ways.append(
            tuple(None if b is None else a ^ b for a, b in zip(ways[source], links))
        )

    def far(options):
        return tuple(pair and (pair[0] ^ 1, pair[1]) for pair in options)

    batches, counts, distances = arrays[:1], [CORES], [((0, 0), (0, 0)), other_core]
    half = (len(arrays) + 1) // 2
    for part in (range(1, half), range(half, len(arrays))):
        mine = batch([arrays[n] for n in part])
        batches += [mine, across(mine, other_core)]
        counts += [CORES * len(part)] * 2
        there = [tuple(distance(way) for way in ways[n]) for n in part]
        distances += [kind for pair in there for kind in (pair, far(pair))]
        distances += [kind for pair in there for kind in (far(pair[::-1]), pair[::-1])]
    return batches, (tuple(counts), tuple(distances))


def on_device(coupling, band_off, band_width, incident, cotangent):
    panel, orders = coupling.shape[1:]
    layers = lax.axis_size("layer")
    rows = lax.axis_size("row")
    groups = layers // GROUP

    def across(array, options):
        pairs = []
        for l in range(layers):
            if options[l % CORES] is None:
                continue
            layer_mask, row_mask = options[l % CORES]
            for r in range(rows):
                pairs.append((l * rows + r, (l ^ layer_mask) * rows + (r ^ row_mask)))
        return lax.ppermute(array, ("layer", "row"), pairs)

    layer = lax.axis_index("layer")
    share = incident.shape[0] // CORES
    field = jnp.where(layer // GROUP == 0, incident, cotangent)
    field = lax.dynamic_slice_in_dim(field, layer % CORES * share, share)
    first = (band_off - band_width).astype(jnp.float32)
    last = (band_off + band_width).astype(jnp.float32)
    ends = [jnp.broadcast_to(end, (SUBLANES, panel)) for end in (first, last)]
    field = jnp.concatenate([field, *ends], axis=0)
    folded = fold(coupling, field)
    batches, distances = gather_batches(folded, across, rows)

    kept, upper, lower, starts, send = run_first(batches, distances, field, orders)
    for step in range(1, groups):
        pairs = []
        for index in range(GROUP * rows):
            forward_from = (step - 1) * GROUP * rows + index
            adjoint_from = (groups - step) * GROUP * rows + index
            pairs.append((forward_from, forward_from + GROUP * rows))
            pairs.append((adjoint_from, adjoint_from - GROUP * rows))
        field = lax.ppermute(send, ("layer", "row"), pairs)
        kept, *send = run_next(step, groups, upper, lower, starts, field, kept)
        send = send[0] if send else None
    return tuple(join(kept, across(kept, ((1, 0), (1, 0)))))


def solution(mesh):
    in_specs = (P("layer", "row", None), P("layer"), P("layer"), P(None, "row"), P(None, "row"))
    out_specs = (P("layer", None, "row"), P("layer", None, "row"))
    return jax.shard_map(
        on_device, mesh=mesh, in_specs=in_specs, out_specs=out_specs, check_vma=False
    )
```

```python
import functools

import jax
import jax.numpy as jnp
from jax import lax
from jax.experimental import pallas as pl
from jax.experimental.pallas import tpu as pltpu
from jax.sharding import PartitionSpec as P

BLOCK = 16
GROUP = 8
LANES = 128
BLOCKS_PER_LANES = LANES // BLOCK
PACKED = LANES - BLOCK
DEGREE = 4
SMALL_GRANT = 4 * 1024 * 1024
CORES = 2


def fold_kernel(off_ref, width_ref, coupling_ref, folded_ref):
    rows, orders = coupling_ref.shape[1:]
    first = off_ref[0] - width_ref[0]
    last = off_ref[0] + width_ref[0]
    first_block = lax.axis_index("row") * (rows // BLOCK)
    lane = lax.broadcasted_iota(jnp.int32, (BLOCK, LANES), 1)
    sub = lax.broadcasted_iota(jnp.int32, (BLOCK, LANES), 0)
    top = orders // LANES - 1
    for local in range(rows // BLOCK):
        if local % BLOCKS_PER_LANES == 0:
            runs = []
        block = first_block + local
        start = (block + first) * BLOCK
        tile = start >> 7
        shift = start & (LANES - 1)
        here = slice(local * BLOCK, (local + 1) * BLOCK)

        def part(index):
            column = pl.multiple_of(jnp.clip(index, 0, top) * LANES, LANES)
            return coupling_ref[0, here, pl.ds(column, LANES)].astype(jnp.float32)

        near = lane >= shift
        column = jnp.where(near, lane, lane + LANES) + tile * LANES
        limit = jnp.minimum((block + last + 1) * BLOCK, orders)
        keep = (column > block * BLOCK + sub) & (column < limit)
        folded = jnp.where(keep, jnp.where(near, part(tile), part(tile + 1)), 0.0)
        is_last = block * BLOCK + sub == orders - 1
        folded = jnp.where(is_last, first.astype(jnp.float32), folded)
        runs.append(pltpu.roll(folded, (-first * BLOCK) & (LANES - 1), 1))
        if len(runs) == BLOCKS_PER_LANES:
            base = local * BLOCK // LANES * PACKED
            for b, run in enumerate(runs[:-1]):
                hole = lane // BLOCK == (b - 1) % BLOCKS_PER_LANES
                folded_ref[base + b * BLOCK : base + (b + 1) * BLOCK, :] = jnp.where(
                    hole, runs[-1], run
                ).astype(jnp.bfloat16)


def fold(coupling, band_off, band_width):
    rows, orders = coupling.shape[1:]
    smem = pl.BlockSpec(memory_space=pltpu.SMEM)
    vmem = pl.BlockSpec(memory_space=pltpu.VMEM)
    return pl.pallas_call(
        fold_kernel,
        out_shape=jax.ShapeDtypeStruct((rows // LANES * PACKED, LANES), jnp.bfloat16),
        in_specs=[smem, smem, vmem],
        out_specs=vmem,
        compiler_params=pltpu.CompilerParams(vmem_limit_bytes=SMALL_GRANT),
        name="fold",
    )(band_off, band_width, coupling)


def batch_kernel(*refs):
    rows = refs[-1].shape[1]
    for index, piece in enumerate(refs[:-1]):
        refs[-1][index] = piece[:rows, :]


def batch(pieces):
    vmem = pl.BlockSpec(memory_space=pltpu.VMEM)
    rows = min(piece.shape[0] for piece in pieces)
    return pl.pallas_call(
        batch_kernel,
        out_shape=jax.ShapeDtypeStruct((len(pieces), rows, LANES), pieces[0].dtype),
        in_specs=[vmem] * len(pieces),
        out_specs=vmem,
        compiler_params=pltpu.CompilerParams(vmem_limit_bytes=SMALL_GRANT),
        name="batch",
    )(*pieces)


def corner_kernel(folded, field, out):
    rows, panel = folded.shape[0], field.shape[1]
    count = field.shape[0]
    out[:rows, :] = folded[...]
    for u in range(panel // LANES):
        here = slice(rows + u * count, rows + (u + 1) * count)
        out[here, :] = field[:, u * LANES : (u + 1) * LANES].astype(jnp.bfloat16)


def corner(folded, field):
    vmem = pl.BlockSpec(memory_space=pltpu.VMEM)
    extra = field.size // LANES
    return pl.pallas_call(
        corner_kernel,
        out_shape=jax.ShapeDtypeStruct((folded.shape[0] + extra, LANES), folded.dtype),
        in_specs=[vmem] * 2,
        out_specs=vmem,
        compiler_params=pltpu.CompilerParams(vmem_limit_bytes=SMALL_GRANT),
        name="corner",
    )(folded, field)


def place(pieces, distances, folds):
    slot = lax.axis_index("layer") % GROUP
    row = lax.axis_index("row")
    rows = folds.shape[1] // lax.axis_size("row")
    for (ref, index), options in zip(pieces, distances):
        layer_mask, row_mask = by_core(options)
        here = pl.ds(pl.multiple_of((row ^ row_mask) * rows, BLOCK), rows)
        folds[slot ^ layer_mask, here, :] = ref[index, :rows, :]


def by_core(options):
    core = lax.axis_index("layer") % CORES
    return [jnp.where(core == 0, *pair) for pair in zip(*options)]


def place_field(own, others, field):
    row = lax.axis_index("row")
    count, panel = own.shape
    tiles = panel // LANES
    for u in range(tiles):
        field[row * tiles + u] = own[:, u * LANES : (u + 1) * LANES]
    for piece, row_mask in others:
        first = piece.shape[0] - tiles * count
        for u in range(tiles):
            here = slice(first + u * count, first + (u + 1) * count)
            field[(row ^ row_mask) * tiles + u] = piece[here, :].astype(jnp.float32)


def fill_masks(masks):
    row = lax.broadcasted_iota(jnp.int32, (LANES, LANES), 0)
    lane = lax.broadcasted_iota(jnp.int32, (LANES, LANES), 1)
    masks[0] = (lane >= row // BLOCK * BLOCK).astype(jnp.float32).astype(jnp.bfloat16)
    masks[1] = (row >= lane // BLOCK * BLOCK).astype(jnp.float32).astype(jnp.bfloat16)
    masks[2] = (row < LANES - 1).astype(jnp.float32).astype(jnp.bfloat16)
    own = lane // BLOCK != (row // BLOCK + BLOCKS_PER_LANES - 1) % BLOCKS_PER_LANES
    masks[3] = own.astype(jnp.float32).astype(jnp.bfloat16)


def expand(folds, slot, masks, upper, lower):
    tiles = upper.shape[0]
    lane = lax.broadcasted_iota(jnp.int32, (1, LANES), 1)
    eighth = folds[slot, (tiles - 1) * PACKED : (tiles - 1) * PACKED + BLOCK, :]
    last_row = eighth.astype(jnp.float32)[BLOCK - 1 :, :]
    last_row = jnp.where(lane >= PACKED, last_row, -float(LANES))
    first = jnp.max(last_row).astype(jnp.int32)
    for t in range(tiles):
        packed = folds[slot, t * PACKED : (t + 1) * PACKED, :]
        own = packed * masks[3, :PACKED, :]
        rest = packed - own
        eighth = [rest[b : b + BLOCK] for b in range(0, PACKED, BLOCK)]
        while len(eighth) > 1:
            eighth = [sum(eighth[i : i + 2][1:], eighth[i]) for i in range(0, len(eighth), 2)]
        run = jnp.concatenate([own, eighth[0]], axis=0)
        if t == tiles - 1:
            run = run * masks[2]
        near = run * masks[0]
        upper[t, :, :LANES] = near
        upper[t, :, LANES:] = run - near
        turned = run.T
        near = turned * masks[1]
        lower[t, :, :LANES] = near
        lower[(t + 1) % tiles, :, LANES:] = turned - near
    return first


def turn(parts, amount):
    step = 1
    while step < len(parts):
        moved = parts[step:] + parts[:step]
        there = amount & step != 0
        parts = [jnp.where(there, new, old) for new, old in zip(moved, parts)]
        step *= 2
    return parts


def banded_product(v, upper, lower, start):
    tiles = len(v)
    whole = start >> 3
    fine = (start & (BLOCKS_PER_LANES - 1)) * BLOCK
    lane = lax.broadcasted_iota(jnp.int32, v[0].shape, 1)
    turned = [pltpu.roll(part, (LANES - fine) & (LANES - 1), 1) for part in v]
    moved = turn(
        [
            jnp.where(lane < LANES - fine, turned[u], turned[(u + 1) % tiles])
            for u in range(tiles)
        ],
        whole,
    )
    first = [
        jnp.dot(v[t].astype(jnp.bfloat16), upper[t], preferred_element_type=jnp.float32)
        for t in range(tiles)
    ]
    second = [
        jnp.dot(moved[u].astype(jnp.bfloat16), lower[u], preferred_element_type=jnp.float32)
        for u in range(tiles)
    ]
    sums = [first[t][:, :LANES] + first[t - 1][:, LANES:] for t in range(tiles)]
    turned = [pltpu.roll(part, fine, 1) for part in sums]
    ahead = turn(
        [jnp.where(lane >= fine, turned[u], turned[u - 1]) for u in range(tiles)], -whole
    )
    return [
        ahead[u] - (second[u][:, :LANES] + second[(u + 1) % tiles][:, LANES:])
        for u in range(tiles)
    ]


def run_layer(x, sign, upper, lower, start):
    v = x
    for divisor in range(DEGREE, 0, -1):
        scale = sign * (1.0 / divisor)
        product = banded_product(v, upper, lower, start)
        v = [part + scale * term for part, term in zip(x, product)]
    return v


def cascade_first_kernel(distances, row_masks, *refs):
    pieces = []
    for count in distances[0]:
        pieces += [(refs[0], index) for index in range(count)]
        refs = refs[1:]
    others, refs = refs[: len(row_masks)], refs[len(row_masks) :]
    own, kept, upper, lower, starts, send, folds, masks, field = refs
    place(pieces, distances[1], folds)
    fill_masks(masks)
    place_field(own, list(zip(others, row_masks)), field)
    x = [field[u] for u in range(field.shape[0])]
    forward = lax.axis_index("layer") // GROUP == 0
    sign = jnp.where(forward, -1.0, 1.0)

    def prepare(k):
        slot = jnp.where(forward, k, GROUP - 1 - k)
        start = expand(folds, slot, masks, upper.at[k], lower.at[k])
        starts[k : k + 1, :] = jnp.full((1, LANES), start, jnp.int32)
        return start

    start = prepare(0)
    for k in range(GROUP):
        following = prepare(k + 1) if k + 1 < GROUP else None
        x = run_layer(x, sign, upper.at[k], lower.at[k], start)
        start = following
    mine = own_panel(x, kept.shape[-1])
    kept[0] = mine
    kept[1] = mine
    write_whole(x, send)


def cascade_next_kernel(step, groups, *refs):
    upper, lower, starts, field, before, kept, *send = refs
    panel = kept.shape[-1]
    group = lax.axis_index("layer") // GROUP
    forward = group == step
    backward = group == groups - 1 - step
    sign = jnp.where(forward, -1.0, 1.0)
    same_order = forward == (group == 0)
    x = field[...].astype(jnp.float32)
    x = [x[:, u : u + LANES] for u in range(0, x.shape[1], LANES)]

    order = [jnp.where(same_order, k, GROUP - 1 - k) for k in range(GROUP)]
    begin = [jnp.max(starts[pl.ds(at, 1), :]) for at in order]
    for at, start in zip(order, begin):
        x = run_layer(x, sign, upper.at[at], lower.at[at], start)
    mine = own_panel(x, panel)
    kept[0] = jnp.where(forward, mine, before[0])
    kept[1] = jnp.where(backward, mine, before[1])
    if send:
        write_whole(x, *send)


def write_whole(x, send):
    for u, part in enumerate(x):
        send[:, u * LANES : (u + 1) * LANES] = part.astype(jnp.bfloat16)


def own_panel(x, panel):
    row = lax.axis_index("row")
    tiles = panel // LANES
    mine = x[:tiles]
    for index in range(1, len(x) // tiles):
        there = x[index * tiles : (index + 1) * tiles]
        mine = [jnp.where(row == index, new, old) for new, old in zip(there, mine)]
    return jnp.concatenate(mine, axis=1)


def join_kernel(mine, theirs, *outs):
    core = lax.axis_index("layer") % CORES
    count = mine.shape[1]
    for kind, out in enumerate(outs):
        for part, at in ((mine, core), (theirs, 1 - core)):
            out[0, pl.ds(pl.multiple_of(at * count, count), count), :] = part[kind]


def join(mine, theirs):
    kinds, count, panel = mine.shape
    vmem = pl.BlockSpec(memory_space=pltpu.VMEM)
    return pl.pallas_call(
        join_kernel,
        out_shape=[jax.ShapeDtypeStruct((1, CORES * count, panel), mine.dtype)] * kinds,
        in_specs=[vmem] * 2,
        out_specs=[vmem] * kinds,
        compiler_params=pltpu.CompilerParams(vmem_limit_bytes=SMALL_GRANT),
        name="join",
    )(mine, theirs)


def run_first(batches, distances, others, row_masks, field, orders):
    count, panel = field.shape
    tiles = orders // LANES
    vmem = pl.BlockSpec(memory_space=pltpu.VMEM)
    window = jax.ShapeDtypeStruct((GROUP, tiles, LANES, 2 * LANES), jnp.bfloat16)
    return pl.pallas_call(
        functools.partial(cascade_first_kernel, distances, row_masks),
        out_shape=[
            jax.ShapeDtypeStruct((2, count, panel), jnp.float32),
            window,
            window,
            jax.ShapeDtypeStruct((GROUP, LANES), jnp.int32),
            jax.ShapeDtypeStruct((count, orders), jnp.bfloat16),
        ],
        in_specs=[vmem] * (len(batches) + len(others) + 1),
        out_specs=[vmem] * 5,
        scratch_shapes=[
            pltpu.VMEM((GROUP, tiles * PACKED, LANES), jnp.bfloat16),
            pltpu.VMEM((4, LANES, LANES), jnp.bfloat16),
            pltpu.VMEM((tiles, count, LANES), jnp.float32),
        ],
        compiler_params=pltpu.CompilerParams(vmem_limit_bytes=24 * 1024 * 1024),
        name="cascade_first",
    )(*batches, *others, field)


def run_next(step, groups, upper, lower, starts, field, kept):
    vmem = pl.BlockSpec(memory_space=pltpu.VMEM)
    out_shape = [jax.ShapeDtypeStruct(kept.shape, jnp.float32)]
    if step < groups - 1:
        out_shape.append(jax.ShapeDtypeStruct(field.shape, jnp.bfloat16))
    return pl.pallas_call(
        functools.partial(cascade_next_kernel, step, groups),
        out_shape=out_shape,
        in_specs=[vmem] * 5,
        out_specs=[vmem] * len(out_shape),
        compiler_params=pltpu.CompilerParams(vmem_limit_bytes=24 * 1024 * 1024),
        name=f"cascade_{step}",
    )(upper, lower, starts, field, kept)


def gather_batches(own, corner, across, rows):
    bits = [(0, 1 << b) for b in range(rows.bit_length() - 1)]
    bits += [(1 << b, 0) for b in range(1, GROUP.bit_length() - 1)]
    count = len(bits)

    def members(subset):
        return [b for b in range(count) if subset >> b & 1]

    def distance(subset):
        return tuple(
            tuple(sum(bits[(b + core) % count][axis] for b in members(subset)) for axis in (0, 1))
            for core in range(CORES)
        )

    subsets = sorted(range(1 << count), key=lambda m: (m.bit_count(), m))
    pieces = {0: own}
    for subset in subsets[1 : count + 1]:
        pieces[subset] = across(own, distance(subset))
    pieces[subsets[-1]] = across(corner, distance(subsets[-1]))
    for subset in subsets[count + 1 : -1]:
        which = members(subset)
        link = next((b for b in which if (b + 1) % count in which), which[0])
        pieces[subset] = across(pieces[subset ^ 1 << link], distance(1 << link))
    batches, counts, distances = [], [], []
    for part in (subsets[: count + 1], subsets[count + 1 :]):
        mine = batch([pieces[subset] for subset in part])
        batches += [mine, across(mine, ((1, 0), (1, 0)))]
        counts += [len(part), len(part)]
        distances += [distance(subset) for subset in part]
        distances += [
            tuple((a ^ 1, b) for a, b in options[::-1]) for options in distances[-len(part) :]
        ]
    return pieces[subsets[-1]], batches, (tuple(counts), tuple(distances))


def on_device(coupling, band_off, band_width, incident, cotangent):
    panel, orders = coupling.shape[1:]
    layers = lax.axis_size("layer")
    rows = lax.axis_size("row")
    groups = layers // GROUP

    def across(array, options):
        pairs = []
        for l in range(layers):
            layer_mask, row_mask = options[l % CORES]
            for r in range(rows):
                pairs.append((l * rows + r, (l ^ layer_mask) * rows + (r ^ row_mask)))
        return lax.ppermute(array, ("layer", "row"), pairs)

    folded = fold(coupling, band_off, band_width)
    layer = lax.axis_index("layer")
    share = incident.shape[0] // CORES
    folded, incident, cotangent = lax.optimization_barrier((folded, incident, cotangent))
    field = jnp.where(layer // GROUP == 0, incident, cotangent)
    field = lax.dynamic_slice_in_dim(field, layer % CORES * share, share)
    whole = corner(folded, field)
    from_corner, batches, distances = gather_batches(folded, whole, across, rows)
    others, row_masks = [from_corner], [rows - 1]
    for mask in range(1, rows - 1):
        others.append(across(whole, ((0, mask), (0, mask))))
        row_masks.append(mask)
    kept, upper, lower, starts, send = run_first(
        batches, distances, others, tuple(row_masks), field, orders
    )
    for step in range(1, groups):
        pairs = []
        for index in range(GROUP * rows):
            forward_from = (step - 1) * GROUP * rows + index
            adjoint_from = (groups - step) * GROUP * rows + index
            pairs.append((forward_from, forward_from + GROUP * rows))
            pairs.append((adjoint_from, adjoint_from - GROUP * rows))
        field = lax.ppermute(send, ("layer", "row"), pairs)
        kept, *send = run_next(step, groups, upper, lower, starts, field, kept)
        send = send[0] if send else None
    return tuple(join(kept, across(kept, ((1, 0), (1, 0)))))


def solution(mesh):
    in_specs = (P("layer", "row", None), P("layer"), P("layer"), P(None, "row"), P(None, "row"))
    out_specs = (P("layer", None, "row"), P("layer", None, "row"))
    return jax.shard_map(
        on_device, mesh=mesh, in_specs=in_specs, out_specs=out_specs, check_vma=False
    )
```

```python
import functools

import jax
import jax.numpy as jnp
from jax import lax
from jax.experimental import pallas as pl
from jax.experimental.pallas import tpu as pltpu
from jax.sharding import PartitionSpec as P

BLOCK = 16
GROUP = 8
LANES = 128
BLOCKS_PER_LANES = LANES // BLOCK
PACKED = LANES - BLOCK
DEGREE = 4
SMALL_GRANT = 4 * 1024 * 1024
CORES = 2


def fold_kernel(off_ref, width_ref, coupling_ref, folded_ref):
    rows, orders = coupling_ref.shape[1:]
    first = off_ref[0] - width_ref[0]
    last = off_ref[0] + width_ref[0]
    first_block = lax.axis_index("row") * (rows // BLOCK)
    lane = lax.broadcasted_iota(jnp.int32, (BLOCK, LANES), 1)
    sub = lax.broadcasted_iota(jnp.int32, (BLOCK, LANES), 0)
    top = orders // LANES - 1
    for local in range(rows // BLOCK):
        if local % BLOCKS_PER_LANES == 0:
            runs = []
        block = first_block + local
        start = (block + first) * BLOCK
        tile = start >> 7
        shift = start & (LANES - 1)
        here = slice(local * BLOCK, (local + 1) * BLOCK)

        def part(index):
            column = pl.multiple_of(jnp.clip(index, 0, top) * LANES, LANES)
            return coupling_ref[0, here, pl.ds(column, LANES)].astype(jnp.float32)

        near = lane >= shift
        column = jnp.where(near, lane, lane + LANES) + tile * LANES
        limit = jnp.minimum((block + last + 1) * BLOCK, orders)
        keep = (column > block * BLOCK + sub) & (column < limit)
        folded = jnp.where(keep, jnp.where(near, part(tile), part(tile + 1)), 0.0)
        is_last = block * BLOCK + sub == orders - 1
        folded = jnp.where(is_last, first.astype(jnp.float32), folded)
        runs.append(pltpu.roll(folded, (-first * BLOCK) & (LANES - 1), 1))
        if len(runs) == BLOCKS_PER_LANES:
            base = local * BLOCK // LANES * PACKED
            for b, run in enumerate(runs[:-1]):
                hole = lane // BLOCK == (b - 1) % BLOCKS_PER_LANES
                folded_ref[base + b * BLOCK : base + (b + 1) * BLOCK, :] = jnp.where(
                    hole, runs[-1], run
                ).astype(jnp.bfloat16)


def fold(coupling, band_off, band_width):
    rows, orders = coupling.shape[1:]
    smem = pl.BlockSpec(memory_space=pltpu.SMEM)
    vmem = pl.BlockSpec(memory_space=pltpu.VMEM)
    return pl.pallas_call(
        fold_kernel,
        out_shape=jax.ShapeDtypeStruct((rows // LANES * PACKED, LANES), jnp.bfloat16),
        in_specs=[smem, smem, vmem],
        out_specs=vmem,
        compiler_params=pltpu.CompilerParams(vmem_limit_bytes=SMALL_GRANT),
        name="fold",
    )(band_off, band_width, coupling)


def batch_kernel(*refs):
    rows = refs[-1].shape[1]
    for index, piece in enumerate(refs[:-1]):
        refs[-1][index] = piece[:rows, :]


def batch(pieces):
    vmem = pl.BlockSpec(memory_space=pltpu.VMEM)
    rows = min(piece.shape[0] for piece in pieces)
    return pl.pallas_call(
        batch_kernel,
        out_shape=jax.ShapeDtypeStruct((len(pieces), rows, LANES), pieces[0].dtype),
        in_specs=[vmem] * len(pieces),
        out_specs=vmem,
        compiler_params=pltpu.CompilerParams(vmem_limit_bytes=SMALL_GRANT),
        name="batch",
    )(*pieces)


def place(pieces, distances, folds):
    slot = lax.axis_index("layer") % GROUP
    row = lax.axis_index("row")
    rows = folds.shape[1] // lax.axis_size("row")
    for (ref, index), options in zip(pieces, distances):
        layer_mask, row_mask = by_core(options)
        here = pl.ds(pl.multiple_of((row ^ row_mask) * rows, BLOCK), rows)
        folds[slot ^ layer_mask, here, :] = ref[index, :rows, :]


def by_core(options):
    core = lax.axis_index("layer") % CORES
    return [jnp.where(core == 0, *pair) for pair in zip(*options)]


def place_field(own, others, field):
    row = lax.axis_index("row")
    tiles = own.shape[1] // LANES
    for part, row_mask in [(own, 0), *others]:
        for u in range(tiles):
            field[(row ^ row_mask) * tiles + u] = part[:, u * LANES : (u + 1) * LANES]


def fill_masks(masks):
    row = lax.broadcasted_iota(jnp.int32, (LANES, LANES), 0)
    lane = lax.broadcasted_iota(jnp.int32, (LANES, LANES), 1)
    masks[0] = (lane >= row // BLOCK * BLOCK).astype(jnp.float32).astype(jnp.bfloat16)
    masks[1] = (row >= lane // BLOCK * BLOCK).astype(jnp.float32).astype(jnp.bfloat16)
    masks[2] = (row < LANES - 1).astype(jnp.float32).astype(jnp.bfloat16)
    own = lane // BLOCK != (row // BLOCK + BLOCKS_PER_LANES - 1) % BLOCKS_PER_LANES
    masks[3] = own.astype(jnp.float32).astype(jnp.bfloat16)


def expand(folds, slot, masks, upper, lower):
    tiles = upper.shape[0]
    lane = lax.broadcasted_iota(jnp.int32, (1, LANES), 1)
    eighth = folds[slot, (tiles - 1) * PACKED : (tiles - 1) * PACKED + BLOCK, :]
    last_row = eighth.astype(jnp.float32)[BLOCK - 1 :, :]
    last_row = jnp.where(lane >= PACKED, last_row, -float(LANES))
    first = jnp.max(last_row).astype(jnp.int32)
    for t in range(tiles):
        packed = folds[slot, t * PACKED : (t + 1) * PACKED, :]
        own = packed * masks[3, :PACKED, :]
        rest = packed - own
        eighth = [rest[b : b + BLOCK] for b in range(0, PACKED, BLOCK)]
        while len(eighth) > 1:
            eighth = [sum(eighth[i : i + 2][1:], eighth[i]) for i in range(0, len(eighth), 2)]
        run = jnp.concatenate([own, eighth[0]], axis=0)
        if t == tiles - 1:
            run = run * masks[2]
        near = run * masks[0]
        upper[t, :, :LANES] = near
        upper[t, :, LANES:] = run - near
        turned = run.T
        near = turned * masks[1]
        lower[t, :, :LANES] = near
        lower[(t + 1) % tiles, :, LANES:] = turned - near
    return first


def turn(parts, amount):
    step = 1
    while step < len(parts):
        moved = parts[step:] + parts[:step]
        there = amount & step != 0
        parts = [jnp.where(there, new, old) for new, old in zip(moved, parts)]
        step *= 2
    return parts


def banded_product(v, upper, lower, start):
    tiles = len(v)
    whole = start >> 3
    fine = (start & (BLOCKS_PER_LANES - 1)) * BLOCK
    lane = lax.broadcasted_iota(jnp.int32, v[0].shape, 1)
    turned = [pltpu.roll(part, (LANES - fine) & (LANES - 1), 1) for part in v]
    moved = turn(
        [
            jnp.where(lane < LANES - fine, turned[u], turned[(u + 1) % tiles])
            for u in range(tiles)
        ],
        whole,
    )
    first = [
        jnp.dot(v[t].astype(jnp.bfloat16), upper[t], preferred_element_type=jnp.float32)
        for t in range(tiles)
    ]
    second = [
        jnp.dot(moved[u].astype(jnp.bfloat16), lower[u], preferred_element_type=jnp.float32)
        for u in range(tiles)
    ]
    sums = [first[t][:, :LANES] + first[t - 1][:, LANES:] for t in range(tiles)]
    turned = [pltpu.roll(part, fine, 1) for part in sums]
    ahead = turn(
        [jnp.where(lane >= fine, turned[u], turned[u - 1]) for u in range(tiles)], -whole
    )
    return [
        ahead[u] - (second[u][:, :LANES] + second[(u + 1) % tiles][:, LANES:])
        for u in range(tiles)
    ]


def run_layer(x, sign, upper, lower, start):
    v = x
    for divisor in range(DEGREE, 0, -1):
        scale = sign * (1.0 / divisor)
        product = banded_product(v, upper, lower, start)
        v = [part + scale * term for part, term in zip(x, product)]
    return v


def cascade_first_kernel(distances, shares, *refs):
    pieces = []
    for count in distances[0]:
        pieces += [(refs[0], index) for index in range(count)]
        refs = refs[1:]
    (own, *others), refs = refs[:shares], refs[shares:]
    kept, upper, lower, starts, send, folds, masks, field = refs
    place(pieces, distances[1], folds)
    fill_masks(masks)
    place_field(own, [(part, n + 1) for n, part in enumerate(others)], field)
    x = [field[u] for u in range(field.shape[0])]
    forward = lax.axis_index("layer") // GROUP == 0
    sign = jnp.where(forward, -1.0, 1.0)

    def prepare(k):
        slot = jnp.where(forward, k, GROUP - 1 - k)
        start = expand(folds, slot, masks, upper.at[k], lower.at[k])
        starts[k : k + 1, :] = jnp.full((1, LANES), start, jnp.int32)
        return start

    start = prepare(0)
    for k in range(GROUP):
        following = prepare(k + 1) if k + 1 < GROUP else None
        x = run_layer(x, sign, upper.at[k], lower.at[k], start)
        start = following
    mine = own_panel(x, kept.shape[-1])
    kept[0] = mine
    kept[1] = mine
    write_whole(x, send)


def cascade_next_kernel(step, groups, *refs):
    upper, lower, starts, field, before, kept, *send = refs
    panel = kept.shape[-1]
    group = lax.axis_index("layer") // GROUP
    forward = group == step
    backward = group == groups - 1 - step
    sign = jnp.where(forward, -1.0, 1.0)
    same_order = forward == (group == 0)
    x = field[...].astype(jnp.float32)
    x = [x[:, u : u + LANES] for u in range(0, x.shape[1], LANES)]

    order = [jnp.where(same_order, k, GROUP - 1 - k) for k in range(GROUP)]
    begin = [jnp.max(starts[pl.ds(at, 1), :]) for at in order]
    for at, start in zip(order, begin):
        x = run_layer(x, sign, upper.at[at], lower.at[at], start)
    mine = own_panel(x, panel)
    kept[0] = jnp.where(forward, mine, before[0])
    kept[1] = jnp.where(backward, mine, before[1])
    if send:
        write_whole(x, *send)


def write_whole(x, send):
    for u, part in enumerate(x):
        send[:, u * LANES : (u + 1) * LANES] = part.astype(jnp.bfloat16)


def own_panel(x, panel):
    row = lax.axis_index("row")
    tiles = panel // LANES
    mine = x[:tiles]
    for index in range(1, len(x) // tiles):
        there = x[index * tiles : (index + 1) * tiles]
        mine = [jnp.where(row == index, new, old) for new, old in zip(there, mine)]
    return jnp.concatenate(mine, axis=1)


def join_kernel(mine, theirs, *outs):
    core = lax.axis_index("layer") % CORES
    count = mine.shape[1]
    for kind, out in enumerate(outs):
        for part, at in ((mine, core), (theirs, 1 - core)):
            out[0, pl.ds(pl.multiple_of(at * count, count), count), :] = part[kind]


def join(mine, theirs):
    kinds, count, panel = mine.shape
    vmem = pl.BlockSpec(memory_space=pltpu.VMEM)
    return pl.pallas_call(
        join_kernel,
        out_shape=[jax.ShapeDtypeStruct((1, CORES * count, panel), mine.dtype)] * kinds,
        in_specs=[vmem] * 2,
        out_specs=[vmem] * kinds,
        compiler_params=pltpu.CompilerParams(vmem_limit_bytes=SMALL_GRANT),
        name="join",
    )(mine, theirs)


def run_first(batches, distances, fields, orders):
    count, panel = fields[0].shape
    tiles = orders // LANES
    vmem = pl.BlockSpec(memory_space=pltpu.VMEM)
    window = jax.ShapeDtypeStruct((GROUP, tiles, LANES, 2 * LANES), jnp.bfloat16)
    return pl.pallas_call(
        functools.partial(cascade_first_kernel, distances, len(fields)),
        out_shape=[
            jax.ShapeDtypeStruct((2, count, panel), jnp.float32),
            window,
            window,
            jax.ShapeDtypeStruct((GROUP, LANES), jnp.int32),
            jax.ShapeDtypeStruct((count, orders), jnp.bfloat16),
        ],
        in_specs=[vmem] * (len(batches) + len(fields)),
        out_specs=[vmem] * 5,
        scratch_shapes=[
            pltpu.VMEM((GROUP, tiles * PACKED, LANES), jnp.bfloat16),
            pltpu.VMEM((4, LANES, LANES), jnp.bfloat16),
            pltpu.VMEM((tiles, count, LANES), jnp.float32),
        ],
        compiler_params=pltpu.CompilerParams(vmem_limit_bytes=24 * 1024 * 1024),
        name="cascade_first",
    )(*batches, *fields)


def run_next(step, groups, upper, lower, starts, field, kept):
    vmem = pl.BlockSpec(memory_space=pltpu.VMEM)
    out_shape = [jax.ShapeDtypeStruct(kept.shape, jnp.float32)]
    if step < groups - 1:
        out_shape.append(jax.ShapeDtypeStruct(field.shape, jnp.bfloat16))
    return pl.pallas_call(
        functools.partial(cascade_next_kernel, step, groups),
        out_shape=out_shape,
        in_specs=[vmem] * 5,
        out_specs=[vmem] * len(out_shape),
        compiler_params=pltpu.CompilerParams(vmem_limit_bytes=24 * 1024 * 1024),
        name=f"cascade_{step}",
    )(upper, lower, starts, field, kept)


def gather_batches(own, start_fields, across, rows):
    bits = [(0, 1 << b) for b in range(rows.bit_length() - 1)]
    bits += [(1 << b, 0) for b in range(1, GROUP.bit_length() - 1)]
    count = len(bits)

    def members(subset):
        return [b for b in range(count) if subset >> b & 1]

    def distance(subset):
        return tuple(
            tuple(sum(bits[(b + core) % count][axis] for b in members(subset)) for axis in (0, 1))
            for core in range(CORES)
        )

    subsets = sorted(range(1 << count), key=lambda m: (m.bit_count(), m))
    pieces = {0: own}
    for subset in subsets[1 : count + 1] + subsets[-1:]:
        pieces[subset] = across(own, distance(subset))
    for subset in subsets[count + 1 : -1]:
        which = members(subset)
        link = next((b for b in which if (b + 1) % count in which), which[0])
        pieces[subset] = across(pieces[subset ^ 1 << link], distance(1 << link))
    batches, counts, distances = [], [], []
    pieces[subsets[count]], fields = start_fields(pieces[subsets[count]])
    fields, pieces[subsets[-1]] = lax.optimization_barrier((fields, pieces[subsets[-1]]))
    for part in (subsets[: count + 1], subsets[count + 1 :]):
        mine = batch([pieces[subset] for subset in part])
        batches += [mine, across(mine, ((1, 0), (1, 0)))]
        counts += [len(part), len(part)]
        distances += [distance(subset) for subset in part]
        distances += [
            tuple((a ^ 1, b) for a, b in options[::-1]) for options in distances[-len(part) :]
        ]
    return fields, batches, (tuple(counts), tuple(distances))


def on_device(coupling, band_off, band_width, incident, cotangent):
    panel, orders = coupling.shape[1:]
    layers = lax.axis_size("layer")
    rows = lax.axis_size("row")
    groups = layers // GROUP

    def across(array, options):
        pairs = []
        for l in range(layers):
            layer_mask, row_mask = options[l % CORES]
            for r in range(rows):
                pairs.append((l * rows + r, (l ^ layer_mask) * rows + (r ^ row_mask)))
        return lax.ppermute(array, ("layer", "row"), pairs)

    folded = fold(coupling, band_off, band_width)
    layer = lax.axis_index("layer")
    share = incident.shape[0] // CORES

    def start_fields(after):
        after, first, last = lax.optimization_barrier((after, incident, cotangent))
        layer = lax.axis_index("layer")
        share = incident.shape[0] // CORES
        own = jnp.where(layer // GROUP == 0, first, last)
        own = lax.dynamic_slice_in_dim(own, layer % CORES * share, share)
        return after, [own] + [across(own, ((0, m), (0, m))) for m in range(1, rows)]

    fields, batches, distances = gather_batches(folded, start_fields, across, rows)
    kept, upper, lower, starts, send = run_first(batches, distances, fields, orders)
    for step in range(1, groups):
        pairs = []
        for index in range(GROUP * rows):
            forward_from = (step - 1) * GROUP * rows + index
            adjoint_from = (groups - step) * GROUP * rows + index
            pairs.append((forward_from, forward_from + GROUP * rows))
            pairs.append((adjoint_from, adjoint_from - GROUP * rows))
        field = lax.ppermute(send, ("layer", "row"), pairs)
        kept, *send = run_next(step, groups, upper, lower, starts, field, kept)
        send = send[0] if send else None
    return tuple(join(kept, across(kept, ((1, 0), (1, 0)))))


def solution(mesh):
    in_specs = (P("layer", "row", None), P("layer"), P("layer"), P(None, "row"), P(None, "row"))
    out_specs = (P("layer", None, "row"), P("layer", None, "row"))
    return jax.shard_map(
        on_device, mesh=mesh, in_specs=in_specs, out_specs=out_specs, check_vma=False
    )
```

```python
import functools

import jax
import jax.numpy as jnp
from jax import lax
from jax.experimental import pallas as pl
from jax.experimental.pallas import tpu as pltpu
from jax.sharding import PartitionSpec as P

BLOCK = 16
GROUP = 8
LANES = 128
BLOCKS_PER_LANES = LANES // BLOCK
PACKED = LANES - BLOCK
DEGREE = 4
GROUP_ROWS = 32
SMALL_GRANT = 4 * 1024 * 1024
CORES = 2


def fold_kernel(off_ref, width_ref, coupling_ref, folded_ref):
    rows, orders = coupling_ref.shape[1:]
    first = off_ref[0] - width_ref[0]
    last = off_ref[0] + width_ref[0]
    first_block = lax.axis_index("row") * (rows // BLOCK)
    lane = lax.broadcasted_iota(jnp.int32, (BLOCK, LANES), 1)
    sub = lax.broadcasted_iota(jnp.int32, (BLOCK, LANES), 0)
    top = orders // LANES - 1
    for local in range(rows // BLOCK):
        if local % BLOCKS_PER_LANES == 0:
            runs = []
        block = first_block + local
        start = (block + first) * BLOCK
        tile = start >> 7
        shift = start & (LANES - 1)
        here = slice(local * BLOCK, (local + 1) * BLOCK)

        def part(index):
            column = pl.multiple_of(jnp.clip(index, 0, top) * LANES, LANES)
            return coupling_ref[0, here, pl.ds(column, LANES)].astype(jnp.float32)

        near = lane >= shift
        column = jnp.where(near, lane, lane + LANES) + tile * LANES
        limit = jnp.minimum((block + last + 1) * BLOCK, orders)
        keep = (column > block * BLOCK + sub) & (column < limit)
        folded = jnp.where(keep, jnp.where(near, part(tile), part(tile + 1)), 0.0)
        is_last = block * BLOCK + sub == orders - 1
        folded = jnp.where(is_last, first.astype(jnp.float32), folded)
        runs.append(pltpu.roll(folded, (-first * BLOCK) & (LANES - 1), 1))
        if len(runs) == BLOCKS_PER_LANES:
            base = local * BLOCK // LANES * PACKED
            for b, run in enumerate(runs[:-1]):
                hole = lane // BLOCK == (b - 1) % BLOCKS_PER_LANES
                folded_ref[base + b * BLOCK : base + (b + 1) * BLOCK, :] = jnp.where(
                    hole, runs[-1], run
                ).astype(jnp.bfloat16)


def fold(coupling, band_off, band_width):
    rows, orders = coupling.shape[1:]
    smem = pl.BlockSpec(memory_space=pltpu.SMEM)
    vmem = pl.BlockSpec(memory_space=pltpu.VMEM)
    return pl.pallas_call(
        fold_kernel,
        out_shape=jax.ShapeDtypeStruct((rows // LANES * PACKED, LANES), jnp.bfloat16),
        in_specs=[smem, smem, vmem],
        out_specs=vmem,
        compiler_params=pltpu.CompilerParams(vmem_limit_bytes=SMALL_GRANT),
        name="fold",
    )(band_off, band_width, coupling)


def batch_kernel(*refs):
    rows = refs[-1].shape[1]
    for index, piece in enumerate(refs[:-1]):
        refs[-1][index] = piece[:rows, :]


def batch(pieces):
    vmem = pl.BlockSpec(memory_space=pltpu.VMEM)
    rows = min(piece.shape[0] for piece in pieces)
    return pl.pallas_call(
        batch_kernel,
        out_shape=jax.ShapeDtypeStruct((len(pieces), rows, LANES), pieces[0].dtype),
        in_specs=[vmem] * len(pieces),
        out_specs=vmem,
        compiler_params=pltpu.CompilerParams(vmem_limit_bytes=SMALL_GRANT),
        name="batch",
    )(*pieces)


def corner_kernel(folded, field, out):
    rows, panel = folded.shape[0], field.shape[1]
    count = field.shape[0]
    out[:rows, :] = folded[...]
    for u in range(panel // LANES):
        here = slice(rows + u * count, rows + (u + 1) * count)
        out[here, :] = field[:, u * LANES : (u + 1) * LANES].astype(jnp.bfloat16)


def corner(folded, field):
    vmem = pl.BlockSpec(memory_space=pltpu.VMEM)
    extra = field.size // LANES
    return pl.pallas_call(
        corner_kernel,
        out_shape=jax.ShapeDtypeStruct((folded.shape[0] + extra, LANES), folded.dtype),
        in_specs=[vmem] * 2,
        out_specs=vmem,
        compiler_params=pltpu.CompilerParams(vmem_limit_bytes=SMALL_GRANT),
        name="corner",
    )(folded, field)


def place(pieces, distances, folds):
    slot = lax.axis_index("layer") % GROUP
    row = lax.axis_index("row")
    rows = folds.shape[1] // lax.axis_size("row")
    for (ref, index), options in zip(pieces, distances):
        layer_mask, row_mask = by_core(options)
        here = pl.ds(pl.multiple_of((row ^ row_mask) * rows, BLOCK), rows)
        folds[slot ^ layer_mask, here, :] = ref[index, :rows, :]


def by_core(options):
    core = lax.axis_index("layer") % CORES
    return [jnp.where(core == 0, *pair) for pair in zip(*options)]


def place_field(own, others, field):
    row = lax.axis_index("row")
    count, panel = own.shape
    tiles = panel // LANES
    for u in range(tiles):
        field[row * tiles + u] = own[:, u * LANES : (u + 1) * LANES]
    for piece, row_mask in others:
        first = piece.shape[0] - tiles * count
        for u in range(tiles):
            here = slice(first + u * count, first + (u + 1) * count)
            field[(row ^ row_mask) * tiles + u] = piece[here, :].astype(jnp.float32)


def fill_masks(masks):
    row = lax.broadcasted_iota(jnp.int32, (LANES, LANES), 0)
    lane = lax.broadcasted_iota(jnp.int32, (LANES, LANES), 1)
    masks[0] = (row < LANES - 1).astype(jnp.float32).astype(jnp.bfloat16)
    own = lane // BLOCK != (row // BLOCK + BLOCKS_PER_LANES - 1) % BLOCKS_PER_LANES
    masks[1] = own.astype(jnp.float32).astype(jnp.bfloat16)
    masks[2] = (row >= lane // BLOCK * BLOCK).astype(jnp.float32).astype(jnp.bfloat16)


def expand(folds, slot, masks, both):
    tiles = both.shape[0] // LANES
    lane = lax.broadcasted_iota(jnp.int32, (1, LANES), 1)
    eighth = folds[slot, (tiles - 1) * PACKED : (tiles - 1) * PACKED + BLOCK, :]
    last_row = eighth.astype(jnp.float32)[BLOCK - 1 :, :]
    last_row = jnp.where(lane >= PACKED, last_row, -float(LANES))
    first = jnp.max(last_row).astype(jnp.int32)
    near, far = [], []
    for t in range(tiles):
        packed = folds[slot, t * PACKED : (t + 1) * PACKED, :]
        own = packed * masks[1, :PACKED, :]
        rest = packed - own
        eighth = [rest[b : b + BLOCK] for b in range(0, PACKED, BLOCK)]
        while len(eighth) > 1:
            eighth = [sum(eighth[i : i + 2][1:], eighth[i]) for i in range(0, len(eighth), 2)]
        run = jnp.concatenate([own, eighth[0]], axis=0)
        if t == tiles - 1:
            run = run * masks[0]
        both[t * LANES : (t + 1) * LANES, :LANES] = run
        turned = run.T
        near.append(turned * masks[2])
        far.append(turned - near[-1])
    for t in range(tiles):
        turned = (near[t] + far[t - 1]).astype(jnp.float32)
        turned = pltpu.roll(turned, first * BLOCK & (LANES - 1), 1).astype(jnp.bfloat16)
        for b in range(BLOCKS_PER_LANES):
            at = (t * BLOCKS_PER_LANES + b + first) & (tiles * BLOCKS_PER_LANES - 1)
            here = pl.ds(pl.multiple_of(at * BLOCK, BLOCK), BLOCK)
            both[here, LANES:] = turned[b * BLOCK : (b + 1) * BLOCK]
    return first


def turn(parts, amount):
    step = 1
    while step < len(parts):
        moved = parts[step:] + parts[:step]
        there = amount & step != 0
        parts = [jnp.where(there, new, old) for new, old in zip(moved, parts)]
        step *= 2
    return parts


def banded_product(v, both, start):
    tiles, fields = len(v), v[0].shape[0]
    whole = start >> 3
    fine = (start & (BLOCKS_PER_LANES - 1)) * BLOCK
    lane = lax.broadcasted_iota(jnp.int32, v[0].shape, 1)
    groups = LANES // GROUP_ROWS
    keeps = [
        (lane >= c * GROUP_ROWS).astype(jnp.float32).astype(jnp.bfloat16)
        for c in range(1, groups)
    ]
    upper, lower = [[None] * tiles for _ in range(2)], [[None] * tiles for _ in range(2)]
    for t in range(tiles):
        part = v[t].astype(jnp.bfloat16)
        spread = jnp.concatenate([part] + [part * keep for keep in keeps], axis=0)
        product = jnp.dot(
            spread,
            both[t * LANES : (t + 1) * LANES, :],
            preferred_element_type=jnp.float32,
        )
        sums = [product[c * fields : (c + 1) * fields] for c in range(groups)]
        following = jnp.zeros_like(v[t])
        same = sums[-1][:, LANES:]
        for c in range(groups - 2, -1, -1):
            here = lane < (c + 1) * GROUP_ROWS
            following = jnp.where(here, sums[c + 1][:, :LANES], following)
            same = jnp.where(here, sums[c][:, LANES:], same)
        upper[0][t], upper[1][t] = sums[0][:, :LANES] - following, following
        lower[0][t], lower[1][t] = same, sums[0][:, LANES:] - same
    turned = [pltpu.roll(upper[0][t] + upper[1][t - 1], fine, 1) for t in range(tiles)]
    ahead = turn(
        [jnp.where(lane >= fine, turned[t], turned[t - 1]) for t in range(tiles)], -whole
    )
    back = (LANES - fine) & (LANES - 1)
    turned = [
        pltpu.roll(lower[0][t] + lower[1][(t + 1) % tiles], back, 1) for t in range(tiles)
    ]
    behind = turn(
        [
            jnp.where(lane < LANES - fine, turned[t], turned[(t + 1) % tiles])
            for t in range(tiles)
        ],
        whole,
    )
    return [a - b for a, b in zip(ahead, behind)]


def run_layer(x, sign, both, start):
    v = x
    for divisor in range(DEGREE, 0, -1):
        scale = sign * (1.0 / divisor)
        product = banded_product(v, both, start)
        v = [part + scale * term for part, term in zip(x, product)]
    return v


def cascade_first_kernel(distances, row_masks, *refs):
    pieces = []
    for count in distances[0]:
        pieces += [(refs[0], index) for index in range(count)]
        refs = refs[1:]
    others, refs = refs[: len(row_masks)], refs[len(row_masks) :]
    own, kept, both, starts, send, folds, masks, field = refs
    place(pieces, distances[1], folds)
    fill_masks(masks)
    place_field(own, list(zip(others, row_masks)), field)
    x = [field[u] for u in range(field.shape[0])]
    forward = lax.axis_index("layer") // GROUP == 0
    sign = jnp.where(forward, -1.0, 1.0)

    def prepare(k):
        slot = jnp.where(forward, k, GROUP - 1 - k)
        start = expand(folds, slot, masks, both.at[k])
        starts[k : k + 1, :] = jnp.full((1, LANES), start, jnp.int32)
        return start

    start = prepare(0)
    for k in range(GROUP):
        following = prepare(k + 1) if k + 1 < GROUP else None
        x = run_layer(x, sign, both.at[k], start)
        start = following
    mine = own_panel(x, kept.shape[-1])
    kept[0] = mine
    kept[1] = mine
    write_whole(x, send)


def cascade_next_kernel(step, groups, *refs):
    both, starts, field, before, kept, *send = refs
    panel = kept.shape[-1]
    group = lax.axis_index("layer") // GROUP
    forward = group == step
    backward = group == groups - 1 - step
    sign = jnp.where(forward, -1.0, 1.0)
    same_order = forward == (group == 0)
    x = field[...].astype(jnp.float32)
    x = [x[:, u : u + LANES] for u in range(0, x.shape[1], LANES)]

    order = [jnp.where(same_order, k, GROUP - 1 - k) for k in range(GROUP)]
    begin = [jnp.max(starts[pl.ds(at, 1), :]) for at in order]
    for at, start in zip(order, begin):
        x = run_layer(x, sign, both.at[at], start)
    mine = own_panel(x, panel)
    kept[0] = jnp.where(forward, mine, before[0])
    kept[1] = jnp.where(backward, mine, before[1])
    if send:
        write_whole(x, *send)


def write_whole(x, send):
    for u, part in enumerate(x):
        send[:, u * LANES : (u + 1) * LANES] = part.astype(jnp.bfloat16)


def own_panel(x, panel):
    row = lax.axis_index("row")
    tiles = panel // LANES
    mine = x[:tiles]
    for index in range(1, len(x) // tiles):
        there = x[index * tiles : (index + 1) * tiles]
        mine = [jnp.where(row == index, new, old) for new, old in zip(there, mine)]
    return jnp.concatenate(mine, axis=1)


def join_kernel(mine, theirs, *outs):
    core = lax.axis_index("layer") % CORES
    count = mine.shape[1]
    for kind, out in enumerate(outs):
        for part, at in ((mine, core), (theirs, 1 - core)):
            out[0, pl.ds(pl.multiple_of(at * count, count), count), :] = part[kind]


def join(mine, theirs):
    kinds, count, panel = mine.shape
    vmem = pl.BlockSpec(memory_space=pltpu.VMEM)
    return pl.pallas_call(
        join_kernel,
        out_shape=[jax.ShapeDtypeStruct((1, CORES * count, panel), mine.dtype)] * kinds,
        in_specs=[vmem] * 2,
        out_specs=[vmem] * kinds,
        compiler_params=pltpu.CompilerParams(vmem_limit_bytes=SMALL_GRANT),
        name="join",
    )(mine, theirs)


def run_first(batches, distances, others, row_masks, field, orders):
    count, panel = field.shape
    tiles = orders // LANES
    vmem = pl.BlockSpec(memory_space=pltpu.VMEM)
    return pl.pallas_call(
        functools.partial(cascade_first_kernel, distances, row_masks),
        out_shape=[
            jax.ShapeDtypeStruct((2, count, panel), jnp.float32),
            jax.ShapeDtypeStruct((GROUP, orders, 2 * LANES), jnp.bfloat16),
            jax.ShapeDtypeStruct((GROUP, LANES), jnp.int32),
            jax.ShapeDtypeStruct((count, orders), jnp.bfloat16),
        ],
        in_specs=[vmem] * (len(batches) + len(others) + 1),
        out_specs=[vmem] * 4,
        scratch_shapes=[
            pltpu.VMEM((GROUP, tiles * PACKED, LANES), jnp.bfloat16),
            pltpu.VMEM((3, LANES, LANES), jnp.bfloat16),
            pltpu.VMEM((tiles, count, LANES), jnp.float32),
        ],
        compiler_params=pltpu.CompilerParams(vmem_limit_bytes=24 * 1024 * 1024),
        name="cascade_first",
    )(*batches, *others, field)


def run_next(step, groups, both, starts, field, kept):
    vmem = pl.BlockSpec(memory_space=pltpu.VMEM)
    out_shape = [jax.ShapeDtypeStruct(kept.shape, jnp.float32)]
    if step < groups - 1:
        out_shape.append(jax.ShapeDtypeStruct(field.shape, jnp.bfloat16))
    return pl.pallas_call(
        functools.partial(cascade_next_kernel, step, groups),
        out_shape=out_shape,
        in_specs=[vmem] * 4,
        out_specs=[vmem] * len(out_shape),
        compiler_params=pltpu.CompilerParams(vmem_limit_bytes=24 * 1024 * 1024),
        name=f"cascade_{step}",
    )(both, starts, field, kept)


def gather_batches(own, corner, across, rows):
    bits = [(0, 1 << b) for b in range(rows.bit_length() - 1)]
    bits += [(1 << b, 0) for b in range(1, GROUP.bit_length() - 1)]
    count = len(bits)

    def members(subset):
        return [b for b in range(count) if subset >> b & 1]

    def distance(subset):
        return tuple(
            tuple(sum(bits[(b + core) % count][axis] for b in members(subset)) for axis in (0, 1))
            for core in range(CORES)
        )

    subsets = sorted(range(1 << count), key=lambda m: (m.bit_count(), m))
    pieces = {0: own}
    for subset in subsets[1 : count + 1]:
        pieces[subset] = across(own, distance(subset))
    pieces[subsets[-1]] = across(corner, distance(subsets[-1]))
    for subset in subsets[count + 1 : -1]:
        which = members(subset)
        link = next((b for b in which if (b + 1) % count in which), which[0])
        pieces[subset] = across(pieces[subset ^ 1 << link], distance(1 << link))
    batches, counts, distances = [], [], []
    for part in (subsets[: count + 1], subsets[count + 1 :]):
        mine = batch([pieces[subset] for subset in part])
        batches += [mine, across(mine, ((1, 0), (1, 0)))]
        counts += [len(part), len(part)]
        distances += [distance(subset) for subset in part]
        distances += [
            tuple((a ^ 1, b) for a, b in options[::-1]) for options in distances[-len(part) :]
        ]
    return pieces[subsets[-1]], batches, (tuple(counts), tuple(distances))


def on_device(coupling, band_off, band_width, incident, cotangent):
    panel, orders = coupling.shape[1:]
    layers = lax.axis_size("layer")
    rows = lax.axis_size("row")
    groups = layers // GROUP

    def across(array, options):
        pairs = []
        for l in range(layers):
            layer_mask, row_mask = options[l % CORES]
            for r in range(rows):
                pairs.append((l * rows + r, (l ^ layer_mask) * rows + (r ^ row_mask)))
        return lax.ppermute(array, ("layer", "row"), pairs)

    folded = fold(coupling, band_off, band_width)
    layer = lax.axis_index("layer")
    share = incident.shape[0] // CORES
    folded, incident, cotangent = lax.optimization_barrier((folded, incident, cotangent))
    field = jnp.where(layer // GROUP == 0, incident, cotangent)
    field = lax.dynamic_slice_in_dim(field, layer % CORES * share, share)
    whole = corner(folded, field)
    from_corner, batches, distances = gather_batches(folded, whole, across, rows)
    others, row_masks = [from_corner], [rows - 1]
    for mask in range(1, rows - 1):
        others.append(across(whole, ((0, mask), (0, mask))))
        row_masks.append(mask)
    kept, both, starts, send = run_first(
        batches, distances, others, tuple(row_masks), field, orders
    )
    for step in range(1, groups):
        pairs = []
        for index in range(GROUP * rows):
            forward_from = (step - 1) * GROUP * rows + index
            adjoint_from = (groups - step) * GROUP * rows + index
            pairs.append((forward_from, forward_from + GROUP * rows))
            pairs.append((adjoint_from, adjoint_from - GROUP * rows))
        field = lax.ppermute(send, ("layer", "row"), pairs)
        kept, *send = run_next(step, groups, both, starts, field, kept)
        send = send[0] if send else None
    return tuple(join(kept, across(kept, ((1, 0), (1, 0)))))


def solution(mesh):
    in_specs = (P("layer", "row", None), P("layer"), P("layer"), P(None, "row"), P(None, "row"))
    out_specs = (P("layer", None, "row"), P("layer", None, "row"))
    return jax.shard_map(
        on_device, mesh=mesh, in_specs=in_specs, out_specs=out_specs, check_vma=False
    )
```

```python
import functools

import jax
import jax.numpy as jnp
from jax import lax
from jax.experimental import pallas as pl
from jax.experimental.pallas import tpu as pltpu
from jax.sharding import PartitionSpec as P

BLOCK = 16
GROUP = 8
LANES = 128
BLOCKS_PER_LANES = LANES // BLOCK
PACKED = LANES - BLOCK
DEGREE = 4
SMALL_GRANT = 4 * 1024 * 1024
CORES = 2


def fold_kernel(off_ref, width_ref, coupling_ref, folded_ref):
    rows, orders = coupling_ref.shape[1:]
    first = off_ref[0] - width_ref[0]
    last = off_ref[0] + width_ref[0]
    first_block = lax.axis_index("row") * (rows // BLOCK)
    lane = lax.broadcasted_iota(jnp.int32, (BLOCK, LANES), 1)
    sub = lax.broadcasted_iota(jnp.int32, (BLOCK, LANES), 0)
    top = orders // LANES - 1
    for local in range(rows // BLOCK):
        if local % BLOCKS_PER_LANES == 0:
            runs = []
        block = first_block + local
        start = (block + first) * BLOCK
        tile = start >> 7
        shift = start & (LANES - 1)
        here = slice(local * BLOCK, (local + 1) * BLOCK)

        def part(index):
            column = pl.multiple_of(jnp.clip(index, 0, top) * LANES, LANES)
            return coupling_ref[0, here, pl.ds(column, LANES)].astype(jnp.float32)

        near = lane >= shift
        column = jnp.where(near, lane, lane + LANES) + tile * LANES
        limit = jnp.minimum((block + last + 1) * BLOCK, orders)
        keep = (column > block * BLOCK + sub) & (column < limit)
        folded = jnp.where(keep, jnp.where(near, part(tile), part(tile + 1)), 0.0)
        is_last = block * BLOCK + sub == orders - 1
        folded = jnp.where(is_last, first.astype(jnp.float32), folded)
        runs.append(pltpu.roll(folded, (-first * BLOCK) & (LANES - 1), 1))
        if len(runs) == BLOCKS_PER_LANES:
            base = local * BLOCK // LANES * PACKED
            for b, run in enumerate(runs[:-1]):
                hole = lane // BLOCK == (b - 1) % BLOCKS_PER_LANES
                folded_ref[base + b * BLOCK : base + (b + 1) * BLOCK, :] = jnp.where(
                    hole, runs[-1], run
                ).astype(jnp.bfloat16)


def fold(coupling, band_off, band_width):
    rows, orders = coupling.shape[1:]
    smem = pl.BlockSpec(memory_space=pltpu.SMEM)
    vmem = pl.BlockSpec(memory_space=pltpu.VMEM)
    return pl.pallas_call(
        fold_kernel,
        out_shape=jax.ShapeDtypeStruct((rows // LANES * PACKED, LANES), jnp.bfloat16),
        in_specs=[smem, smem, vmem],
        out_specs=vmem,
        compiler_params=pltpu.CompilerParams(vmem_limit_bytes=SMALL_GRANT),
        name="fold",
    )(band_off, band_width, coupling)


def batch_kernel(*refs):
    rows = refs[-1].shape[1]
    for index, piece in enumerate(refs[:-1]):
        refs[-1][index] = piece[:rows, :]


def batch(pieces):
    vmem = pl.BlockSpec(memory_space=pltpu.VMEM)
    rows = min(piece.shape[0] for piece in pieces)
    return pl.pallas_call(
        batch_kernel,
        out_shape=jax.ShapeDtypeStruct((len(pieces), rows, LANES), pieces[0].dtype),
        in_specs=[vmem] * len(pieces),
        out_specs=vmem,
        compiler_params=pltpu.CompilerParams(vmem_limit_bytes=SMALL_GRANT),
        name="batch",
    )(*pieces)


def corner_kernel(folded, field, out):
    rows, panel = folded.shape[0], field.shape[1]
    count = field.shape[0]
    out[:rows, :] = folded[...]
    for u in range(panel // LANES):
        here = slice(rows + u * count, rows + (u + 1) * count)
        out[here, :] = field[:, u * LANES : (u + 1) * LANES].astype(jnp.bfloat16)


def corner(folded, field):
    vmem = pl.BlockSpec(memory_space=pltpu.VMEM)
    extra = field.size // LANES
    return pl.pallas_call(
        corner_kernel,
        out_shape=jax.ShapeDtypeStruct((folded.shape[0] + extra, LANES), folded.dtype),
        in_specs=[vmem] * 2,
        out_specs=vmem,
        compiler_params=pltpu.CompilerParams(vmem_limit_bytes=SMALL_GRANT),
        name="corner",
    )(folded, field)


def place(pieces, distances, folds):
    slot = lax.axis_index("layer") % GROUP
    row = lax.axis_index("row")
    rows = folds.shape[1] // lax.axis_size("row")
    for (ref, index), options in zip(pieces, distances):
        layer_mask, row_mask = by_core(options)
        here = pl.ds(pl.multiple_of((row ^ row_mask) * rows, BLOCK), rows)
        folds[slot ^ layer_mask, here, :] = ref[index, :rows, :]


def by_core(options):
    core = lax.axis_index("layer") % CORES
    return [jnp.where(core == 0, *pair) for pair in zip(*options)]


def place_field(own, others, field):
    row = lax.axis_index("row")
    count, panel = own.shape
    tiles = panel // LANES
    for u in range(tiles):
        field[row * tiles + u] = own[:, u * LANES : (u + 1) * LANES]
    for piece, row_mask in others:
        first = piece.shape[0] - tiles * count
        for u in range(tiles):
            here = slice(first + u * count, first + (u + 1) * count)
            field[(row ^ row_mask) * tiles + u] = piece[here, :].astype(jnp.float32)


def fill_masks(masks):
    row = lax.broadcasted_iota(jnp.int32, (LANES, LANES), 0)
    lane = lax.broadcasted_iota(jnp.int32, (LANES, LANES), 1)
    masks[0] = (lane >= row // BLOCK * BLOCK).astype(jnp.float32).astype(jnp.bfloat16)
    masks[1] = (row >= lane // BLOCK * BLOCK).astype(jnp.float32).astype(jnp.bfloat16)
    masks[2] = (row < LANES - 1).astype(jnp.float32).astype(jnp.bfloat16)
    own = lane // BLOCK != (row // BLOCK + BLOCKS_PER_LANES - 1) % BLOCKS_PER_LANES
    masks[3] = own.astype(jnp.float32).astype(jnp.bfloat16)


def expand(folds, slot, masks, upper, lower):
    tiles = upper.shape[0]
    lane = lax.broadcasted_iota(jnp.int32, (1, LANES), 1)
    eighth = folds[slot, (tiles - 1) * PACKED : (tiles - 1) * PACKED + BLOCK, :]
    last_row = eighth.astype(jnp.float32)[BLOCK - 1 :, :]
    last_row = jnp.where(lane >= PACKED, last_row, -float(LANES))
    first = jnp.max(last_row).astype(jnp.int32)
    for t in range(tiles):
        packed = folds[slot, t * PACKED : (t + 1) * PACKED, :]
        own = packed * masks[3, :PACKED, :]
        rest = packed - own
        eighth = [rest[b : b + BLOCK] for b in range(0, PACKED, BLOCK)]
        while len(eighth) > 1:
            eighth = [sum(eighth[i : i + 2][1:], eighth[i]) for i in range(0, len(eighth), 2)]
        run = jnp.concatenate([own, eighth[0]], axis=0)
        if t == tiles - 1:
            run = run * masks[2]
        near = run * masks[0]
        upper[t, :, :LANES] = near
        upper[t, :, LANES:] = run - near
        turned = run.T
        near = turned * masks[1]
        lower[t, :, :LANES] = near
        lower[(t + 1) % tiles, :, LANES:] = turned - near
    return first


def turn(parts, amount):
    step = 1
    while step < len(parts):
        moved = parts[step:] + parts[:step]
        there = amount & step != 0
        parts = [jnp.where(there, new, old) for new, old in zip(moved, parts)]
        step *= 2
    return parts


def banded_product(v, upper, lower, start):
    tiles = len(v)
    whole = start >> 3
    fine = (start & (BLOCKS_PER_LANES - 1)) * BLOCK
    lane = lax.broadcasted_iota(jnp.int32, v[0].shape, 1)
    turned = [pltpu.roll(part, (LANES - fine) & (LANES - 1), 1) for part in v]
    moved = turn(
        [
            jnp.where(lane < LANES - fine, turned[u], turned[(u + 1) % tiles])
            for u in range(tiles)
        ],
        whole,
    )
    first = [
        jnp.dot(v[t].astype(jnp.bfloat16), upper[t], preferred_element_type=jnp.float32)
        for t in range(tiles)
    ]
    second = [
        jnp.dot(moved[u].astype(jnp.bfloat16), lower[u], preferred_element_type=jnp.float32)
        for u in range(tiles)
    ]
    sums = [first[t][:, :LANES] + first[t - 1][:, LANES:] for t in range(tiles)]
    turned = [pltpu.roll(part, fine, 1) for part in sums]
    ahead = turn(
        [jnp.where(lane >= fine, turned[u], turned[u - 1]) for u in range(tiles)], -whole
    )
    return [
        ahead[u] - (second[u][:, :LANES] + second[(u + 1) % tiles][:, LANES:])
        for u in range(tiles)
    ]


def run_layer(x, sign, upper, lower, start):
    v = x
    for divisor in range(DEGREE, 0, -1):
        scale = sign * (1.0 / divisor)
        product = banded_product(v, upper, lower, start)
        v = [part + scale * term for part, term in zip(x, product)]
    return v


def cascade_first_kernel(distances, row_masks, *refs):
    pieces = []
    for count in distances[0]:
        pieces += [(refs[0], index) for index in range(count)]
        refs = refs[1:]
    others, refs = refs[: len(row_masks)], refs[len(row_masks) :]
    own, mine, upper, lower, starts, send, folds, masks, field = refs
    place(pieces, distances[1], folds)
    fill_masks(masks)
    place_field(own, list(zip(others, row_masks)), field)
    x = [field[u] for u in range(field.shape[0])]
    forward = lax.axis_index("layer") // GROUP == 0
    sign = jnp.where(forward, -1.0, 1.0)

    def prepare(k):
        slot = jnp.where(forward, k, GROUP - 1 - k)
        start = expand(folds, slot, masks, upper.at[k], lower.at[k])
        starts[k : k + 1, :] = jnp.full((1, LANES), start, jnp.int32)
        return start

    start = prepare(0)
    for k in range(GROUP):
        following = prepare(k + 1) if k + 1 < GROUP else None
        x = run_layer(x, sign, upper.at[k], lower.at[k], start)
        start = following
    mine[...] = own_panel(x, mine.shape[-1])
    write_whole(x, send)


def cascade_next_kernel(step, groups, *refs):
    upper, lower, starts, field, mine, *send = refs
    group = lax.axis_index("layer") // GROUP
    forward = group == step
    sign = jnp.where(forward, -1.0, 1.0)
    same_order = forward == (group == 0)
    x = field[...].astype(jnp.float32)
    x = [x[:, u : u + LANES] for u in range(0, x.shape[1], LANES)]

    order = [jnp.where(same_order, k, GROUP - 1 - k) for k in range(GROUP)]
    begin = [jnp.max(starts[pl.ds(at, 1), :]) for at in order]
    for at, start in zip(order, begin):
        x = run_layer(x, sign, upper.at[at], lower.at[at], start)
    mine[...] = own_panel(x, mine.shape[-1])
    if send:
        write_whole(x, *send)


def write_whole(x, send):
    for u, part in enumerate(x):
        send[:, u * LANES : (u + 1) * LANES] = part.astype(jnp.bfloat16)


def own_panel(x, panel):
    row = lax.axis_index("row")
    tiles = panel // LANES
    mine = x[:tiles]
    for index in range(1, len(x) // tiles):
        there = x[index * tiles : (index + 1) * tiles]
        mine = [jnp.where(row == index, new, old) for new, old in zip(there, mine)]
    return jnp.concatenate(mine, axis=1)


def join_kernel(groups, *refs):
    core = lax.axis_index("layer") % CORES
    group = lax.axis_index("layer") // GROUP
    count = refs[0].shape[0]
    for out, step in zip(refs[-2:], (group, groups - 1 - group)):
        for parts, at in ((refs[:groups], core), (refs[groups : 2 * groups], 1 - core)):
            chosen = parts[0][...]
            for index in range(1, groups):
                chosen = jnp.where(step == index, parts[index][...], chosen)
            out[0, pl.ds(pl.multiple_of(at * count, count), count), :] = chosen


def join(mine, theirs):
    count, panel = mine[0].shape
    vmem = pl.BlockSpec(memory_space=pltpu.VMEM)
    return pl.pallas_call(
        functools.partial(join_kernel, len(mine)),
        out_shape=[jax.ShapeDtypeStruct((1, CORES * count, panel), mine[0].dtype)] * 2,
        in_specs=[vmem] * (2 * len(mine)),
        out_specs=[vmem] * 2,
        compiler_params=pltpu.CompilerParams(vmem_limit_bytes=SMALL_GRANT),
        name="join",
    )(*mine, *theirs)


def run_first(batches, distances, others, row_masks, field, orders):
    count, panel = field.shape
    tiles = orders // LANES
    vmem = pl.BlockSpec(memory_space=pltpu.VMEM)
    window = jax.ShapeDtypeStruct((GROUP, tiles, LANES, 2 * LANES), jnp.bfloat16)
    return pl.pallas_call(
        functools.partial(cascade_first_kernel, distances, row_masks),
        out_shape=[
            jax.ShapeDtypeStruct((count, panel), jnp.float32),
            window,
            window,
            jax.ShapeDtypeStruct((GROUP, LANES), jnp.int32),
            jax.ShapeDtypeStruct((count, orders), jnp.bfloat16),
        ],
        in_specs=[vmem] * (len(batches) + len(others) + 1),
        out_specs=[vmem] * 5,
        scratch_shapes=[
            pltpu.VMEM((GROUP, tiles * PACKED, LANES), jnp.bfloat16),
            pltpu.VMEM((4, LANES, LANES), jnp.bfloat16),
            pltpu.VMEM((tiles, count, LANES), jnp.float32),
        ],
        compiler_params=pltpu.CompilerParams(vmem_limit_bytes=24 * 1024 * 1024),
        name="cascade_first",
    )(*batches, *others, field)


def run_next(step, groups, upper, lower, starts, field, panel):
    vmem = pl.BlockSpec(memory_space=pltpu.VMEM)
    out_shape = [jax.ShapeDtypeStruct((field.shape[0], panel), jnp.float32)]
    if step < groups - 1:
        out_shape.append(jax.ShapeDtypeStruct(field.shape, jnp.bfloat16))
    return pl.pallas_call(
        functools.partial(cascade_next_kernel, step, groups),
        out_shape=out_shape,
        in_specs=[vmem] * 4,
        out_specs=[vmem] * len(out_shape),
        compiler_params=pltpu.CompilerParams(vmem_limit_bytes=24 * 1024 * 1024),
        name=f"cascade_{step}",
    )(upper, lower, starts, field)


def gather_batches(own, corner, across, rows):
    bits = [(0, 1 << b) for b in range(rows.bit_length() - 1)]
    bits += [(1 << b, 0) for b in range(1, GROUP.bit_length() - 1)]
    count = len(bits)

    def members(subset):
        return [b for b in range(count) if subset >> b & 1]

    def distance(subset):
        return tuple(
            tuple(sum(bits[(b + core) % count][axis] for b in members(subset)) for axis in (0, 1))
            for core in range(CORES)
        )

    subsets = sorted(range(1 << count), key=lambda m: (m.bit_count(), m))
    pieces = {0: own}
    for subset in subsets[1 : count + 1]:
        pieces[subset] = across(own, distance(subset))
    pieces[subsets[-1]] = across(corner, distance(subsets[-1]))
    for subset in subsets[count + 1 : -1]:
        which = members(subset)
        link = next((b for b in which if (b + 1) % count in which), which[0])
        pieces[subset] = across(pieces[subset ^ 1 << link], distance(1 << link))
    batches, counts, distances = [], [], []
    for part in (subsets[: count + 1], subsets[count + 1 :]):
        mine = batch([pieces[subset] for subset in part])
        batches += [mine, across(mine, ((1, 0), (1, 0)))]
        counts += [len(part), len(part)]
        distances += [distance(subset) for subset in part]
        distances += [
            tuple((a ^ 1, b) for a, b in options[::-1]) for options in distances[-len(part) :]
        ]
    return pieces[subsets[-1]], batches, (tuple(counts), tuple(distances))


def on_device(coupling, band_off, band_width, incident, cotangent):
    panel, orders = coupling.shape[1:]
    layers = lax.axis_size("layer")
    rows = lax.axis_size("row")
    groups = layers // GROUP

    def across(array, options):
        pairs = []
        for l in range(layers):
            layer_mask, row_mask = options[l % CORES]
            for r in range(rows):
                pairs.append((l * rows + r, (l ^ layer_mask) * rows + (r ^ row_mask)))
        return lax.ppermute(array, ("layer", "row"), pairs)

    folded = fold(coupling, band_off, band_width)
    layer = lax.axis_index("layer")
    share = incident.shape[0] // CORES
    folded, incident, cotangent = lax.optimization_barrier((folded, incident, cotangent))
    field = jnp.where(layer // GROUP == 0, incident, cotangent)
    field = lax.dynamic_slice_in_dim(field, layer % CORES * share, share)
    whole = corner(folded, field)
    from_corner, batches, distances = gather_batches(folded, whole, across, rows)
    others, row_masks = [from_corner], [rows - 1]
    for mask in range(1, rows - 1):
        others.append(across(whole, ((0, mask), (0, mask))))
        row_masks.append(mask)
    mine, upper, lower, starts, send = run_first(
        batches, distances, others, tuple(row_masks), field, orders
    )
    results = []
    for step in range(1, groups):
        pairs = []
        for index in range(GROUP * rows):
            forward_from = (step - 1) * GROUP * rows + index
            adjoint_from = (groups - step) * GROUP * rows + index
            pairs.append((forward_from, forward_from + GROUP * rows))
            pairs.append((adjoint_from, adjoint_from - GROUP * rows))
        field = lax.ppermute(send, ("layer", "row"), pairs)
        theirs = across(mine, ((1, 0), (1, 0)))
        field, theirs = lax.optimization_barrier((field, theirs))
        results.append((mine, theirs))
        mine, *send = run_next(step, groups, upper, lower, starts, field, panel)
        send = send[0] if send else None
    results.append((mine, across(mine, ((1, 0), (1, 0)))))
    return tuple(join(*zip(*results)))


def solution(mesh):
    in_specs = (P("layer", "row", None), P("layer"), P("layer"), P(None, "row"), P(None, "row"))
    out_specs = (P("layer", None, "row"), P("layer", None, "row"))
    return jax.shard_map(
        on_device, mesh=mesh, in_specs=in_specs, out_specs=out_specs, check_vma=False
    )
```
